32 devices in a mesh: rep: 4 (over z), fsdp: 8 (over y, x, core).
Axes of the slice: x: 2, y: 2, z: 4, core: 2. Of those that a mesh axis runs over, the one named last changes fastest.
Arguments:
- tokens: bfloat16 [16384, 1536], P(('rep', 'fsdp')), may hold values from -6 to 6
- cotangent: bfloat16 [16384, 1536], P(('rep', 'fsdp')), may hold values from -6 to 6
- lengths: int32 [4, 8, 2], P('rep', 'fsdp'), may hold values from 128 to 384, as said below
- dealing: int32 [4, 8, 8], P('rep', 'fsdp'), may hold values from 0 to 7, each once within a row
- norm_gain: bfloat16 [1536], P('fsdp'), may hold values from 0.5 to 1.5
- in_weight: bfloat16 [1536, 6448], P('fsdp'), may hold values from -0.15625 to 0.15625
- conv_weight: bfloat16 [4, 3328], P(None, 'fsdp'), may hold values from -3 to 3
- conv_bias: bfloat16 [3328], P('fsdp'), may hold values from -3 to 3
- dt_bias: bfloat16 [48], P('fsdp'), may hold values from -6 to -1
- a_log: bfloat16 [48], P('fsdp'), may hold values from 0 to 2.6875
- d_skip: bfloat16 [48], P('fsdp'), may hold values from 0.5 to 1.5
- gated_gain: bfloat16 [3072], P('fsdp'), may hold values from 0.5 to 1.5
- out_weight: bfloat16 [3072, 1536], P('fsdp'), may hold values from -0.109375 to 0.109375
Outputs:
- output: bfloat16 [16384, 1536], P(('rep', 'fsdp'))
- input_grad: bfloat16 [16384, 1536], P(('rep', 'fsdp'))
- norm_gain_grad: float32 [1536], P('fsdp')
- in_weight_grad: float32 [1536, 6448], P('fsdp')
- conv_weight_grad: float32 [4, 3328], P(None, 'fsdp')
- conv_bias_grad: float32 [3328], P('fsdp')
- dt_bias_grad: float32 [48], P('fsdp')
- a_log_grad: float32 [48], P('fsdp')
- d_skip_grad: float32 [48], P('fsdp')
- gated_gain_grad: float32 [3072], P('fsdp')
- out_weight_grad: float32 [3072, 1536], P('fsdp')
The draws below stay inside these ranges and needn't reach their ends.
Inputs may be any that keep to these rules, and one draw needn't show every extreme that they name: Each device's 2 lengths sum to 512. Each row dealing[r, f, :] is a permutation, so every device of a group receives exactly one block from every device of it.
All inputs are finite; a program needn't handle non-finite values.
Results may differ from the reference program's by a relative error of at most 0.0066.
Values may be sent and summed in bfloat16 or wider, within the bound.
No kernel may reach another device: no remote copies, remote signals or barrier semaphores. Data moves between devices by JAX's collectives and lax.ppermute only.
A program may use at most 320 MiB of HBM per device.

```python
import jax
import jax.numpy as jnp
from jax import lax

D = 1536
DI = 3072
HEAD_DIM = 64
NSTATE = 128
KW = 4
SPAN = 256
SEQ_DEV = 2
TOK_DEV = 512
HEADS = 48
CONVD = 3328
NPROJ = 6448
TOKENS = 16384
N_REP = 4
N_FSDP = 8


def draw_lengths(key, part):
    key = jax.random.fold_in(key, 7)
    first = jax.random.randint(key, (N_REP, N_FSDP), TOK_DEV // 4, TOK_DEV - TOK_DEV // 4 + 1, dtype=jnp.int32)
    first = first.at[0, 0].set(TOK_DEV // 4)
    return jnp.stack([first, TOK_DEV - first], axis=-1).astype(jnp.int32)


def block_levels(stream_key, shape, cuts, least, top_value):
    def one(position, parts):
        heights = jax.random.uniform(jax.random.fold_in(jax.random.fold_in(stream_key, 6), position), (parts,), jnp.float32, least / len(cuts), top_value / len(cuts))
        return jnp.repeat(jnp.exp(heights), shape[position] // parts).reshape((-1,) + (1,) * (len(shape) - position - 1))

    gain = one(*cuts[0])
    for cut in cuts[1:]:
        gain = gain * one(*cut)
    return gain


def noise(stream_key, shape, scale, most, shards=(), held_as=jnp.bfloat16):
    entries = jax.random.normal(stream_key, shape, jnp.float32) * scale
    if len(shards) > 0:
        entries = block_levels(stream_key, shape, shards, -0.22, 0.18) * entries
    return jnp.clip(entries, min=-most, max=most).astype(held_as)


def setup_inputs(seed: int = 0) -> dict:
    key_list = jax.random.split(jax.random.key(seed), 14)
    tokens = noise(key_list[0], (TOKENS, D), 1.0, 6.0, ((0, 32),))
    cotangent = noise(key_list[1], (TOKENS, D), 1.0, 6.0, ((0, 32),))
    lengths = draw_lengths(jax.random.fold_in(key_list[13], 71), 0)
    dealing = jax.vmap(lambda own: jax.random.permutation(own, N_FSDP))(jax.random.split(key_list[3], N_REP * N_FSDP)).reshape((N_REP, N_FSDP, N_FSDP)).astype(jnp.int32)
    norm_gain = jnp.clip(1.0 + 0.1 * jax.random.normal(key_list[4], (D,), jnp.float32), 0.5, 1.5).astype(jnp.bfloat16)
    in_weight = noise(key_list[5], (D, NPROJ), D ** -0.5, 0.15625, ((0, 8),))
    conv_weight = noise(key_list[6], (KW, CONVD), KW ** -0.5, 3.0, ((1, 8),))
    conv_bias = noise(key_list[7], (CONVD,), 0.5, 3.0, ((0, 8),))
    dt_bias = jnp.clip(-6.0 + 5.0 * jax.random.uniform(key_list[8], (HEADS,), jnp.float32) ** block_levels(key_list[8], (HEADS,), ((0, 8),), -0.2, 0.2), -6.0, -1.0).astype(jnp.bfloat16)
    a_log = jnp.clip(2.6875 * jax.random.uniform(key_list[9], (HEADS,), jnp.float32) ** block_levels(key_list[9], (HEADS,), ((0, 8),), -0.2, 0.2), 0.0, 2.6875).astype(jnp.bfloat16)
    d_skip = jnp.clip(0.5 + 1.0 * jax.random.uniform(key_list[10], (HEADS,), jnp.float32) ** block_levels(key_list[10], (HEADS,), ((0, 8),), -0.2, 0.2), 0.5, 1.5).astype(jnp.bfloat16)
    gated_gain = jnp.clip(1.0 + 0.1 * jax.random.normal(key_list[11], (DI,), jnp.float32), 0.5, 1.5).astype(jnp.bfloat16)
    out_weight = noise(key_list[12], (DI, D), DI ** -0.5, 0.109375, ((0, 8),))
    return {"tokens": tokens, "cotangent": cotangent, "lengths": lengths, "dealing": dealing, "norm_gain": norm_gain, "in_weight": in_weight, "conv_weight": conv_weight, "conv_bias": conv_bias, "dt_bias": dt_bias, "a_log": a_log, "d_skip": d_skip, "gated_gain": gated_gain, "out_weight": out_weight}


epsilon = 1e-05

@jax.custom_vjp
def low(v):
    return lax.optimization_barrier(v.astype(jnp.bfloat16)).astype(jnp.float32)

@jax.custom_vjp
def low_back(v):
    return v

def low_keep(v):
    return (low(v), None)

def low_pass(kept, grad):
    return (grad,)

def back_keep(v):
    return (v, None)

def back_low(kept, grad):
    return (low(grad),)
low.defvjp(low_keep, low_pass)
low_back.defvjp(back_keep, back_low)

def segment_ids(seq_lengths, rows):
    ends = jnp.cumsum(seq_lengths.astype(jnp.int32)).astype(jnp.int32)
    places = jnp.arange(rows, dtype=jnp.int32)
    return lax.optimization_barrier(jnp.sum((places[:, None] >= ends[None, :]).astype(jnp.int32), axis=1)).astype(jnp.int32)

def block_step(state, inputs):
    inner, step_size, log_decay, b_input, c_output, segment, carry_mask, last_mask = inputs
    cumulative = jnp.cumsum(log_decay, axis=0)
    places = jnp.arange(SPAN, dtype=jnp.int32)
    causal = (places[:, None] >= places[None, :]) & (segment[:, None] == segment[None, :])
    mask = causal.astype(jnp.float32)[:, :, None]
    spread = cumulative[:, None, :] - cumulative[None, :, :]
    decay = jnp.exp(jnp.where(mask > 0, spread, 0.0)) * mask
    scores = jnp.dot(c_output, b_input.T, precision=lax.Precision.HIGHEST)
    weighted = inner * step_size[:, :, None]
    mixing = scores[:, :, None] * decay
    local_out = jnp.einsum('tsh,shp->thp', mixing, weighted, precision=lax.Precision.HIGHEST)
    carried = jnp.einsum('tn,hnp->thp', c_output, state, precision=lax.Precision.HIGHEST)
    result = local_out + carried * (jnp.exp(cumulative) * carry_mask[:, None])[:, :, None]
    end_weight = jnp.exp(cumulative[-1][None, :] - cumulative) * last_mask[:, None]
    new_state = jnp.exp(cumulative[-1])[:, None, None] * state * carry_mask[-1]
    new_state = new_state + jnp.einsum('sn,shp->hnp', b_input, weighted * end_weight[:, :, None], precision=lax.Precision.HIGHEST)
    return (new_state, result)

def mixer_core(projected, segment, conv_weight, conv_bias, dt_bias, a_log, d_skip, gated_gain):
    length = projected.shape[0]
    gate_part = projected[:, :DI]
    conv_input = projected[:, DI:2 * DI + 2 * NSTATE]
    step_raw = projected[:, 2 * DI + 2 * NSTATE:]
    mixed = conv_bias + conv_weight[KW - 1] * conv_input
    for offset in range(1, KW):
        shifted = jnp.concatenate([jnp.zeros((offset, conv_input.shape[1]), jnp.float32), conv_input[:-offset]], axis=0)
        earlier = jnp.concatenate([jnp.full((offset,), -1, jnp.int32), segment[:-offset]])
        keep_mask = (earlier == segment).astype(jnp.float32)[:, None]
        mixed = mixed + conv_weight[KW - 1 - offset] * shifted * keep_mask
    activated = jax.nn.silu(mixed)
    inner = activated[:, :DI].reshape(length, HEADS, HEAD_DIM)
    b_input = activated[:, DI:DI + NSTATE]
    c_output = activated[:, DI + NSTATE:]
    step_size = jax.nn.softplus(step_raw + dt_bias)
    log_decay = -jnp.exp(a_log) * step_size
    blocks = length // SPAN
    seg_blocks = segment.reshape(blocks, SPAN)
    before = jnp.concatenate([jnp.full((1,), -1, jnp.int32), seg_blocks[:-1, -1]])
    carry_mask = (seg_blocks == before[:, None]).astype(jnp.float32)
    last_mask = (seg_blocks == seg_blocks[:, -1:]).astype(jnp.float32)
    scanned = (inner.reshape(blocks, SPAN, HEADS, HEAD_DIM), step_size.reshape(blocks, SPAN, HEADS), log_decay.reshape(blocks, SPAN, HEADS), b_input.reshape(blocks, SPAN, NSTATE), c_output.reshape(blocks, SPAN, NSTATE), seg_blocks, carry_mask, last_mask)
    start_state = jnp.zeros((HEADS, NSTATE, HEAD_DIM), jnp.float32)
    final_state, outputs = lax.scan(jax.checkpoint(block_step), start_state, scanned)
    ssm_out = outputs.reshape(length, HEADS, HEAD_DIM) + d_skip[None, :, None] * inner
    gated = ssm_out.reshape(length, DI) * jax.nn.silu(gate_part)
    return gated * lax.rsqrt(lax.optimization_barrier(jnp.mean(gated * gated, axis=-1, keepdims=True)) + epsilon) * gated_gain

def block_forward(hidden, segment, norm_gain, in_weight, conv_weight, conv_bias, dt_bias, a_log, d_skip, gated_gain, out_weight):
    normed = low(hidden * lax.rsqrt(lax.optimization_barrier(jnp.mean(hidden * hidden, axis=-1, keepdims=True)) + epsilon) * norm_gain)
    projected = low_back(jnp.dot(normed, in_weight, precision=lax.Precision.HIGHEST))
    gated = low(mixer_core(projected, segment, conv_weight, conv_bias, dt_bias, a_log, d_skip, gated_gain))
    return hidden + jnp.dot(gated, out_weight, precision=lax.Precision.HIGHEST)

def reference(tokens, cotangent, lengths, dealing, norm_gain, in_weight, conv_weight, conv_bias, dt_bias, a_log, d_skip, gated_gain, out_weight):
    groups = N_FSDP
    replicas = N_REP
    block_rows = TOK_DEV // N_FSDP
    inverse = jnp.argsort(dealing, axis=-1).astype(jnp.int32)

    def deal(values):
        split = values.reshape(replicas, groups, groups, block_rows, D)
        moved = jnp.take_along_axis(split, inverse[:, :, :, None, None], axis=2)
        return jnp.swapaxes(moved, 1, 2).reshape(replicas * groups, TOK_DEV, D)

    def undeal(values):
        split = jnp.swapaxes(values.reshape(replicas, groups, groups, block_rows, D), 1, 2)
        moved = jnp.take_along_axis(split, dealing.astype(jnp.int32)[:, :, :, None, None], axis=2)
        return moved.reshape(replicas * groups * TOK_DEV, D)
    dealt_x = deal(tokens).astype(jnp.float32)
    dealt_cot = deal(cotangent).astype(jnp.float32)
    flat_lengths = lengths.reshape(replicas * groups, SEQ_DEV)
    segments = jnp.stack([segment_ids(flat_lengths[index], TOK_DEV) for index in range(replicas * groups)])
    params = (norm_gain.astype(jnp.float32), in_weight.astype(jnp.float32), conv_weight.astype(jnp.float32), conv_bias.astype(jnp.float32), dt_bias.astype(jnp.float32), a_log.astype(jnp.float32), d_skip.astype(jnp.float32), gated_gain.astype(jnp.float32), out_weight.astype(jnp.float32))

    def device_step(totals, inputs):
        hidden, cot, segment = inputs

        def forward(hidden_in, *weights):
            return block_forward(hidden_in, segment, *weights)
        result, backward = jax.vjp(forward, hidden, *params)
        grads = backward(cot)
        summed = tuple((total + grad for total, grad in zip(totals, grads[1:])))
        return (summed, (result, grads[0]))
    start = tuple((jnp.zeros_like(param) for param in params))
    totals, (results, input_grads) = lax.scan(device_step, start, (dealt_x, dealt_cot, segments))
    output = undeal(results).astype(jnp.bfloat16)
    input_grad = undeal(input_grads).astype(jnp.bfloat16)
    return (output, input_grad, totals[0], totals[1], totals[2], totals[3], totals[4], totals[5], totals[6], totals[7], totals[8])
```

```python
import functools

import jax
import jax.numpy as jnp
from jax import lax
from jax.experimental import pallas as pl
from jax.experimental.pallas import tpu as pltpu
from jax.sharding import PartitionSpec as P

DI = 3072
HEAD_DIM = 64
NSTATE = 128
KW = 4
HEADS = 48
BCD = 384

epsilon = 1e-05


Q = 128
GROUP = 8
LANES = GROUP * HEAD_DIM
NEG = -1e30
VMEM = 56 * 1024 * 1024


def dot32(a, b, dims=(((1,), (0,)), ((), ())), precision=None):
    return lax.dot_general(a, b, dims, preferred_element_type=jnp.float32, precision=precision)


NT = (((1,), (1,)), ((), ()))


def row_ids(start, rows, cols):
    return lax.broadcasted_iota(jnp.int32, (rows, cols), 0) + start


def shifted_down(ref, cols, c, first, width):
    if c == 0:
        tall = jnp.concatenate([jnp.zeros((8, width), jnp.float32), ref[0:Q, cols]], axis=0)
    else:
        tall = ref[c * Q - 8 : c * Q + Q, cols]
    place = row_ids(c * Q, Q, width)
    outs = [tall[8:]]
    for j in range(1, KW):
        moved = pltpu.roll(tall, j, 0)[8:]
        keep = (place >= j) & ((place < first) | (place >= first + j))
        outs.append(jnp.where(keep, moved, 0.0))
    return outs


def conv_back(ref, cols, c, first, width, taps):
    tall = ref[c * Q : c * Q + Q + 8, cols]
    place = row_ids(c * Q, Q, width)
    total = taps[KW - 1] * tall[:Q]
    for j in range(1, KW):
        moved = pltpu.roll(tall, Q + 8 - j, 0)[:Q]
        keep = (place < first - j) | (place >= first)
        total = total + taps[KW - 1 - j] * jnp.where(keep, moved, 0.0)
    return total


def sum_rows(v):
    return jnp.sum(v, axis=0, keepdims=True)


def prep_kernel(first_ref, bcd_ref, conv_ref, head_ref, bn_ref, cn_ref, bt_ref, ct_ref, s_ref, st_ref, cum_ref, cp_ref, cumt_ref, cpt_ref):
    first = first_ref[0]
    tri = (row_ids(0, Q, Q) >= lax.broadcasted_iota(jnp.int32, (Q, Q), 1)).astype(jnp.float32)
    rate = -jnp.exp(head_ref[1:2, :])
    lane = lax.broadcasted_iota(jnp.int32, (Q, 128), 1)
    for c in range(bcd_ref.shape[0] // Q):
        rows = slice(c * Q, c * Q + Q)
        moved = shifted_down(bcd_ref, slice(0, 2 * NSTATE), c, first, 2 * NSTATE)
        mixed = conv_ref[4:5, :] + conv_ref[3:4, :] * moved[0]
        for j in range(1, KW):
            mixed = mixed + conv_ref[KW - 1 - j : KW - j, :] * moved[j]
        act = mixed * jax.nn.sigmoid(mixed)
        b32, c32 = act[:, :NSTATE], act[:, NSTATE:]
        b16, c16 = b32.astype(jnp.bfloat16), c32.astype(jnp.bfloat16)
        bn_ref[rows, :] = b16
        cn_ref[rows, :] = c16
        bt_ref[:, rows] = b32.T.astype(jnp.bfloat16)
        ct_ref[:, rows] = c32.T.astype(jnp.bfloat16)
        s_ref[rows, :] = dot32(c16, b16, NT)
        st_ref[rows, :] = dot32(b16, c16, NT)
        raw = jnp.where(lane < HEADS, bcd_ref[rows, 2 * NSTATE :] + head_ref[0:1, :], 0.0)
        step = jax.nn.softplus(raw)
        cum = dot32(tri, rate * step, precision=lax.Precision.HIGHEST)
        cp = cum - jnp.log(jnp.maximum(step, 1e-37))
        cum_ref[rows, :] = cum
        cp_ref[rows, :] = cp
        cumt_ref[:, rows] = cum.T
        cpt_ref[:, rows] = cp.T


def chunk_masks(first, c, transposed):
    base = c * Q
    row = row_ids(base, Q, Q)
    col = lax.broadcasted_iota(jnp.int32, (Q, Q), 1) + base
    ordered = (col >= row) if transposed else (row >= col)
    inside = ordered & ((row >= first) == (col >= first))
    carry = ((row >= first) == (base - 1 >= first)) & (base > 0)
    last = (row >= first) == (base + Q - 1 >= first)
    through = (base > 0) & ((base + Q - 1 >= first) == (base - 1 >= first))
    return inside, carry, last, through


def lane_column(values, k):
    return jnp.broadcast_to(values[:, k : k + 1], (Q, Q))


def forward_kernel(base, first_ref, z_ref, x_ref, conv_ref, gain_ref, bn_ref, cn_ref, bt_ref, s_ref, cum_ref, cp_ref, cpt_ref, y_ref, g_ref, sq_ref, states_ref, state):
    first = first_ref[0]
    group = base + pl.program_id(0)
    half = lax.broadcasted_iota(jnp.int32, (Q, Q), 1) < HEAD_DIM
    state[...] = jnp.zeros_like(state)

    @pl.when(pl.program_id(0) == 0)
    def _():
        sq_ref[...] = jnp.zeros_like(sq_ref)

    shift = (Q - GROUP * group) % Q
    for c in range(x_ref.shape[0] // Q):
        rows = slice(c * Q, c * Q + Q)
        inside, carry, last, through = chunk_masks(first, c, False)
        cum = pltpu.roll(cum_ref[rows, :], shift, 1)
        cp = pltpu.roll(cp_ref[rows, :], shift, 1)
        cpt = cpt_ref[pl.ds(pl.multiple_of(group * GROUP, GROUP), GROUP), rows]
        scores = s_ref[rows, :]
        c16 = cn_ref[rows, :]
        squares = jnp.zeros((Q, Q), jnp.float32)
        for p in range(GROUP // 2):
            cols = slice(p * Q, p * Q + Q)
            moved = shifted_down(x_ref, cols, c, first, Q)
            mixed = conv_ref[4:5, cols] + conv_ref[3:4, cols] * moved[0]
            for j in range(1, KW):
                mixed = mixed + conv_ref[KW - 1 - j : KW - j, cols] * moved[j]
            xs = mixed * jax.nn.sigmoid(mixed)
            x16 = xs.astype(jnp.bfloat16)
            locals_, cums, cps = [], [], []
            for e in range(2):
                k = 2 * p + e
                cum_b = lane_column(cum, k)
                decay = jnp.exp(jnp.where(inside, cum_b - cpt[k : k + 1, :], NEG))
                locals_.append(dot32((scores * decay).astype(jnp.bfloat16), x16))
                cums.append(cum_b)
                cps.append(lane_column(cp, k))
            cum_pair = jnp.where(half, cums[0], cums[1])
            cp_pair = jnp.where(half, cps[0], cps[1])
            y = jnp.where(half, locals_[0], locals_[1])
            old = state[:, cols]
            old16 = old.astype(jnp.bfloat16)
            states_ref[c * NSTATE : (c + 1) * NSTATE, cols] = old16
            if c > 0:
                y = y + jnp.where(carry, jnp.exp(cum_pair), 0.0) * dot32(c16, old16)
            y_ref[rows, cols] = y
            end = cum_pair[Q - 1 : Q, :]
            weight = jnp.where(last, jnp.exp(end - cp_pair), 0.0)
            fresh = dot32(bt_ref[:, rows], (weight * xs).astype(jnp.bfloat16))
            keep = jnp.where(through, jnp.exp(end), 0.0)
            state[:, cols] = fresh if c == 0 else keep * old + fresh
            zv = z_ref[rows, cols]
            g = (y + gain_ref[0:1, cols] * xs) * (zv * jax.nn.sigmoid(zv))
            g_ref[rows, cols] = g
            squares = squares + g * g
        sq_ref[rows, :] += squares


def split_dot(values, right):
    high = values.astype(jnp.bfloat16)
    low = (values - high.astype(jnp.float32)).astype(jnp.bfloat16)
    return dot32(high, right) + dot32(low, right)


def backward_kernel(base, first_ref, z_ref, x_ref, y_ref, dg_ref, rk_ref, conv_ref, gain_ref, bn_ref, cn_ref, ct_ref, st_ref, cum_ref, cp_ref, cumt_ref, states_ref, dz_ref, dx_ref, grads_ref, dst_ref, db_ref, dc_ref, u_ref, v_ref, w_ref, flow_ref, dstate, dconv):
    first = first_ref[0]
    group = base + pl.program_id(0)
    lane = lax.broadcasted_iota(jnp.int32, (Q, Q), 1)
    half = lane < HEAD_DIM
    dstate[...] = jnp.zeros_like(dstate)
    rows_all = x_ref.shape[0]
    dconv[rows_all : rows_all + 8, :] = jnp.zeros((8, dconv.shape[1]), jnp.float32)
    grads_ref[...] = jnp.zeros_like(grads_ref)
    flow_ref[...] = jnp.zeros_like(flow_ref)

    @pl.when(pl.program_id(0) == 0)
    def _():
        for ref in (dst_ref, db_ref, dc_ref, u_ref, v_ref, w_ref):
            ref[...] = jnp.zeros_like(ref)

    shift = (Q - GROUP * group) % Q
    chunks = rows_all // Q
    for c in range(chunks - 1, -1, -1):
        rows = slice(c * Q, c * Q + Q)
        inside, carry, last, through = chunk_masks(first, c, True)
        cum = pltpu.roll(cum_ref[rows, :], shift, 1)
        cp = pltpu.roll(cp_ref[rows, :], shift, 1)
        cumt = cumt_ref[pl.ds(pl.multiple_of(group * GROUP, GROUP), GROUP), rows]
        scores_t = st_ref[rows, :]
        b16, c16t = bn_ref[rows, :], ct_ref[:, rows]
        scale = lane_column(rk_ref[rows, :], 0)
        pull = lane_column(rk_ref[rows, :], 1)
        dst = jnp.zeros((Q, Q), jnp.float32)
        db = jnp.zeros((Q, NSTATE), jnp.float32)
        dc = jnp.zeros((Q, NSTATE), jnp.float32)
        us, vs, ws = (jnp.zeros((Q, Q), jnp.float32) for _ in range(3))
        for p in range(GROUP // 2):
            cols = slice(p * Q, p * Q + Q)
            moved = shifted_down(x_ref, cols, c, first, Q)
            mixed = conv_ref[4:5, cols] + conv_ref[3:4, cols] * moved[0]
            for j in range(1, KW):
                mixed = mixed + conv_ref[KW - 1 - j : KW - j, cols] * moved[j]
            sx = jax.nn.sigmoid(mixed)
            xs = mixed * sx
            x16 = xs.astype(jnp.bfloat16)
            zv = z_ref[rows, cols]
            sz = jax.nn.sigmoid(zv)
            silu_z = zv * sz
            skip, gain = gain_ref[0:1, cols], gain_ref[1:2, cols]
            y = y_ref[rows, cols]
            ssm = y + skip * xs
            g = ssm * silu_z
            gs = dg_ref[rows, cols] * scale
            grads_ref[6:7, cols] += sum_rows(gs * g)
            d_g = gain * gs - g * pull
            dz_ref[rows, cols] = (d_g * ssm * (sz + silu_z * (1.0 - sz))).astype(dz_ref.dtype)
            d_ssm = d_g * silu_z
            grads_ref[5:6, cols] += sum_rows(d_ssm * xs)
            dy16 = d_ssm.astype(jnp.bfloat16)
            locals_, cums, cps = [], [], []
            for e in range(2):
                k = 2 * p + e
                cp_b = lane_column(cp, k)
                decay = jnp.exp(jnp.where(inside, cumt[k : k + 1, :] - cp_b, NEG))
                locals_.append(dot32((scores_t * decay).astype(jnp.bfloat16), dy16))
                x_half = jnp.where(half == (e == 0), x16, jnp.zeros_like(x16))
                dst = dst + decay * dot32(x_half, dy16, NT)
                cums.append(lane_column(cum, k))
                cps.append(cp_b)
            cum_pair = jnp.where(half, cums[0], cums[1])
            cp_pair = jnp.where(half, cps[0], cps[1])
            dx = jnp.where(half, locals_[0], locals_[1])
            dy32, x32 = dy16.astype(jnp.float32), x16.astype(jnp.float32)
            pick = (lane == GROUP * group + 2 * p + (row_ids(0, Q, Q) >= HEAD_DIM).astype(jnp.int32)).astype(jnp.bfloat16)
            in_dot = x32 * dx
            us = us + split_dot(dy32 * y - in_dot, pick)
            vs = vs + split_dot(in_dot, pick)
            end = cum_pair[Q - 1 : Q, :]
            keep = jnp.where(through, jnp.exp(end), 0.0)
            if c < chunks - 1:
                later = dstate[:, cols]
                later16 = later.astype(jnp.bfloat16)
                weight = jnp.where(last, jnp.exp(end - cp_pair), 0.0)
                carried = weight * dot32(b16, later16)
                dx = dx + carried
                ws = ws + split_dot(xs * carried, pick)
                db = db + dot32((weight * xs).astype(jnp.bfloat16), later16, NT)
            if c > 0:
                ey16 = (jnp.where(carry, jnp.exp(cum_pair), 0.0) * d_ssm).astype(jnp.bfloat16)
                old16 = states_ref[c * NSTATE : (c + 1) * NSTATE, cols]
                dc = dc + dot32(ey16, old16, NT)
                fresh = dot32(c16t, ey16)
                if c < chunks - 1:
                    flow_ref[c : c + 1, cols] = keep * sum_rows(later * old16.astype(jnp.float32))
                    fresh = keep * later + fresh
                dstate[:, cols] = fresh
            d_mixed = (dx + skip * d_ssm) * (sx + xs * (1.0 - sx))
            dconv[rows, cols] = d_mixed
            grads_ref[4:5, cols] += sum_rows(d_mixed)
            for j in range(KW):
                grads_ref[KW - 1 - j : KW - j, cols] += sum_rows(d_mixed * moved[j])
            taps = [conv_ref[i : i + 1, cols] for i in range(KW)]
            dx_ref[rows, cols] = conv_back(dconv, cols, c, first, Q, taps).astype(dx_ref.dtype)
        dst_ref[rows, :] += dst
        db_ref[rows, :] += db
        dc_ref[rows, :] += dc
        u_ref[rows, :] += us
        v_ref[rows, :] += vs
        w_ref[rows, :] += ws


def post_kernel(first_ref, bcd_ref, conv_ref, head_ref, bn_ref, cn_ref, dst_ref, db_ref, dc_ref, u_ref, v_ref, w_ref, flow_ref, d_ref, grads_ref, hgrads_ref, dconv):
    first = first_ref[0]
    rows_all = bcd_ref.shape[0]
    wide = 2 * NSTATE
    dconv[rows_all : rows_all + 8, :] = jnp.zeros((8, wide), jnp.float32)
    grads_ref[...] = jnp.zeros_like(grads_ref)
    hgrads_ref[...] = jnp.zeros_like(hgrads_ref)
    lane = lax.broadcasted_iota(jnp.int32, (Q, 128), 1)
    rate = -jnp.exp(head_ref[1:2, :])
    spread = (lax.broadcasted_iota(jnp.int32, (DI, 128), 0) // HEAD_DIM == lax.broadcasted_iota(jnp.int32, (DI, 128), 1)).astype(jnp.float32)
    flow = dot32(flow_ref[...], spread, precision=lax.Precision.HIGHEST)
    row, col = row_ids(0, Q, Q), lax.broadcasted_iota(jnp.int32, (Q, Q), 1)
    earlier_sum = (col < row).astype(jnp.float32)
    for c in range(rows_all // Q - 1, -1, -1):
        rows = slice(c * Q, c * Q + Q)
        moved = shifted_down(bcd_ref, slice(0, wide), c, first, wide)
        mixed = conv_ref[4:5, :] + conv_ref[3:4, :] * moved[0]
        for j in range(1, KW):
            mixed = mixed + conv_ref[KW - 1 - j : KW - j, :] * moved[j]
        sx = jax.nn.sigmoid(mixed)
        dst = jnp.sum(dst_ref[:, rows, :], axis=0)
        d_b = jnp.sum(db_ref[:, rows, :], axis=0) + dot32(dst.astype(jnp.bfloat16), cn_ref[rows, :])
        d_c = jnp.sum(dc_ref[:, rows, :], axis=0) + dot32(dst.T.astype(jnp.bfloat16), bn_ref[rows, :])
        d_mixed = jnp.concatenate([d_b, d_c], axis=1) * (sx + mixed * sx * (1.0 - sx))
        dconv[rows, :] = d_mixed
        grads_ref[4:5, :] += sum_rows(d_mixed)
        for j in range(KW):
            grads_ref[KW - 1 - j : KW - j, :] += sum_rows(d_mixed * moved[j])
        taps = [conv_ref[i : i + 1, :] for i in range(KW)]
        d_ref[rows, :wide] = conv_back(dconv, slice(0, wide), c, first, wide, taps).astype(d_ref.dtype)
        carried = jnp.sum(w_ref[:, rows, :], axis=0)
        later_sum = ((col >= row) & ((row + c * Q >= first) == (col + c * Q >= first))).astype(jnp.float32)
        d_la = dot32(later_sum, jnp.sum(u_ref[:, rows, :], axis=0), precision=lax.Precision.HIGHEST)
        d_la = d_la + dot32(earlier_sum, carried, precision=lax.Precision.HIGHEST) + flow[c : c + 1, :]
        d_log = jnp.sum(v_ref[:, rows, :], axis=0) + carried
        raw = bcd_ref[rows, wide:] + head_ref[0:1, :]
        step = jax.nn.softplus(raw)
        sig = jax.nn.sigmoid(raw)
        ratio = jnp.where(raw < -17.0, 1.0, sig / jnp.maximum(step, 1e-37))
        d_raw = jnp.where(lane < HEADS, d_log * ratio + d_la * rate * sig, 0.0)
        d_ref[rows, wide:] = d_raw.astype(d_ref.dtype)
        hgrads_ref[0:1, :] += sum_rows(d_raw)
        hgrads_ref[1:2, :] += sum_rows(jnp.where(lane < HEADS, d_la * rate * step, 0.0))


def smem():
    return pl.BlockSpec(memory_space=pltpu.SMEM)


def whole(shape):
    return pl.BlockSpec(shape, lambda g: (0,) * len(shape))


def run_prep(first, bcd, conv, heads):
    rows = bcd.shape[0]
    f32, b16 = jnp.float32, jnp.bfloat16
    shapes = [((rows, 128), b16), ((rows, 128), b16), ((128, rows), b16), ((128, rows), b16), ((rows, Q), f32), ((rows, Q), f32), ((rows, 128), f32), ((rows, 128), f32), ((128, rows), f32), ((128, rows), f32)]
    return pl.pallas_call(
        prep_kernel,
        grid=(1,),
        in_specs=[smem(), whole((rows, BCD)), whole((8, 2 * NSTATE)), whole((8, 128))],
        out_specs=[whole(s) for s, _ in shapes],
        out_shape=[jax.ShapeDtypeStruct(s, d) for s, d in shapes],
        compiler_params=pltpu.CompilerParams(vmem_limit_bytes=VMEM),
    )(first, bcd, conv, heads)


def run_forward(base, count, first, z, x, conv, gains, prep):
    rows = x.shape[0]
    bn, cn, bt, ct, s, st, cum, cp, cumt, cpt = prep
    f32, b16 = jnp.float32, jnp.bfloat16
    chunks = rows // Q
    at = lambda g: (0, g + base)
    here = lambda g: (0, g)
    return pl.pallas_call(
        functools.partial(forward_kernel, base),
        grid=(count,),
        in_specs=[smem(), pl.BlockSpec((rows, LANES), at), pl.BlockSpec((rows, LANES), at), pl.BlockSpec((8, LANES), at), pl.BlockSpec((8, LANES), at)]
        + [whole(v.shape) for v in (bn, cn, bt, s, cum, cp, cpt)],
        out_specs=[pl.BlockSpec((rows, LANES), here), pl.BlockSpec((rows, LANES), here), whole((rows, Q)), pl.BlockSpec((chunks * NSTATE, LANES), here)],
        out_shape=[jax.ShapeDtypeStruct((rows, count * LANES), f32), jax.ShapeDtypeStruct((rows, count * LANES), f32), jax.ShapeDtypeStruct((rows, Q), f32), jax.ShapeDtypeStruct((chunks * NSTATE, count * LANES), b16)],
        scratch_shapes=[pltpu.VMEM((NSTATE, LANES), f32)],
        compiler_params=pltpu.CompilerParams(vmem_limit_bytes=VMEM),
        cost_estimate=pl.CostEstimate(flops=count * 1200000000, bytes_accessed=count * 6000000, transcendentals=0),
    )(first, z, x, conv, gains, bn, cn, bt, s, cum, cp, cpt)


def run_backward(base, count, first, z, x, y, dg, rk, conv, gains, prep, states):
    rows = x.shape[0]
    bn, cn, bt, ct, s, st, cum, cp, cumt, cpt = prep
    f32, b16 = jnp.float32, jnp.bfloat16
    chunks = rows // Q
    at = lambda g: (0, g + base)
    here = lambda g: (0, g)
    block = pl.BlockSpec((rows, LANES), at)
    local = pl.BlockSpec((rows, LANES), here)
    sums = [(rows, Q), (rows, NSTATE), (rows, NSTATE), (rows, 128), (rows, 128), (rows, 128)]
    return pl.pallas_call(
        functools.partial(backward_kernel, base),
        grid=(count,),
        in_specs=[smem(), block, block, block, block, whole(rk.shape), pl.BlockSpec((8, LANES), at), pl.BlockSpec((8, LANES), at)]
        + [whole(v.shape) for v in (bn, cn, ct, st, cum, cp, cumt)]
        + [pl.BlockSpec((chunks * NSTATE, LANES), at)],
        out_specs=[local, local, pl.BlockSpec((8, LANES), here)] + [whole(v) for v in sums] + [pl.BlockSpec((8, LANES), here)],
        out_shape=[jax.ShapeDtypeStruct((rows, count * LANES), b16)] * 2 + [jax.ShapeDtypeStruct((8, count * LANES), f32)] + [jax.ShapeDtypeStruct(v, f32) for v in sums] + [jax.ShapeDtypeStruct((8, count * LANES), f32)],
        scratch_shapes=[pltpu.VMEM((NSTATE, LANES), f32), pltpu.VMEM((rows + 8, LANES), f32)],
        compiler_params=pltpu.CompilerParams(vmem_limit_bytes=VMEM),
        cost_estimate=pl.CostEstimate(flops=count * 4000000000, bytes_accessed=count * 8000000, transcendentals=0),
    )(first, z, x, y, dg, rk, conv, gains, bn, cn, ct, st, cum, cp, cumt, states)


def run_post(first, bcd, conv, heads, prep, *sums):
    rows = bcd.shape[0]
    bn, cn = prep[0], prep[1]
    f32 = jnp.float32
    return pl.pallas_call(
        post_kernel,
        grid=(1,),
        in_specs=[smem(), whole((rows, BCD)), whole((8, 2 * NSTATE)), whole((8, 128)), whole(bn.shape), whole(cn.shape)] + [whole(t.shape) for t in sums],
        out_specs=[whole((rows, BCD)), whole((8, 2 * NSTATE)), whole((8, 128))],
        out_shape=[jax.ShapeDtypeStruct((rows, BCD), jnp.bfloat16), jax.ShapeDtypeStruct((8, 2 * NSTATE), f32), jax.ShapeDtypeStruct((8, 128), f32)],
        scratch_shapes=[pltpu.VMEM((rows + 8, 2 * NSTATE), f32)],
        compiler_params=pltpu.CompilerParams(vmem_limit_bytes=VMEM),
    )(first, bcd, conv, heads, bn, cn, *sums)


def contract_rows(left, right, kind=jnp.float32):
    return lax.dot_general(left, right, (((0,), (0,)), ((), ())), preferred_element_type=kind)


def contract_cols(left, right):
    return lax.dot_general(left, right, NT, preferred_element_type=jnp.float32)


def pad_lanes(v, width):
    return jnp.pad(v, ((0, 0), (0, width - v.shape[1])))


def per_device(tokens, cotangent, lengths, dealing, norm_gain, in_weight, conv_weight, conv_bias, dt_bias, a_log, d_skip, gated_gain, out_weight):
    f32, b16 = jnp.float32, jnp.bfloat16
    groups = lax.axis_size("fsdp")
    tok_rows, width = tokens.shape
    block_rows = tok_rows // groups
    targets = dealing.reshape(groups)
    inverse = jnp.argsort(targets)
    first = lengths.reshape(-1)[:1]

    small = jnp.concatenate([norm_gain, conv_weight.reshape(-1), conv_bias, dt_bias, a_log, d_skip, gated_gain])
    sizes = [v.size for v in (norm_gain, conv_weight, conv_bias, dt_bias, a_log, d_skip, gated_gain)]
    small_all = lax.all_gather(jnp.pad(small, (0, -small.size % 128)), "fsdp", axis=0, tiled=False).astype(f32)
    in_full = lax.all_gather(in_weight, "fsdp", axis=0, tiled=True)
    out_full = lax.all_gather(out_weight, "fsdp", axis=0, tiled=True)

    def deal(values):
        blocks = values.reshape(groups, block_rows, width)[inverse]
        return lax.all_to_all(blocks, "fsdp", split_axis=0, concat_axis=0, tiled=True).reshape(tok_rows, width)

    def undeal(values):
        blocks = lax.all_to_all(values.reshape(groups, block_rows, width), "fsdp", split_axis=0, concat_axis=0, tiled=True)
        return blocks[targets].reshape(tok_rows, width)

    hidden = deal(tokens).astype(f32)
    cot = deal(cotangent)

    ends, parts = 0, []
    for size in sizes:
        parts.append(small_all[:, ends : ends + size])
        ends += size
    gain = parts[0].reshape(1, -1)
    taps = parts[1].reshape(groups, KW, -1).transpose(1, 0, 2).reshape(KW, -1)
    bias, step_bias, rate, skip, ggain = (v.reshape(1, -1) for v in parts[2:])
    conv = jnp.concatenate([taps, bias, jnp.zeros((3, bias.shape[1]), f32)])
    heads = pad_lanes(jnp.concatenate([step_bias, rate, jnp.zeros((6, HEADS), f32)]), 128)
    gains = jnp.concatenate([jnp.repeat(skip, HEAD_DIM, axis=1), ggain, jnp.zeros((6, DI), f32)])
    conv_x, conv_bc = conv[:, :DI], conv[:, DI:]

    rn = lax.rsqrt(jnp.mean(hidden * hidden, axis=-1, keepdims=True) + epsilon)
    normed = (hidden * rn * gain).astype(b16)
    w_z, w_x, w_b = in_full[:, :DI], in_full[:, DI : 2 * DI], pad_lanes(in_full[:, 2 * DI :], BCD)
    z, x, bcd = (jnp.dot(normed, w, preferred_element_type=f32) for w in (w_z, w_x, w_b))

    prep = run_prep(first, bcd, conv_bc, heads)
    y, g, sq, states = run_forward(0, HEADS // GROUP, first, z, x, conv_x, gains, prep)
    r = lax.rsqrt(jnp.sum(sq, axis=-1, keepdims=True) / DI + epsilon)
    gated = (g * r * ggain).astype(b16)
    branch = jnp.dot(gated, out_full, preferred_element_type=f32)
    result = (hidden + branch).astype(b16)
    output = undeal(result)
    cot32 = cot.astype(f32)
    pull = r * r * (jnp.sum(cot32 * branch, axis=-1, keepdims=True) / DI)
    rk = pad_lanes(jnp.concatenate([r, pull], axis=1), 128)
    d_gated = contract_cols(cot, out_full)
    out_term = contract_rows(gated, cot, b16)
    s_out = lax.psum_scatter(out_term, "fsdp", scatter_dimension=0, tiled=True)

    d_z, d_x, xgrads, *sums, flow = run_backward(0, HEADS // GROUP, first, z, x, y, d_gated, rk, conv_x, gains, prep, states)
    d_b, bgrads, hgrads = run_post(first, bcd, conv_bc, heads, prep, *[t[None] for t in sums], flow)
    in_term = jnp.concatenate([contract_rows(normed, d_z, b16), contract_rows(normed, d_x, b16), contract_rows(normed, d_b, b16)[:, : in_weight.shape[1] - 2 * DI]], axis=1)
    s_in = lax.psum_scatter(in_term, "fsdp", scatter_dimension=0, tiled=True)
    d_normed = contract_cols(d_z, w_z) + contract_cols(d_x, w_x) + contract_cols(d_b, w_b)
    g_gain = jnp.sum(d_normed * hidden * rn, axis=0)
    d_scaled = d_normed * gain
    d_hidden = rn * d_scaled - hidden * (rn * rn * rn * jnp.mean(hidden * d_scaled, axis=-1, keepdims=True))
    input_grad = undeal((cot32 + d_hidden).astype(b16))

    g_conv = jnp.concatenate([xgrads[:KW], bgrads[:KW]], axis=1)
    g_cbias = jnp.concatenate([xgrads[KW], bgrads[KW]])
    g_dskip = jnp.sum(xgrads[5].reshape(HEADS, HEAD_DIM), axis=1)
    spread = [
        g_gain.reshape(groups, -1),
        g_conv.reshape(KW, groups, -1).transpose(1, 0, 2).reshape(groups, -1),
        g_cbias.reshape(groups, -1),
        hgrads[0, :HEADS].reshape(groups, -1),
        hgrads[1, :HEADS].reshape(groups, -1),
        g_dskip.reshape(groups, -1),
        xgrads[6].reshape(groups, -1),
    ]
    packed = pad_lanes(jnp.concatenate(spread, axis=1), small_all.shape[1])
    s_small = jnp.sum(lax.all_to_all(packed, "fsdp", split_axis=0, concat_axis=0, tiled=True), axis=0)
    r_small = jnp.sum(lax.all_gather(s_small, "rep", axis=0, tiled=False), axis=0)
    r_in = lax.psum(s_in, "rep").astype(f32)
    r_out = lax.psum(s_out, "rep").astype(f32)
    ends, outs = 0, []
    for size in sizes:
        outs.append(r_small[ends : ends + size])
        ends += size
    return (output, input_grad, outs[0], r_in, outs[1].reshape(conv_weight.shape), outs[2], outs[3], outs[4], outs[5], outs[6], r_out)


def solution(mesh):
    placed = (
        P(("rep", "fsdp"), None),
        P(("rep", "fsdp"), None),
        P("rep", "fsdp", None),
        P("rep", "fsdp", None),
        P("fsdp"),
        P("fsdp", None),
        P(None, "fsdp"),
        P("fsdp"),
        P("fsdp"),
        P("fsdp"),
        P("fsdp"),
        P("fsdp"),
        P("fsdp", None),
    )
    return jax.shard_map(
        per_device,
        mesh=mesh,
        in_specs=placed,
        out_specs=(
            P(("rep", "fsdp"), None),
            P(("rep", "fsdp"), None),
            P("fsdp"),
            P("fsdp", None),
            P(None, "fsdp"),
            P("fsdp"),
            P("fsdp"),
            P("fsdp"),
            P("fsdp"),
            P("fsdp"),
            P("fsdp", None),
        ),
        check_vma=False,
    )
```

```python
import functools

import jax
import jax.numpy as jnp
from jax import lax
from jax.experimental import pallas as pl
from jax.experimental.pallas import tpu as pltpu
from jax.sharding import PartitionSpec as P

DI = 3072
HEAD_DIM = 64
NSTATE = 128
KW = 4
HEADS = 48
BCD = 384

epsilon = 1e-05


Q = 128
GROUP = 8
LANES = GROUP * HEAD_DIM
NEG = -1e30
VMEM = 56 * 1024 * 1024


def dot32(a, b, dims=(((1,), (0,)), ((), ())), precision=None):
    return lax.dot_general(a, b, dims, preferred_element_type=jnp.float32, precision=precision)


NT = (((1,), (1,)), ((), ()))


def row_ids(start, rows, cols):
    return lax.broadcasted_iota(jnp.int32, (rows, cols), 0) + start


def shifted_down(ref, cols, c, first, width):
    if c == 0:
        tall = jnp.concatenate([jnp.zeros((8, width), jnp.float32), ref[0:Q, cols]], axis=0)
    else:
        tall = ref[c * Q - 8 : c * Q + Q, cols]
    place = row_ids(c * Q, Q, width)
    outs = [tall[8:]]
    for j in range(1, KW):
        moved = pltpu.roll(tall, j, 0)[8:]
        keep = (place >= j) & ((place < first) | (place >= first + j))
        outs.append(jnp.where(keep, moved, 0.0))
    return outs


def conv_back(ref, cols, c, first, width, taps):
    tall = ref[c * Q : c * Q + Q + 8, cols]
    place = row_ids(c * Q, Q, width)
    total = taps[KW - 1] * tall[:Q]
    for j in range(1, KW):
        moved = pltpu.roll(tall, Q + 8 - j, 0)[:Q]
        keep = (place < first - j) | (place >= first)
        total = total + taps[KW - 1 - j] * jnp.where(keep, moved, 0.0)
    return total


def sum_rows(v):
    return jnp.sum(v, axis=0, keepdims=True)


def prep_kernel(first_ref, bcd_ref, conv_ref, head_ref, bn_ref, cn_ref, bt_ref, ct_ref, s_ref, st_ref, cum_ref, cp_ref, cumt_ref, cpt_ref):
    first = first_ref[0]
    tri = (row_ids(0, Q, Q) >= lax.broadcasted_iota(jnp.int32, (Q, Q), 1)).astype(jnp.float32)
    rate = -jnp.exp(head_ref[1:2, :])
    lane = lax.broadcasted_iota(jnp.int32, (Q, 128), 1)
    for c in range(bcd_ref.shape[0] // Q):
        rows = slice(c * Q, c * Q + Q)
        moved = shifted_down(bcd_ref, slice(0, 2 * NSTATE), c, first, 2 * NSTATE)
        mixed = conv_ref[4:5, :] + conv_ref[3:4, :] * moved[0]
        for j in range(1, KW):
            mixed = mixed + conv_ref[KW - 1 - j : KW - j, :] * moved[j]
        act = mixed * jax.nn.sigmoid(mixed)
        b32, c32 = act[:, :NSTATE], act[:, NSTATE:]
        b16, c16 = b32.astype(jnp.bfloat16), c32.astype(jnp.bfloat16)
        bn_ref[rows, :] = b16
        cn_ref[rows, :] = c16
        bt_ref[:, rows] = b32.T.astype(jnp.bfloat16)
        ct_ref[:, rows] = c32.T.astype(jnp.bfloat16)
        s_ref[rows, :] = dot32(c16, b16, NT)
        st_ref[rows, :] = dot32(b16, c16, NT)
        raw = jnp.where(lane < HEADS, bcd_ref[rows, 2 * NSTATE :] + head_ref[0:1, :], 0.0)
        step = jax.nn.softplus(raw)
        cum = dot32(tri, rate * step, precision=lax.Precision.HIGHEST)
        cp = cum - jnp.log(jnp.maximum(step, 1e-37))
        cum_ref[rows, :] = cum
        cp_ref[rows, :] = cp
        cumt_ref[:, rows] = cum.T
        cpt_ref[:, rows] = cp.T


def chunk_masks(first, c, transposed):
    base = c * Q
    row = row_ids(base, Q, Q)
    col = lax.broadcasted_iota(jnp.int32, (Q, Q), 1) + base
    ordered = (col >= row) if transposed else (row >= col)
    inside = ordered & ((row >= first) == (col >= first))
    carry = ((row >= first) == (base - 1 >= first)) & (base > 0)
    last = (row >= first) == (base + Q - 1 >= first)
    through = (base > 0) & ((base + Q - 1 >= first) == (base - 1 >= first))
    return inside, carry, last, through


def lane_column(values, k):
    return jnp.broadcast_to(values[:, k : k + 1], (Q, Q))


def forward_kernel(base, first_ref, z_ref, x_ref, conv_ref, gain_ref, bn_ref, cn_ref, bt_ref, s_ref, cum_ref, cp_ref, cpt_ref, y_ref, g_ref, sq_ref, states_ref, state):
    first = first_ref[0]
    group = base + pl.program_id(0)
    half = lax.broadcasted_iota(jnp.int32, (Q, Q), 1) < HEAD_DIM
    state[...] = jnp.zeros_like(state)

    @pl.when(pl.program_id(0) == 0)
    def _():
        sq_ref[...] = jnp.zeros_like(sq_ref)

    shift = (Q - GROUP * group) % Q
    for c in range(x_ref.shape[0] // Q):
        rows = slice(c * Q, c * Q + Q)
        inside, carry, last, through = chunk_masks(first, c, False)
        cum = pltpu.roll(cum_ref[rows, :], shift, 1)
        cp = pltpu.roll(cp_ref[rows, :], shift, 1)
        cpt = cpt_ref[pl.ds(pl.multiple_of(group * GROUP, GROUP), GROUP), rows]
        scores = s_ref[rows, :]
        c16 = cn_ref[rows, :]
        squares = jnp.zeros((Q, Q), jnp.float32)
        for p in range(GROUP // 2):
            cols = slice(p * Q, p * Q + Q)
            moved = shifted_down(x_ref, cols, c, first, Q)
            mixed = conv_ref[4:5, cols] + conv_ref[3:4, cols] * moved[0]
            for j in range(1, KW):
                mixed = mixed + conv_ref[KW - 1 - j : KW - j, cols] * moved[j]
            xs = mixed * jax.nn.sigmoid(mixed)
            x16 = xs.astype(jnp.bfloat16)
            locals_, cums, cps = [], [], []
            for e in range(2):
                k = 2 * p + e
                cum_b = lane_column(cum, k)
                decay = jnp.exp(jnp.where(inside, cum_b - cpt[k : k + 1, :], NEG))
                locals_.append(dot32((scores * decay).astype(jnp.bfloat16), x16))
                cums.append(cum_b)
                cps.append(lane_column(cp, k))
            cum_pair = jnp.where(half, cums[0], cums[1])
            cp_pair = jnp.where(half, cps[0], cps[1])
            y = jnp.where(half, locals_[0], locals_[1])
            old = state[:, cols]
            old16 = old.astype(jnp.bfloat16)
            states_ref[c * NSTATE : (c + 1) * NSTATE, cols] = old16
            if c > 0:
                y = y + jnp.where(carry, jnp.exp(cum_pair), 0.0) * dot32(c16, old16)
            y_ref[rows, cols] = y
            end = cum_pair[Q - 1 : Q, :]
            weight = jnp.where(last, jnp.exp(end - cp_pair), 0.0)
            fresh = dot32(bt_ref[:, rows], (weight * xs).astype(jnp.bfloat16))
            keep = jnp.where(through, jnp.exp(end), 0.0)
            state[:, cols] = fresh if c == 0 else keep * old + fresh
            zv = z_ref[rows, cols]
            g = (y + gain_ref[0:1, cols] * xs) * (zv * jax.nn.sigmoid(zv))
            g_ref[rows, cols] = g
            squares = squares + g * g
        sq_ref[rows, :] += squares


def split_dot(values, right):
    high = values.astype(jnp.bfloat16)
    low = (values - high.astype(jnp.float32)).astype(jnp.bfloat16)
    return dot32(high, right) + dot32(low, right)


def backward_kernel(base, count, first_ref, z_ref, x_ref, y_ref, dg_ref, rk_ref, conv_ref, gain_ref, bn_ref, cn_ref, ct_ref, st_ref, cum_ref, cp_ref, cumt_ref, states_ref, d_ref, grads_ref, dst_ref, db_ref, dc_ref, u_ref, v_ref, w_ref, flow_ref, dstate, dconv):
    first = first_ref[0]
    group = base + pl.program_id(0)
    lane = lax.broadcasted_iota(jnp.int32, (Q, Q), 1)
    half = lane < HEAD_DIM
    dstate[...] = jnp.zeros_like(dstate)
    rows_all = x_ref.shape[0]
    dconv[rows_all : rows_all + 8, :] = jnp.zeros((8, dconv.shape[1]), jnp.float32)
    grads_ref[...] = jnp.zeros_like(grads_ref)
    flow_ref[...] = jnp.zeros_like(flow_ref)

    @pl.when(pl.program_id(0) == 0)
    def _():
        for ref in (dst_ref, db_ref, dc_ref, u_ref, v_ref, w_ref):
            ref[...] = jnp.zeros_like(ref)

    shift = (Q - GROUP * group) % Q
    chunks = rows_all // Q
    for c in range(chunks - 1, -1, -1):
        rows = slice(c * Q, c * Q + Q)
        inside, carry, last, through = chunk_masks(first, c, True)
        cum = pltpu.roll(cum_ref[rows, :], shift, 1)
        cp = pltpu.roll(cp_ref[rows, :], shift, 1)
        cumt = cumt_ref[pl.ds(pl.multiple_of(group * GROUP, GROUP), GROUP), rows]
        scores_t = st_ref[rows, :]
        b16, c16t = bn_ref[rows, :], ct_ref[:, rows]
        scale = lane_column(rk_ref[rows, :], 0)
        pull = lane_column(rk_ref[rows, :], 1)
        dst = jnp.zeros((Q, Q), jnp.float32)
        db = jnp.zeros((Q, NSTATE), jnp.float32)
        dc = jnp.zeros((Q, NSTATE), jnp.float32)
        us, vs, ws = (jnp.zeros((Q, Q), jnp.float32) for _ in range(3))
        for p in range(GROUP // 2):
            cols = slice(p * Q, p * Q + Q)
            moved = shifted_down(x_ref, cols, c, first, Q)
            mixed = conv_ref[4:5, cols] + conv_ref[3:4, cols] * moved[0]
            for j in range(1, KW):
                mixed = mixed + conv_ref[KW - 1 - j : KW - j, cols] * moved[j]
            sx = jax.nn.sigmoid(mixed)
            xs = mixed * sx
            x16 = xs.astype(jnp.bfloat16)
            zv = z_ref[rows, cols]
            sz = jax.nn.sigmoid(zv)
            silu_z = zv * sz
            skip, gain = gain_ref[0:1, cols], gain_ref[1:2, cols]
            y = y_ref[rows, cols]
            ssm = y + skip * xs
            g = ssm * silu_z
            gs = dg_ref[rows, cols] * scale
            grads_ref[6:7, cols] += sum_rows(gs * g)
            d_g = gain * gs - g * pull
            z_cols = pl.ds(pl.multiple_of(pl.program_id(0) * LANES + p * Q, Q), Q)
            d_ref[rows, z_cols] = (d_g * ssm * (sz + silu_z * (1.0 - sz))).astype(d_ref.dtype)
            d_ssm = d_g * silu_z
            grads_ref[5:6, cols] += sum_rows(d_ssm * xs)
            dy16 = d_ssm.astype(jnp.bfloat16)
            locals_, cums, cps = [], [], []
            for e in range(2):
                k = 2 * p + e
                cp_b = lane_column(cp, k)
                decay = jnp.exp(jnp.where(inside, cumt[k : k + 1, :] - cp_b, NEG))
                locals_.append(dot32((scores_t * decay).astype(jnp.bfloat16), dy16))
                x_half = jnp.where(half == (e == 0), x16, jnp.zeros_like(x16))
                dst = dst + decay * dot32(x_half, dy16, NT)
                cums.append(lane_column(cum, k))
                cps.append(cp_b)
            cum_pair = jnp.where(half, cums[0], cums[1])
            cp_pair = jnp.where(half, cps[0], cps[1])
            dx = jnp.where(half, locals_[0], locals_[1])
            dy32, x32 = dy16.astype(jnp.float32), x16.astype(jnp.float32)
            pick = (lane == GROUP * group + 2 * p + (row_ids(0, Q, Q) >= HEAD_DIM).astype(jnp.int32)).astype(jnp.bfloat16)
            in_dot = x32 * dx
            us = us + split_dot(dy32 * y - in_dot, pick)
            vs = vs + split_dot(in_dot, pick)
            end = cum_pair[Q - 1 : Q, :]
            keep = jnp.where(through, jnp.exp(end), 0.0)
            if c < chunks - 1:
                later = dstate[:, cols]
                later16 = later.astype(jnp.bfloat16)
                weight = jnp.where(last, jnp.exp(end - cp_pair), 0.0)
                carried = weight * dot32(b16, later16)
                dx = dx + carried
                ws = ws + split_dot(xs * carried, pick)
                db = db + dot32((weight * xs).astype(jnp.bfloat16), later16, NT)
            if c > 0:
                ey16 = (jnp.where(carry, jnp.exp(cum_pair), 0.0) * d_ssm).astype(jnp.bfloat16)
                old16 = states_ref[c * NSTATE : (c + 1) * NSTATE, cols]
                dc = dc + dot32(ey16, old16, NT)
                fresh = dot32(c16t, ey16)
                if c < chunks - 1:
                    flow_ref[c : c + 1, cols] = keep * sum_rows(later * old16.astype(jnp.float32))
                    fresh = keep * later + fresh
                dstate[:, cols] = fresh
            d_mixed = (dx + skip * d_ssm) * (sx + xs * (1.0 - sx))
            dconv[rows, cols] = d_mixed
            grads_ref[4:5, cols] += sum_rows(d_mixed)
            for j in range(KW):
                grads_ref[KW - 1 - j : KW - j, cols] += sum_rows(d_mixed * moved[j])
            taps = [conv_ref[i : i + 1, cols] for i in range(KW)]
            x_cols = pl.ds(pl.multiple_of((pl.program_id(0) + count) * LANES + p * Q, Q), Q)
            d_ref[rows, x_cols] = conv_back(dconv, cols, c, first, Q, taps).astype(d_ref.dtype)
        dst_ref[rows, :] += dst
        db_ref[rows, :] += db
        dc_ref[rows, :] += dc
        u_ref[rows, :] += us
        v_ref[rows, :] += vs
        w_ref[rows, :] += ws


def post_kernel(first_ref, bcd_ref, conv_ref, head_ref, bn_ref, cn_ref, dst_ref, db_ref, dc_ref, u_ref, v_ref, w_ref, flow_ref, d_ref, grads_ref, hgrads_ref, dconv):
    first = first_ref[0]
    rows_all = bcd_ref.shape[0]
    wide = 2 * NSTATE
    dconv[rows_all : rows_all + 8, :] = jnp.zeros((8, wide), jnp.float32)
    grads_ref[...] = jnp.zeros_like(grads_ref)
    hgrads_ref[...] = jnp.zeros_like(hgrads_ref)
    lane = lax.broadcasted_iota(jnp.int32, (Q, 128), 1)
    rate = -jnp.exp(head_ref[1:2, :])
    spread = (lax.broadcasted_iota(jnp.int32, (DI, 128), 0) // HEAD_DIM == lax.broadcasted_iota(jnp.int32, (DI, 128), 1)).astype(jnp.float32)
    flow = dot32(flow_ref[...], spread, precision=lax.Precision.HIGHEST)
    row, col = row_ids(0, Q, Q), lax.broadcasted_iota(jnp.int32, (Q, Q), 1)
    earlier_sum = (col < row).astype(jnp.float32)
    for c in range(rows_all // Q - 1, -1, -1):
        rows = slice(c * Q, c * Q + Q)
        moved = shifted_down(bcd_ref, slice(0, wide), c, first, wide)
        mixed = conv_ref[4:5, :] + conv_ref[3:4, :] * moved[0]
        for j in range(1, KW):
            mixed = mixed + conv_ref[KW - 1 - j : KW - j, :] * moved[j]
        sx = jax.nn.sigmoid(mixed)
        dst = jnp.sum(dst_ref[:, rows, :], axis=0)
        d_b = jnp.sum(db_ref[:, rows, :], axis=0) + dot32(dst.astype(jnp.bfloat16), cn_ref[rows, :])
        d_c = jnp.sum(dc_ref[:, rows, :], axis=0) + dot32(dst.T.astype(jnp.bfloat16), bn_ref[rows, :])
        d_mixed = jnp.concatenate([d_b, d_c], axis=1) * (sx + mixed * sx * (1.0 - sx))
        dconv[rows, :] = d_mixed
        grads_ref[4:5, :] += sum_rows(d_mixed)
        for j in range(KW):
            grads_ref[KW - 1 - j : KW - j, :] += sum_rows(d_mixed * moved[j])
        taps = [conv_ref[i : i + 1, :] for i in range(KW)]
        d_ref[rows, :wide] = conv_back(dconv, slice(0, wide), c, first, wide, taps).astype(d_ref.dtype)
        carried = jnp.sum(w_ref[:, rows, :], axis=0)
        later_sum = ((col >= row) & ((row + c * Q >= first) == (col + c * Q >= first))).astype(jnp.float32)
        d_la = dot32(later_sum, jnp.sum(u_ref[:, rows, :], axis=0), precision=lax.Precision.HIGHEST)
        d_la = d_la + dot32(earlier_sum, carried, precision=lax.Precision.HIGHEST) + flow[c : c + 1, :]
        d_log = jnp.sum(v_ref[:, rows, :], axis=0) + carried
        raw = bcd_ref[rows, wide:] + head_ref[0:1, :]
        step = jax.nn.softplus(raw)
        sig = jax.nn.sigmoid(raw)
        ratio = jnp.where(raw < -17.0, 1.0, sig / jnp.maximum(step, 1e-37))
        d_raw = jnp.where(lane < HEADS, d_log * ratio + d_la * rate * sig, 0.0)
        d_ref[rows, wide:] = d_raw.astype(d_ref.dtype)
        hgrads_ref[0:1, :] += sum_rows(d_raw)
        hgrads_ref[1:2, :] += sum_rows(jnp.where(lane < HEADS, d_la * rate * step, 0.0))


def smem():
    return pl.BlockSpec(memory_space=pltpu.SMEM)


def whole(shape):
    return pl.BlockSpec(shape, lambda g: (0,) * len(shape))


def run_prep(first, bcd, conv, heads):
    rows = bcd.shape[0]
    f32, b16 = jnp.float32, jnp.bfloat16
    shapes = [((rows, 128), b16), ((rows, 128), b16), ((128, rows), b16), ((128, rows), b16), ((rows, Q), f32), ((rows, Q), f32), ((rows, 128), f32), ((rows, 128), f32), ((128, rows), f32), ((128, rows), f32)]
    return pl.pallas_call(
        prep_kernel,
        grid=(1,),
        in_specs=[smem(), whole((rows, BCD)), whole((8, 2 * NSTATE)), whole((8, 128))],
        out_specs=[whole(s) for s, _ in shapes],
        out_shape=[jax.ShapeDtypeStruct(s, d) for s, d in shapes],
        compiler_params=pltpu.CompilerParams(vmem_limit_bytes=VMEM),
    )(first, bcd, conv, heads)


def run_forward(base, count, first, zx, conv, gains, prep):
    rows = zx.shape[0]
    bn, cn, bt, ct, s, st, cum, cp, cumt, cpt = prep
    f32, b16 = jnp.float32, jnp.bfloat16
    chunks = rows // Q
    at = lambda g: (0, g + base)
    here = lambda g: (0, g)
    return pl.pallas_call(
        functools.partial(forward_kernel, base),
        grid=(count,),
        in_specs=[smem(), pl.BlockSpec((rows, LANES), here), pl.BlockSpec((rows, LANES), lambda g: (0, g + count)), pl.BlockSpec((8, LANES), at), pl.BlockSpec((8, LANES), at)]
        + [whole(v.shape) for v in (bn, cn, bt, s, cum, cp, cpt)],
        out_specs=[pl.BlockSpec((rows, LANES), here), pl.BlockSpec((rows, LANES), here), whole((rows, Q)), pl.BlockSpec((chunks * NSTATE, LANES), here)],
        out_shape=[jax.ShapeDtypeStruct((rows, count * LANES), f32), jax.ShapeDtypeStruct((rows, count * LANES), f32), jax.ShapeDtypeStruct((rows, Q), f32), jax.ShapeDtypeStruct((chunks * NSTATE, count * LANES), b16)],
        scratch_shapes=[pltpu.VMEM((NSTATE, LANES), f32)],
        compiler_params=pltpu.CompilerParams(vmem_limit_bytes=VMEM),
        cost_estimate=pl.CostEstimate(flops=count * 1200000000, bytes_accessed=count * 6000000, transcendentals=0),
    )(first, zx, zx, conv, gains, bn, cn, bt, s, cum, cp, cpt)


def run_backward(base, count, first, zx, y, dg, rk, conv, gains, prep, states):
    rows = zx.shape[0]
    bn, cn, bt, ct, s, st, cum, cp, cumt, cpt = prep
    f32, b16 = jnp.float32, jnp.bfloat16
    chunks = rows // Q
    at = lambda g: (0, g + base)
    here = lambda g: (0, g)
    local = pl.BlockSpec((rows, LANES), here)
    sums = [(rows, Q), (rows, NSTATE), (rows, NSTATE), (rows, 128), (rows, 128), (rows, 128)]
    return pl.pallas_call(
        functools.partial(backward_kernel, base, count),
        grid=(count,),
        in_specs=[smem(), local, pl.BlockSpec((rows, LANES), lambda g: (0, g + count)), local, local, whole(rk.shape), pl.BlockSpec((8, LANES), at), pl.BlockSpec((8, LANES), at)]
        + [whole(v.shape) for v in (bn, cn, ct, st, cum, cp, cumt)]
        + [pl.BlockSpec((chunks * NSTATE, LANES), here)],
        out_specs=[whole((rows, 2 * count * LANES)), pl.BlockSpec((8, LANES), here)] + [whole(v) for v in sums] + [pl.BlockSpec((8, LANES), here)],
        out_shape=[jax.ShapeDtypeStruct((rows, 2 * count * LANES), b16)] + [jax.ShapeDtypeStruct((8, count * LANES), f32)] + [jax.ShapeDtypeStruct(v, f32) for v in sums] + [jax.ShapeDtypeStruct((8, count * LANES), f32)],
        scratch_shapes=[pltpu.VMEM((NSTATE, LANES), f32), pltpu.VMEM((rows + 8, LANES), f32)],
        compiler_params=pltpu.CompilerParams(vmem_limit_bytes=VMEM),
        cost_estimate=pl.CostEstimate(flops=count * 4000000000, bytes_accessed=count * 8000000, transcendentals=0),
    )(first, zx, zx, y, dg, rk, conv, gains, bn, cn, ct, st, cum, cp, cumt, states)


def run_post(first, bcd, conv, heads, prep, *sums):
    rows = bcd.shape[0]
    bn, cn = prep[0], prep[1]
    f32 = jnp.float32
    return pl.pallas_call(
        post_kernel,
        grid=(1,),
        in_specs=[smem(), whole((rows, BCD)), whole((8, 2 * NSTATE)), whole((8, 128)), whole(bn.shape), whole(cn.shape)] + [whole(t.shape) for t in sums],
        out_specs=[whole((rows, BCD)), whole((8, 2 * NSTATE)), whole((8, 128))],
        out_shape=[jax.ShapeDtypeStruct((rows, BCD), jnp.bfloat16), jax.ShapeDtypeStruct((8, 2 * NSTATE), f32), jax.ShapeDtypeStruct((8, 128), f32)],
        scratch_shapes=[pltpu.VMEM((rows + 8, 2 * NSTATE), f32)],
        compiler_params=pltpu.CompilerParams(vmem_limit_bytes=VMEM),
    )(first, bcd, conv, heads, bn, cn, *sums)


def contract_rows(left, right, kind=jnp.float32):
    return lax.dot_general(left, right, (((0,), (0,)), ((), ())), preferred_element_type=kind)


def contract_cols(left, right):
    return lax.dot_general(left, right, NT, preferred_element_type=jnp.float32)


def pad_lanes(v, width):
    return jnp.pad(v, ((0, 0), (0, width - v.shape[1])))


PARTS = 3
ORDER = (1, 3, 5, 7, 6, 2, 4, 0)


def swap(v, bit):
    return lax.ppermute(v, "fsdp", [(i, i ^ bit) for i in range(lax.axis_size("fsdp"))])


def across(v, pairs):
    return lax.ppermute(v, "rep", pairs)


def gather_rows(w):
    groups = lax.axis_size("fsdp")
    if groups != 8:
        return lax.all_gather(w, "fsdp", axis=0, tiled=True)
    rows = w.shape[0]
    one, two, four = swap(w, 1), swap(w, 2), swap(w, 4)
    six = jnp.concatenate([swap(two[: rows // 2], 4), swap(four[rows // 2 :], 2)])
    three, five, seven = swap(two, 1), swap(four, 1), swap(six, 1)
    me = lax.axis_index("fsdp")
    full = jnp.zeros((groups * rows, w.shape[1]), w.dtype)
    for j, piece in enumerate((w, one, two, three, four, five, six, seven)):
        full = lax.dynamic_update_slice(full, piece, ((me ^ j) * rows, 0))
    return full


def send_order(v, blocks):
    if blocks != 8:
        return v
    me = lax.axis_index("fsdp")
    step = v.shape[1] // blocks
    return jnp.concatenate([lax.dynamic_slice(v, (0, (me ^ j) * step), (v.shape[0], step)) for j in ORDER], axis=1)


def scatter_term(left, right):
    groups = lax.axis_size("fsdp")
    b16 = jnp.bfloat16
    if groups != 8:
        return lax.psum_scatter(contract_rows(left, right, b16), "fsdp", scatter_dimension=0, tiled=True).astype(jnp.float32)
    rows = left.shape[1] // groups
    half = rows // 2
    got = swap(contract_rows(left[:, : 4 * rows], right).astype(b16), 1).astype(jnp.float32)
    diag = (contract_rows(left[:, 4 * rows : 5 * rows], right) + got[3 * rows :]).astype(b16)
    from_x, from_y = swap(diag[:half], 2), swap(diag[half:], 4)
    low = jnp.pad(from_y.astype(jnp.float32), ((half, 0), (0, 0)))
    high = jnp.pad(from_x.astype(jnp.float32), ((0, half), (0, 0)))
    to_x = (contract_rows(left[:, 5 * rows : 6 * rows], right) + got[rows : 2 * rows] + low).astype(b16)
    to_y = (contract_rows(left[:, 6 * rows : 7 * rows], right) + got[2 * rows : 3 * rows] + high).astype(b16)
    got_x, got_y = swap(to_x, 2), swap(to_y, 4)
    return contract_rows(left[:, 7 * rows :], right) + got[:rows] + got_x.astype(jnp.float32) + got_y.astype(jnp.float32)


def sum_rep(own):
    b16 = jnp.bfloat16
    if lax.axis_size("rep") != 4:
        return lax.psum(own.astype(b16), "rep")
    place = lax.axis_index("rep")
    inner = (place == 1) | (place == 2)
    half = own.shape[0] // 2
    pair = own + across(own.astype(b16), [(0, 1), (3, 2)]).astype(jnp.float32)
    top, bottom = pair[:half], pair[half:]
    got = across(jnp.where(place == 1, bottom, top).astype(b16), [(1, 2), (2, 1)])
    mine = (jnp.where(place == 1, top, bottom) + got.astype(jnp.float32)).astype(b16)
    other = across(mine, [(1, 2), (2, 1)])
    full = jnp.where(place == 1, jnp.concatenate([mine, other]), jnp.concatenate([other, mine]))
    return jnp.where(inner, full, across(full, [(1, 0), (2, 3)]))


def per_device(tokens, cotangent, lengths, dealing, norm_gain, in_weight, conv_weight, conv_bias, dt_bias, a_log, d_skip, gated_gain, out_weight):
    f32, b16 = jnp.float32, jnp.bfloat16
    groups = lax.axis_size("fsdp")
    tok_rows, width = tokens.shape
    block_rows = tok_rows // groups
    targets = dealing.reshape(groups)
    inverse = jnp.argsort(targets)
    first = lengths.reshape(-1)[:1]
    count = HEADS // GROUP // PARTS
    lanes = count * LANES

    def deal(values):
        blocks = values.reshape(groups, block_rows, width)[inverse]
        return lax.all_to_all(blocks, "fsdp", split_axis=0, concat_axis=0, tiled=True).reshape(tok_rows, width)

    def undeal(values):
        blocks = lax.all_to_all(values.reshape(groups, block_rows, width), "fsdp", split_axis=0, concat_axis=0, tiled=True)
        return blocks[targets].reshape(tok_rows, width)

    small = jnp.concatenate([norm_gain, conv_weight.reshape(-1), conv_bias, dt_bias, a_log, d_skip, gated_gain])
    sizes = [v.size for v in (norm_gain, conv_weight, conv_bias, dt_bias, a_log, d_skip, gated_gain)]
    small_all = lax.all_gather(jnp.pad(small, (0, -small.size % 128)), "fsdp", axis=0, tiled=False).astype(f32)
    hidden = deal(tokens).astype(f32)
    w_b = gather_rows(pad_lanes(in_weight[:, 2 * DI :], BCD))
    w_zx = [gather_rows(jnp.concatenate([in_weight[:, k * lanes : (k + 1) * lanes], in_weight[:, DI + k * lanes : DI + (k + 1) * lanes]], axis=1)) for k in range(PARTS)]
    cot = deal(cotangent)
    out_full = gather_rows(out_weight)

    ends, parts = 0, []
    for size in sizes:
        parts.append(small_all[:, ends : ends + size])
        ends += size
    gain = parts[0].reshape(1, -1)
    taps = parts[1].reshape(groups, KW, -1).transpose(1, 0, 2).reshape(KW, -1)
    bias, step_bias, rate, skip, ggain = (v.reshape(1, -1) for v in parts[2:])
    conv = jnp.concatenate([taps, bias, jnp.zeros((3, bias.shape[1]), f32)])
    heads = pad_lanes(jnp.concatenate([step_bias, rate, jnp.zeros((6, HEADS), f32)]), 128)
    gains = jnp.concatenate([jnp.repeat(skip, HEAD_DIM, axis=1), ggain, jnp.zeros((6, DI), f32)])
    conv_x, conv_bc = conv[:, :DI], conv[:, DI:]

    rn = lax.rsqrt(jnp.mean(hidden * hidden, axis=-1, keepdims=True) + epsilon)
    normed = (hidden * rn * gain).astype(b16)
    normed_sent = send_order(normed, groups)
    bcd = jnp.dot(normed, w_b, preferred_element_type=f32)
    prep = run_prep(first, bcd, conv_bc, heads)
    zx, ys, gs, sqs, states = [], [], [], [], []
    for k in range(PARTS):
        zx.append(jnp.dot(normed, w_zx[k], preferred_element_type=f32))
        y, g, sq, state = run_forward(k * count, count, first, zx[k], conv_x, gains, prep)
        ys.append(y)
        gs.append(g)
        sqs.append(sq)
        states.append(state)
    r = lax.rsqrt(jnp.sum(sum(sqs), axis=-1, keepdims=True) / DI + epsilon)
    gated = (jnp.concatenate(gs, axis=1) * r * ggain).astype(b16)
    branch = jnp.dot(gated, out_full, preferred_element_type=f32)
    output = undeal((hidden + branch).astype(b16))
    cot32 = cot.astype(f32)
    pull = r * r * (jnp.sum(cot32 * branch, axis=-1, keepdims=True) / DI)
    rk = pad_lanes(jnp.concatenate([r, pull], axis=1), 128)
    r_out = sum_rep(scatter_term(send_order(gated, groups), cot)).astype(f32)

    d_zx, xgrads, sums, flows, r_in = [], [], [], [], []
    for k in range(PARTS):
        d_gated = contract_cols(cot, out_full[k * lanes : (k + 1) * lanes])
        d, grads, *more, flow = run_backward(k * count, count, first, zx[k], ys[k], d_gated, rk, conv_x, gains, prep, states[k])
        d_zx.append(d)
        xgrads.append(grads)
        sums.append(more)
        flows.append(flow)
        r_in.append(sum_rep(scatter_term(normed_sent, d)))
    d_b, bgrads, hgrads = run_post(first, bcd, conv_bc, heads, prep, *[jnp.stack(t) for t in zip(*sums)], jnp.concatenate(flows, axis=1))
    r_b = sum_rep(scatter_term(normed_sent, d_b))
    d_normed = contract_cols(d_b, w_b)
    for k in range(PARTS):
        d_normed = d_normed + contract_cols(d_zx[k], w_zx[k])
    xgrads = jnp.concatenate(xgrads, axis=1)
    g_gain = jnp.sum(d_normed * hidden * rn, axis=0)
    d_scaled = d_normed * gain
    d_hidden = rn * d_scaled - hidden * (rn * rn * rn * jnp.mean(hidden * d_scaled, axis=-1, keepdims=True))
    input_grad = undeal((cot32 + d_hidden).astype(b16))

    g_conv = jnp.concatenate([xgrads[:KW], bgrads[:KW]], axis=1)
    g_cbias = jnp.concatenate([xgrads[KW], bgrads[KW]])
    g_dskip = jnp.sum(xgrads[5].reshape(HEADS, HEAD_DIM), axis=1)
    spread = [
        g_gain.reshape(groups, -1),
        g_conv.reshape(KW, groups, -1).transpose(1, 0, 2).reshape(groups, -1),
        g_cbias.reshape(groups, -1),
        hgrads[0, :HEADS].reshape(groups, -1),
        hgrads[1, :HEADS].reshape(groups, -1),
        g_dskip.reshape(groups, -1),
        xgrads[6].reshape(groups, -1),
    ]
    packed = pad_lanes(jnp.concatenate(spread, axis=1), small_all.shape[1])
    s_small = jnp.sum(lax.all_to_all(packed, "fsdp", split_axis=0, concat_axis=0, tiled=True), axis=0)
    r_small = jnp.sum(lax.all_gather(s_small, "rep", axis=0, tiled=False), axis=0)
    pieces = [v[:, :lanes] for v in r_in] + [v[:, lanes:] for v in r_in] + [r_b[:, : in_weight.shape[1] - 2 * DI]]
    r_in = jnp.concatenate(pieces, axis=1).astype(f32)
    ends, outs = 0, []
    for size in sizes:
        outs.append(r_small[ends : ends + size])
        ends += size
    return (output, input_grad, outs[0], r_in, outs[1].reshape(conv_weight.shape), outs[2], outs[3], outs[4], outs[5], outs[6], r_out)


def solution(mesh):
    placed = (
        P(("rep", "fsdp"), None),
        P(("rep", "fsdp"), None),
        P("rep", "fsdp", None),
        P("rep", "fsdp", None),
        P("fsdp"),
        P("fsdp", None),
        P(None, "fsdp"),
        P("fsdp"),
        P("fsdp"),
        P("fsdp"),
        P("fsdp"),
        P("fsdp"),
        P("fsdp", None),
    )
    return jax.shard_map(
        per_device,
        mesh=mesh,
        in_specs=placed,
        out_specs=(
            P(("rep", "fsdp"), None),
            P(("rep", "fsdp"), None),
            P("fsdp"),
            P("fsdp", None),
            P(None, "fsdp"),
            P("fsdp"),
            P("fsdp"),
            P("fsdp"),
            P("fsdp"),
            P("fsdp"),
            P("fsdp", None),
        ),
        check_vma=False,
    )
```

```python
import functools

import jax
import jax.numpy as jnp
from jax import lax
from jax.experimental import pallas as pl
from jax.experimental.pallas import tpu as pltpu
from jax.sharding import PartitionSpec as P

DI = 3072
HEAD_DIM = 64
NSTATE = 128
KW = 4
HEADS = 48
BCD = 384

epsilon = 1e-05


Q = 128
GROUP = 8
LANES = GROUP * HEAD_DIM
NEG = -1e30
VMEM = 56 * 1024 * 1024
BIG = 56 * 1024 * 1024


def dot32(a, b, dims=(((1,), (0,)), ((), ())), precision=None):
    return lax.dot_general(a, b, dims, preferred_element_type=jnp.float32, precision=precision)


NT = (((1,), (1,)), ((), ()))


def row_ids(start, rows, cols):
    return lax.broadcasted_iota(jnp.int32, (rows, cols), 0) + start


def shifted_down(ref, cols, c, first, width):
    if c == 0:
        tall = jnp.concatenate([jnp.zeros((8, width), jnp.float32), ref[0:Q, cols]], axis=0)
    else:
        tall = ref[c * Q - 8 : c * Q + Q, cols]
    place = row_ids(c * Q, Q, width)
    outs = [tall[8:]]
    for j in range(1, KW):
        moved = pltpu.roll(tall, j, 0)[8:]
        keep = (place >= j) & ((place < first) | (place >= first + j))
        outs.append(jnp.where(keep, moved, 0.0))
    return outs


def conv_back(ref, cols, c, first, width, taps):
    tall = ref[c * Q : c * Q + Q + 8, cols]
    place = row_ids(c * Q, Q, width)
    total = taps[KW - 1] * tall[:Q]
    for j in range(1, KW):
        moved = pltpu.roll(tall, Q + 8 - j, 0)[:Q]
        keep = (place < first - j) | (place >= first)
        total = total + taps[KW - 1 - j] * jnp.where(keep, moved, 0.0)
    return total


def sigmoid(v):
    return 0.5 * jnp.tanh(0.5 * v) + 0.5


def sum_rows(v):
    return jnp.sum(v, axis=0, keepdims=True)


def prep_kernel(first_ref, bcd_ref, conv_ref, head_ref, wide_ref, tall_ref, bc_ref, bct_ref):
    first = first_ref[0]
    tri = (row_ids(0, Q, Q) >= lax.broadcasted_iota(jnp.int32, (Q, Q), 1)).astype(jnp.float32)
    rate = -jnp.exp(head_ref[1:2, :])
    lane = lax.broadcasted_iota(jnp.int32, (Q, 128), 1)
    for c in range(bcd_ref.shape[0] // Q):
        rows = slice(c * Q, c * Q + Q)
        moved = shifted_down(bcd_ref, slice(0, 2 * NSTATE), c, first, 2 * NSTATE)
        mixed = conv_ref[4:5, :] + conv_ref[3:4, :] * moved[0]
        for j in range(1, KW):
            mixed = mixed + conv_ref[KW - 1 - j : KW - j, :] * moved[j]
        act = mixed * sigmoid(mixed)
        b32, c32 = act[:, :NSTATE], act[:, NSTATE:]
        b16, c16 = b32.astype(jnp.bfloat16), c32.astype(jnp.bfloat16)
        bc_ref[rows, :] = act.astype(jnp.bfloat16)
        bct_ref[:NSTATE, rows] = b32.T.astype(jnp.bfloat16)
        bct_ref[NSTATE:, rows] = c32.T.astype(jnp.bfloat16)
        wide_ref[rows, :Q] = dot32(c16, b16, NT)
        wide_ref[rows, Q : 2 * Q] = dot32(b16, c16, NT)
        raw = jnp.where(lane < HEADS, bcd_ref[rows, 2 * NSTATE :] + head_ref[0:1, :], 0.0)
        step = jax.nn.softplus(raw)
        cum = dot32(tri, rate * step, precision=lax.Precision.HIGHEST)
        cp = cum - jnp.log(jnp.maximum(step, 1e-37))
        wide_ref[rows, 2 * Q : 3 * Q] = cum
        wide_ref[rows, 3 * Q :] = cp
        tall_ref[:128, rows] = cum.T
        tall_ref[128:, rows] = cp.T


def chunk_masks(first, c, transposed):
    base = c * Q
    row = row_ids(base, Q, Q)
    col = lax.broadcasted_iota(jnp.int32, (Q, Q), 1) + base
    ordered = (col >= row) if transposed else (row >= col)
    inside = ordered & ((row >= first) == (col >= first))
    carry = ((row >= first) == (base - 1 >= first)) & (base > 0)
    last = (row >= first) == (base + Q - 1 >= first)
    through = (base > 0) & ((base + Q - 1 >= first) == (base - 1 >= first))
    return inside, carry, last, through


def lane_column(values, k):
    return jnp.broadcast_to(values[:, k : k + 1], (Q, Q))


def forward_kernel(first_ref, x_ref, conv_ref, gain_ref, wide_ref, tall_ref, bc_ref, bct_ref, ssm_ref, states_ref, state):
    first = first_ref[0]
    group = pl.program_id(0)
    half = lax.broadcasted_iota(jnp.int32, (Q, Q), 1) < HEAD_DIM
    state[...] = jnp.zeros_like(state)

    shift = (Q - GROUP * group) % Q
    for c in range(x_ref.shape[0] // Q):
        rows = slice(c * Q, c * Q + Q)
        inside, carry, last, through = chunk_masks(first, c, False)
        cum = pltpu.roll(wide_ref[rows, 2 * Q : 3 * Q], shift, 1)
        cp = pltpu.roll(wide_ref[rows, 3 * Q :], shift, 1)
        cpt = tall_ref[pl.ds(pl.multiple_of(128 + group * GROUP, GROUP), GROUP), rows]
        scores = wide_ref[rows, :Q]
        c16 = bc_ref[rows, NSTATE:]
        for p in range(GROUP // 2):
            cols = slice(p * Q, p * Q + Q)
            moved = shifted_down(x_ref, cols, c, first, Q)
            mixed = conv_ref[4:5, cols] + conv_ref[3:4, cols] * moved[0]
            for j in range(1, KW):
                mixed = mixed + conv_ref[KW - 1 - j : KW - j, cols] * moved[j]
            xs = mixed * sigmoid(mixed)
            x16 = xs.astype(jnp.bfloat16)
            locals_, cums, cps = [], [], []
            for e in range(2):
                k = 2 * p + e
                cum_b = lane_column(cum, k)
                decay = jnp.exp(jnp.where(inside, cum_b - cpt[k : k + 1, :], NEG))
                locals_.append(dot32((scores * decay).astype(jnp.bfloat16), x16))
                cums.append(cum_b)
                cps.append(lane_column(cp, k))
            cum_pair = jnp.where(half, cums[0], cums[1])
            cp_pair = jnp.where(half, cps[0], cps[1])
            y = jnp.where(half, locals_[0], locals_[1])
            old = state[:, cols]
            old16 = old.astype(jnp.bfloat16)
            states_ref[c * NSTATE : (c + 1) * NSTATE, cols] = old16
            if c > 0:
                y = y + jnp.where(carry, jnp.exp(cum_pair), 0.0) * dot32(c16, old16)
            ssm_ref[rows, cols] = y + gain_ref[0:1, cols] * xs
            end = cum_pair[Q - 1 : Q, :]
            weight = jnp.where(last, jnp.exp(end - cp_pair), 0.0)
            fresh = dot32(bct_ref[:NSTATE, rows], (weight * xs).astype(jnp.bfloat16))
            keep = jnp.where(through, jnp.exp(end), 0.0)
            state[:, cols] = fresh if c == 0 else keep * old + fresh


def gated_kernel(z_ref, ssm_ref, gain_ref, gated_ref, r_ref):
    squares = jnp.zeros((Q, Q), jnp.float32)
    for p in range(z_ref.shape[1] // Q):
        cols = slice(p * Q, p * Q + Q)
        zv = z_ref[:, cols]
        g = ssm_ref[:, cols] * (zv * sigmoid(zv))
        squares = squares + g * g
    r = lax.rsqrt(jnp.sum(squares, axis=-1, keepdims=True) / DI + epsilon)
    wide = jnp.broadcast_to(r, (Q, Q))
    r_ref[...] = wide
    for p in range(z_ref.shape[1] // Q):
        cols = slice(p * Q, p * Q + Q)
        zv = z_ref[:, cols]
        g = ssm_ref[:, cols] * (zv * sigmoid(zv))
        gated_ref[:, cols] = (g * wide * gain_ref[1:2, cols]).astype(gated_ref.dtype)


def gate_kernel(z_ref, ssm_ref, cot_ref, weight_ref, rk_ref, gain_ref, dz_ref, ds_ref, grads_ref):
    grads_ref[...] = jnp.zeros_like(grads_ref)
    for c in range(z_ref.shape[0] // Q):
        rows = slice(c * Q, c * Q + Q)
        scale = lane_column(rk_ref[rows, :], 0)
        pull = lane_column(rk_ref[rows, :], 1)
        d_gated = dot32(cot_ref[rows, :], weight_ref[...], NT)
        for p in range(z_ref.shape[1] // Q):
            cols = slice(p * Q, p * Q + Q)
            zv = z_ref[rows, cols]
            sz = sigmoid(zv)
            silu_z = zv * sz
            ssm = ssm_ref[rows, cols]
            g = ssm * silu_z
            gs = d_gated[:, cols] * scale
            grads_ref[0:1, cols] += sum_rows(gs * g)
            d_g = gain_ref[1:2, cols] * gs - g * pull
            dz_ref[rows, cols] = (d_g * ssm * (sz + silu_z * (1.0 - sz))).astype(dz_ref.dtype)
            ds_ref[rows, cols] = (d_g * silu_z).astype(ds_ref.dtype)


def split_dot(values, right):
    high = values.astype(jnp.bfloat16)
    low = (values - high.astype(jnp.float32)).astype(jnp.bfloat16)
    return dot32(high, right) + dot32(low, right)


def backward_kernel(base, first_ref, x_ref, ssm_ref, ds_ref, conv_ref, gain_ref, wide_ref, tall_ref, bc_ref, bct_ref, states_ref, d_ref, grads_ref, sums_ref, flow_ref, dstate, dconv):
    first = first_ref[0]
    group = base + pl.program_id(0)
    lane = lax.broadcasted_iota(jnp.int32, (Q, Q), 1)
    half = lane < HEAD_DIM
    dstate[...] = jnp.zeros_like(dstate)
    rows_all = x_ref.shape[0]
    dconv[rows_all : rows_all + 8, :] = jnp.zeros((8, dconv.shape[1]), jnp.float32)
    grads_ref[...] = jnp.zeros_like(grads_ref)
    flow_ref[...] = jnp.zeros_like(flow_ref)

    @pl.when(pl.program_id(0) == 0)
    def _():
        sums_ref[...] = jnp.zeros_like(sums_ref)

    shift = (Q - GROUP * group) % Q
    chunks = rows_all // Q
    for c in range(chunks - 1, -1, -1):
        rows = slice(c * Q, c * Q + Q)
        inside, carry, last, through = chunk_masks(first, c, True)
        cum = pltpu.roll(wide_ref[rows, 2 * Q : 3 * Q], shift, 1)
        cp = pltpu.roll(wide_ref[rows, 3 * Q :], shift, 1)
        cumt = tall_ref[pl.ds(pl.multiple_of(group * GROUP, GROUP), GROUP), rows]
        scores_t = wide_ref[rows, Q : 2 * Q]
        b16, c16t = bc_ref[rows, :NSTATE], bct_ref[NSTATE:, rows]
        dst = jnp.zeros((Q, Q), jnp.float32)
        db = jnp.zeros((Q, NSTATE), jnp.float32)
        dc = jnp.zeros((Q, NSTATE), jnp.float32)
        us, vs, ws = (jnp.zeros((Q, Q), jnp.float32) for _ in range(3))
        for p in range(GROUP // 2):
            cols = slice(p * Q, p * Q + Q)
            moved = shifted_down(x_ref, cols, c, first, Q)
            mixed = conv_ref[4:5, cols] + conv_ref[3:4, cols] * moved[0]
            for j in range(1, KW):
                mixed = mixed + conv_ref[KW - 1 - j : KW - j, cols] * moved[j]
            sx = sigmoid(mixed)
            xs = mixed * sx
            x16 = xs.astype(jnp.bfloat16)
            skip = gain_ref[0:1, cols]
            y = ssm_ref[rows, cols] - skip * xs
            dy16 = ds_ref[rows, cols]
            d_ssm = dy16.astype(jnp.float32)
            grads_ref[5:6, cols] += sum_rows(d_ssm * xs)
            locals_, cums, cps = [], [], []
            for e in range(2):
                k = 2 * p + e
                cp_b = lane_column(cp, k)
                decay = jnp.exp(jnp.where(inside, cumt[k : k + 1, :] - cp_b, NEG))
                locals_.append(dot32((scores_t * decay).astype(jnp.bfloat16), dy16))
                x_half = jnp.where(half == (e == 0), x16, jnp.zeros_like(x16))
                dst = dst + decay * dot32(x_half, dy16, NT)
                cums.append(lane_column(cum, k))
                cps.append(cp_b)
            cum_pair = jnp.where(half, cums[0], cums[1])
            cp_pair = jnp.where(half, cps[0], cps[1])
            dx = jnp.where(half, locals_[0], locals_[1])
            x32 = x16.astype(jnp.float32)
            pick = (lane == GROUP * group + 2 * p + (row_ids(0, Q, Q) >= HEAD_DIM).astype(jnp.int32)).astype(jnp.bfloat16)
            in_dot = x32 * dx
            us = us + split_dot(d_ssm * y - in_dot, pick)
            vs = vs + split_dot(in_dot, pick)
            end = cum_pair[Q - 1 : Q, :]
            keep = jnp.where(through, jnp.exp(end), 0.0)
            if c < chunks - 1:
                later = dstate[:, cols]
                later16 = later.astype(jnp.bfloat16)
                weight = jnp.where(last, jnp.exp(end - cp_pair), 0.0)
                carried = weight * dot32(b16, later16)
                dx = dx + carried
                ws = ws + split_dot(xs * carried, pick)
                db = db + dot32((weight * xs).astype(jnp.bfloat16), later16, NT)
            if c > 0:
                ey16 = (jnp.where(carry, jnp.exp(cum_pair), 0.0) * d_ssm).astype(jnp.bfloat16)
                old16 = states_ref[c * NSTATE : (c + 1) * NSTATE, cols]
                dc = dc + dot32(ey16, old16, NT)
                fresh = dot32(c16t, ey16)
                if c < chunks - 1:
                    flow_ref[c : c + 1, cols] = keep * sum_rows(later * old16.astype(jnp.float32))
                    fresh = keep * later + fresh
                dstate[:, cols] = fresh
            d_mixed = (dx + skip * d_ssm) * (sx + xs * (1.0 - sx))
            dconv[rows, cols] = d_mixed
            grads_ref[4:5, cols] += sum_rows(d_mixed)
            for j in range(KW):
                grads_ref[KW - 1 - j : KW - j, cols] += sum_rows(d_mixed * moved[j])
            taps = [conv_ref[i : i + 1, cols] for i in range(KW)]
            d_ref[rows, cols] = conv_back(dconv, cols, c, first, Q, taps).astype(d_ref.dtype)
        for i, term in enumerate((dst, db, dc, us, vs, ws)):
            sums_ref[rows, i * Q : (i + 1) * Q] += term


def post_kernel(calls, first_ref, bcd_ref, conv_ref, head_ref, bc_ref, *refs):
    sums_refs, flow_refs, (d_ref, grads_ref, hgrads_ref, dconv) = refs[:calls], refs[calls:-4], refs[-4:]
    first = first_ref[0]
    rows_all = bcd_ref.shape[0]
    wide = 2 * NSTATE
    dconv[rows_all : rows_all + 8, :] = jnp.zeros((8, wide), jnp.float32)
    grads_ref[...] = jnp.zeros_like(grads_ref)
    hgrads_ref[...] = jnp.zeros_like(hgrads_ref)
    lane = lax.broadcasted_iota(jnp.int32, (Q, 128), 1)
    rate = -jnp.exp(head_ref[1:2, :])
    flow = jnp.zeros((8, 128), jnp.float32)
    start = 0
    for ref in flow_refs:
        width = ref.shape[1]
        spread = (row_ids(start, width, 128) // HEAD_DIM == lax.broadcasted_iota(jnp.int32, (width, 128), 1)).astype(jnp.float32)
        flow = flow + dot32(ref[...], spread, precision=lax.Precision.HIGHEST)
        start += width
    row, col = row_ids(0, Q, Q), lax.broadcasted_iota(jnp.int32, (Q, Q), 1)
    earlier_sum = (col < row).astype(jnp.float32)
    for c in range(rows_all // Q - 1, -1, -1):
        rows = slice(c * Q, c * Q + Q)
        moved = shifted_down(bcd_ref, slice(0, wide), c, first, wide)
        mixed = conv_ref[4:5, :] + conv_ref[3:4, :] * moved[0]
        for j in range(1, KW):
            mixed = mixed + conv_ref[KW - 1 - j : KW - j, :] * moved[j]
        sx = sigmoid(mixed)
        dst, db, dc, us, vs, carried = (functools.reduce(jnp.add, [ref[rows, i * Q : (i + 1) * Q] for ref in sums_refs]) for i in range(6))
        d_b = db + dot32(dst.astype(jnp.bfloat16), bc_ref[rows, NSTATE:])
        d_c = dc + dot32(dst.T.astype(jnp.bfloat16), bc_ref[rows, :NSTATE])
        d_mixed = jnp.concatenate([d_b, d_c], axis=1) * (sx + mixed * sx * (1.0 - sx))
        dconv[rows, :] = d_mixed
        grads_ref[4:5, :] += sum_rows(d_mixed)
        for j in range(KW):
            grads_ref[KW - 1 - j : KW - j, :] += sum_rows(d_mixed * moved[j])
        taps = [conv_ref[i : i + 1, :] for i in range(KW)]
        d_ref[rows, :wide] = conv_back(dconv, slice(0, wide), c, first, wide, taps).astype(d_ref.dtype)
        later_sum = ((col >= row) & ((row + c * Q >= first) == (col + c * Q >= first))).astype(jnp.float32)
        d_la = dot32(later_sum, us, precision=lax.Precision.HIGHEST)
        d_la = d_la + dot32(earlier_sum, carried, precision=lax.Precision.HIGHEST) + flow[c : c + 1, :]
        d_log = vs + carried
        raw = bcd_ref[rows, wide:] + head_ref[0:1, :]
        step = jax.nn.softplus(raw)
        sig = sigmoid(raw)
        ratio = jnp.where(raw < -17.0, 1.0, sig / jnp.maximum(step, 1e-37))
        d_raw = jnp.where(lane < HEADS, d_log * ratio + d_la * rate * sig, 0.0)
        d_ref[rows, wide:] = d_raw.astype(d_ref.dtype)
        hgrads_ref[0:1, :] += sum_rows(d_raw)
        hgrads_ref[1:2, :] += sum_rows(jnp.where(lane < HEADS, d_la * rate * step, 0.0))


def smem():
    return pl.BlockSpec(memory_space=pltpu.SMEM)


def whole(shape):
    return pl.BlockSpec(shape, lambda g: (0,) * len(shape))


def shaped(shape, kind):
    return jax.ShapeDtypeStruct(shape, kind)


def params(limit=VMEM):
    return pltpu.CompilerParams(vmem_limit_bytes=limit)


def cost(flops, size):
    return pl.CostEstimate(flops=flops // 3, bytes_accessed=size // 3, transcendentals=0)


def run_prep(first, bcd, conv, heads):
    rows = bcd.shape[0]
    f32, b16 = jnp.float32, jnp.bfloat16
    shapes = [((rows, 4 * Q), f32), ((256, rows), f32), ((rows, 2 * NSTATE), b16), ((2 * NSTATE, rows), b16)]
    return pl.pallas_call(
        prep_kernel,
        grid=(1,),
        in_specs=[smem(), whole((rows, BCD)), whole((8, 2 * NSTATE)), whole((8, 128))],
        out_specs=[whole(s) for s, _ in shapes],
        out_shape=[shaped(s, d) for s, d in shapes],
        compiler_params=params(),
        cost_estimate=cost(2000000000, 4000000),
    )(first, bcd, conv, heads)


def run_forward(first, x, conv, gains, prep):
    rows, width = x.shape
    chunks = rows // Q
    here = lambda g: (0, g)
    block, eight = pl.BlockSpec((rows, LANES), here), pl.BlockSpec((8, LANES), here)
    return pl.pallas_call(
        forward_kernel,
        grid=(width // LANES,),
        in_specs=[smem(), block, eight, eight] + [whole(v.shape) for v in prep],
        out_specs=[block, pl.BlockSpec((chunks * NSTATE, LANES), here)],
        out_shape=[shaped((rows, width), jnp.float32), shaped((chunks * NSTATE, width), jnp.bfloat16)],
        scratch_shapes=[pltpu.VMEM((NSTATE, LANES), jnp.float32)],
        compiler_params=params(),
        cost_estimate=cost(20000000000, 20000000),
    )(first, x, conv, gains, *prep)


def run_gated(z, ssm, gains):
    rows, width = z.shape
    block = pl.BlockSpec((Q, width), lambda g: (g, 0))
    thin = pl.BlockSpec((Q, Q), lambda g: (g, 0))
    return pl.pallas_call(
        gated_kernel,
        grid=(rows // Q,),
        in_specs=[block, block, whole(gains.shape)],
        out_specs=[block, thin],
        out_shape=[shaped((rows, width), jnp.bfloat16), shaped((rows, Q), jnp.float32)],
        compiler_params=params(),
        cost_estimate=cost(4000000000, 16000000),
    )(z, ssm, gains)


def run_gate(z, ssm, cot, weight, rk, gains):
    rows, width = cot.shape
    b16 = jnp.bfloat16
    here = lambda g: (0, g)
    block, eight = pl.BlockSpec((rows, LANES), here), pl.BlockSpec((8, LANES), here)
    return pl.pallas_call(
        gate_kernel,
        grid=(DI // LANES,),
        in_specs=[block, block, whole(cot.shape), pl.BlockSpec((LANES, width), lambda g: (g, 0)), whole(rk.shape), eight],
        out_specs=[block, block, eight],
        out_shape=[shaped((rows, DI), b16)] * 2 + [shaped((8, DI), jnp.float32)],
        compiler_params=params(),
        cost_estimate=cost(12000000000, 36000000),
    )(z, ssm, cot, weight, rk, gains)


def run_backward(base, count, first, x, ssm, ds, conv, gains, prep, states):
    rows = x.shape[0]
    f32, b16 = jnp.float32, jnp.bfloat16
    chunks = rows // Q
    at = lambda g: (0, g + base)
    here = lambda g: (0, g)
    block, eight = pl.BlockSpec((rows, LANES), at), pl.BlockSpec((8, LANES), at)
    own = pl.BlockSpec((8, LANES), here)
    return pl.pallas_call(
        functools.partial(backward_kernel, base),
        grid=(count,),
        in_specs=[smem(), block, block, block, eight, eight] + [whole(v.shape) for v in prep] + [pl.BlockSpec((chunks * NSTATE, LANES), at)],
        out_specs=[pl.BlockSpec((rows, LANES), here), own, whole((rows, 6 * Q)), own],
        out_shape=[shaped((rows, count * LANES), b16), shaped((8, count * LANES), f32), shaped((rows, 6 * Q), f32), shaped((8, count * LANES), f32)],
        scratch_shapes=[pltpu.VMEM((NSTATE, LANES), f32), pltpu.VMEM((rows + 8, LANES), f32)],
        compiler_params=params(),
        cost_estimate=cost(count * 7000000000, count * 8000000),
    )(first, x, ssm, ds, conv, gains, *prep, states)


def run_post(first, bcd, conv, heads, prep, backs):
    rows = bcd.shape[0]
    bc = prep[2]
    f32 = jnp.float32
    sums = [t for some in zip(*backs) for t in some]
    return pl.pallas_call(
        functools.partial(post_kernel, len(backs)),
        grid=(1,),
        in_specs=[smem(), whole((rows, BCD)), whole((8, 2 * NSTATE)), whole((8, 128)), whole(bc.shape)] + [whole(t.shape) for t in sums],
        out_specs=[whole((rows, BCD)), whole((8, 2 * NSTATE)), whole((8, 128))],
        out_shape=[shaped((rows, BCD), jnp.bfloat16), shaped((8, 2 * NSTATE), f32), shaped((8, 128), f32)],
        scratch_shapes=[pltpu.VMEM((rows + 8, 2 * NSTATE), f32)],
        compiler_params=params(),
        cost_estimate=cost(4000000000, 8000000),
    )(first, bcd, conv, heads, bc, *sums)


def contract_rows(left, right, kind=jnp.float32):
    return lax.dot_general(left, right, (((0,), (0,)), ((), ())), preferred_element_type=kind)


def pad_lanes(v, width):
    return jnp.pad(v, ((0, 0), (0, width - v.shape[1])))


ORDER = (7, 3, 5, 1, 6, 2, 4, 0)
WIDE = 512


def project_kernel(places, me_ref, left_ref, *refs):
    pieces, (out_ref, full_ref) = refs[:-2], refs[-2:]
    part = full_ref.shape[0] // 8
    for (j, skip, rows), ref in zip(places, pieces):
        full_ref[pl.ds(pl.multiple_of((me_ref[0] ^ j) * part + skip, 16), rows), :] = ref[:rows, :]
    out_ref[...] = dot32(left_ref[...], full_ref[...])


def run_project(me, left, pieces, skip, cols):
    rows, inner = left.shape
    step = min(WIDE, cols)
    here = lambda g: (0, g)
    places = tuple((j, start, min(v.shape[0], inner // 8 - start)) for v, j, start in pieces)
    return pl.pallas_call(
        functools.partial(project_kernel, places),
        grid=(cols // step,),
        in_specs=[smem(), whole(left.shape)] + [pl.BlockSpec((v.shape[0], step), lambda g: (0, g + skip // step)) for v, _, _ in pieces],
        out_specs=[pl.BlockSpec((rows, step), here), pl.BlockSpec((inner, step), here)],
        out_shape=[shaped((rows, cols), jnp.float32), shaped((inner, cols), left.dtype)],
        compiler_params=params(),
        cost_estimate=cost(2 * rows * inner * cols, 4 * inner * (rows + cols) + 4 * rows * cols),
    )(me, left, *[v for v, _, _ in pieces])


def unpack_kernel(places, widths, me_ref, *refs):
    pieces, (gain_ref, conv_ref, heads_ref, gains_ref, found) = refs[:-5], refs[-5:]
    span = found.shape[2]
    for j, ref in zip(places, pieces):
        found[me_ref[0] ^ j] = ref[:, :span].astype(jnp.float32)
    for ref in (gain_ref, conv_ref, heads_ref, gains_ref):
        ref[...] = jnp.zeros_like(ref)
    wide, taps, few, long = widths
    for i in range(8):
        gain_ref[:, i * wide : (i + 1) * wide] = found[i, 0:1, :wide]
        conv_ref[0:5, i * taps : (i + 1) * taps] = found[i, 1:6, :taps]
        heads_ref[0:3, i * few : (i + 1) * few] = found[i, 6:9, :few]
        gains_ref[1:2, i * long : (i + 1) * long] = found[i, 9:10, :long]
    spread = (row_ids(0, 128, DI) == lax.broadcasted_iota(jnp.int32, (128, DI), 1) // HEAD_DIM).astype(jnp.float32)
    gains_ref[0:1, :] = dot32(heads_ref[...], spread, precision=lax.Precision.HIGHEST)[2:3, :]


def run_unpack(me, pieces, rows, widths):
    f32 = jnp.float32
    wide, taps, few, long = widths
    shapes = [(1, 8 * wide), (8, 8 * taps), (8, 128), (8, 8 * long)]
    return pl.pallas_call(
        functools.partial(unpack_kernel, tuple(j for _, j, _ in pieces), widths),
        grid=(1,),
        in_specs=[smem()] + [pl.BlockSpec((SMALL, 512), lambda g, at=(rows - start) // SMALL: (at, 0)) for _, _, start in pieces],
        out_specs=[whole(s) for s in shapes],
        out_shape=[shaped(s, f32) for s in shapes],
        scratch_shapes=[pltpu.VMEM((8, SMALL, 512), f32)],
        compiler_params=params(),
        cost_estimate=cost(1000000, 1000000),
    )(me, *[v for v, _, _ in pieces])


def out_kernel(gated_ref, weight_ref, x_ref, cot_ref, r_ref, result_ref, rk_ref, acc):
    weight = weight_ref[...]
    branch = dot32(gated_ref[...], weight)
    result_ref[...] = (x_ref[...].astype(jnp.float32) + branch).astype(result_ref.dtype)
    product = cot_ref[...].astype(jnp.float32) * branch
    part = product[:, :Q]
    for p in range(1, product.shape[1] // Q):
        part = part + product[:, p * Q : (p + 1) * Q]

    @pl.when(pl.program_id(0) == 0)
    def _():
        acc[...] = part

    @pl.when(pl.program_id(0) > 0)
    def _():
        acc[...] += part

    @pl.when(pl.program_id(0) == pl.num_programs(0) - 1)
    def _():
        r = r_ref[...]
        pull = r * r * (jnp.sum(acc[...], axis=-1, keepdims=True) / DI)
        lane = lax.broadcasted_iota(jnp.int32, rk_ref.shape, 1)
        rk_ref[...] = jnp.where(lane == 0, r, jnp.where(lane == 1, pull, 0.0))


def run_out(gated, weight, x, cot, r):
    rows, inner = gated.shape
    width = x.shape[1]
    step = width // 3
    here = lambda g: (0, g)
    return pl.pallas_call(
        out_kernel,
        grid=(3,),
        in_specs=[whole(gated.shape)] + [pl.BlockSpec((v.shape[0], step), here) for v in (weight, x, cot)] + [whole(r.shape)],
        out_specs=[pl.BlockSpec((rows, step), here), whole((rows, 128))],
        out_shape=[shaped((rows, width), x.dtype), shaped((rows, 128), jnp.float32)],
        scratch_shapes=[pltpu.VMEM((rows, Q), jnp.float32)],
        compiler_params=params(),
        cost_estimate=cost(4 * rows * inner * width, 4 * inner * width + 8 * rows * width),
    )(gated, weight, x, cot, r)


def pack_kernel(calls, widths, *refs):
    x_refs, (b_ref, h_ref, g_ref, n_ref, out_ref, conv) = refs[:calls], refs[calls:]
    wide, taps, few, long = widths
    start = 0
    for ref in (*x_refs, b_ref):
        conv[:, start : start + ref.shape[1]] = ref[...]
        start += ref.shape[1]
    inner = 8 * long
    spread = (row_ids(0, inner, 128) // HEAD_DIM == lax.broadcasted_iota(jnp.int32, (inner, 128), 1)).astype(jnp.float32)
    skips = dot32(conv[:, :inner], spread, precision=lax.Precision.HIGHEST)
    out_ref[...] = jnp.zeros_like(out_ref)
    for i in range(8):
        fields = [n_ref[0:1, i * wide : (i + 1) * wide]]
        fields += [conv[k : k + 1, i * taps : (i + 1) * taps] for k in range(KW + 1)]
        fields += [h_ref[k : k + 1, i * few : (i + 1) * few] for k in range(2)] + [skips[5:6, i * few : (i + 1) * few]]
        fields += [g_ref[0:1, i * long : (i + 1) * long]]
        start = 0
        for field in fields:
            out_ref[i : i + 1, start : start + field.shape[1]] = field
            start += field.shape[1]


def run_pack(widths, x_grads, b_grads, h_grads, g_grads, n_grads):
    wide, taps, few, long = widths
    width = wide + (KW + 1) * taps + 3 * few + long
    width += -width % 128
    args = (*x_grads, b_grads, h_grads, g_grads, n_grads)
    return pl.pallas_call(
        functools.partial(pack_kernel, len(x_grads), widths),
        grid=(1,),
        in_specs=[whole(v.shape) for v in args],
        out_specs=whole((8, width)),
        out_shape=shaped((8, width), jnp.float32),
        scratch_shapes=[pltpu.VMEM((8, 8 * taps), jnp.float32)],
        compiler_params=params(),
        cost_estimate=cost(1000000, 1000000),
    )(*args)


def back_kernel(spans, based, *refs):
    out_ref = refs[-1]
    grid = pl.program_id(0)

    @pl.when(grid == 0)
    def _():
        out_ref[...] = refs[0][...] if based else jnp.zeros_like(out_ref)

    refs = refs[based:-1]
    for i, (start, stop) in enumerate(spans):

        @pl.when((grid >= start) & (grid < stop))
        def _():
            out_ref[...] += dot32(refs[2 * i][...], refs[2 * i + 1][...], NT)


def run_back(pairs, base=None):
    rows, inner = pairs[0][0].shape[0], pairs[0][2].shape[0]
    spans, specs, args, start = [], [], [], 0
    if base is not None:
        specs, args = [whole((rows, inner))], [base]
    for grad, left_skip, weight, right_skip, width in pairs:
        step = min(WIDE, width)
        steps = width // step
        spans.append((start, start + steps))

        def at(skip, g, start=start, steps=steps):
            return (0, jnp.clip(g - start, 0, steps - 1) + skip)

        specs += [pl.BlockSpec((rows, step), functools.partial(at, left_skip // step)), pl.BlockSpec((inner, step), functools.partial(at, right_skip // step))]
        args += [grad, weight]
        start += steps
    return pl.pallas_call(
        functools.partial(back_kernel, tuple(spans), int(base is not None)),
        grid=(start,),
        in_specs=specs,
        out_specs=whole((rows, inner)),
        out_shape=shaped((rows, inner), jnp.float32),
        input_output_aliases={0: 0} if base is not None else {},
        compiler_params=params(),
        cost_estimate=cost(3000, 3000),
    )(*args)


def norm_kernel(order, me_ref, x_ref, gain_ref, out_ref, sent_ref, turned):
    rows, width = x_ref.shape
    for c in range(rows // Q):
        place = slice(c * Q, c * Q + Q)
        v = x_ref[place, :].astype(jnp.float32)
        normed = v * lax.rsqrt(jnp.mean(v * v, axis=-1, keepdims=True) + epsilon) * gain_ref[...]
        out_ref[place, :] = normed.astype(out_ref.dtype)
        for p in range(width // Q):
            turned[p * Q : p * Q + Q, place] = normed[:, p * Q : p * Q + Q].T.astype(turned.dtype)
    part = width // len(order)
    for k, j in enumerate(order):
        sent_ref[k * part : (k + 1) * part, :] = turned[pl.ds(pl.multiple_of((me_ref[0] ^ j) * part, 16), part), :]


def run_norm(order, me, x, gain):
    rows, width = x.shape
    b16 = jnp.bfloat16
    return pl.pallas_call(
        functools.partial(norm_kernel, order),
        grid=(1,),
        in_specs=[smem(), whole(x.shape), whole((1, width))],
        out_specs=[whole(x.shape), whole((width, rows))],
        out_shape=[shaped(x.shape, b16), shaped((width, rows), b16)],
        scratch_shapes=[pltpu.VMEM((width, rows), b16)],
        compiler_params=params(),
        cost_estimate=cost(2000000000, 6 * rows * width),
    )(me, x, gain)


def norm_back_kernel(d_ref, x_ref, cot_ref, gain_ref, out_ref, grad_ref):
    @pl.when(pl.program_id(0) == 0)
    def _():
        grad_ref[...] = jnp.zeros_like(grad_ref)

    v = x_ref[...].astype(jnp.float32)
    rn = lax.rsqrt(jnp.mean(v * v, axis=-1, keepdims=True) + epsilon)
    d = d_ref[...]
    grad_ref[0:1, :] += sum_rows(d * v * rn)
    scaled = d * gain_ref[...]
    pull = rn * rn * rn * jnp.mean(v * scaled, axis=-1, keepdims=True)
    out_ref[...] = (cot_ref[...].astype(jnp.float32) + rn * scaled - v * pull).astype(out_ref.dtype)


def run_norm_back(d, x, cot, gain):
    rows, width = x.shape
    block = pl.BlockSpec((Q, width), lambda g: (g, 0))
    return pl.pallas_call(
        norm_back_kernel,
        grid=(rows // Q,),
        in_specs=[block, block, block, whole((1, width))],
        out_specs=[block, whole((8, width))],
        out_shape=[shaped(x.shape, x.dtype), shaped((8, width), jnp.float32)],
        compiler_params=params(),
        cost_estimate=cost(3000, 3000),
    )(d, x, cot, gain)


SMALL = 16
CALLS = ((0, 4), (4, 2))


def partners(bit):
    return [(i, i ^ bit) for i in range(8)]


def rotated(step):
    return [(i, (i + step) % 4) for i in range(4)]


def tie(*values):
    return lax.optimization_barrier(values)


def custom():
    return lax.axis_size("fsdp") == 8 and lax.axis_size("rep") == 4


def gathered_rows(w):
    half = w.shape[0] // 32 * 16
    two, four = yield [(w, "fsdp", partners(j)) for j in (2, 4)], 1
    top, bottom, one = yield [(two[:half], "fsdp", partners(4)), (four[half:], "fsdp", partners(2)), (w, "fsdp", partners(1))], 1
    three, five, other_top, other_bottom = yield [(v, "fsdp", partners(1)) for v in (two, four, top, bottom)], 1
    near = [(w, 0, 0), (one, 1, 0), (two, 2, 0), (three, 3, 0), (four, 4, 0), (five, 5, 0)]
    return near + [(top, 6, 0), (bottom, 6, half), (other_top, 7, 0), (other_bottom, 7, half)]


def dealt(v, turns):
    (got,) = yield [(v, "fsdp", None)], turns
    return got


def widen(v):
    return v.astype(jnp.float32)


def group_sum(product, rows):
    b16 = jnp.bfloat16
    (got,) = yield [(product(0, 4).astype(b16), "fsdp", partners(1))], 1
    terms = [product(4 + i, 5 + i) + widen(got[i * rows : (i + 1) * rows]) for i in range(4)]
    others = yield [(v.astype(b16), "fsdp", partners(j)) for v, j in zip(terms, ORDER[4:7])], 1
    return terms[3] + widen(others[0]) + widen(others[1]) + widen(others[2])


def left_rows(left, right):
    rows = left.shape[0] // 8
    return lambda i, j: jnp.dot(left[i * rows : j * rows], right, preferred_element_type=jnp.float32)


def half_sum(own):
    b16 = jnp.bfloat16
    place = lax.axis_index("rep")
    odd, late = place % 2 == 1, place >= 2
    across = [(0, 2), (1, 3), (2, 0), (3, 1)]
    beside = [(0, 1), (1, 0), (2, 3), (3, 2)]

    def halves(v, second):
        top, bottom = jnp.split(v, 2)
        return jnp.where(second, bottom, top), jnp.where(second, top, bottom)

    def joined(mine, other, second):
        return jnp.where(second, jnp.concatenate([other, mine]), jnp.concatenate([mine, other]))

    keep, send = halves(own, odd)
    (got,) = yield [(send.astype(b16), "rep", beside)], 1
    keep, send = halves(widen(keep) + widen(got), late)
    (got,) = yield [(send.astype(b16), "rep", across)], 1
    mine = (keep + widen(got)).astype(b16)
    (got,) = yield [(mine, "rep", across)], 1
    mine = joined(mine, got, late)
    (got,) = yield [(mine, "rep", beside)], 1
    return joined(mine, got, odd)


def small_sum(rows):
    place = lax.axis_index("rep")
    (got,) = yield [(rows, "fsdp", None)], 1
    row = jnp.sum(got, axis=0, keepdims=True)
    got = yield [(row, "rep", rotated(k)) for k in (1, 2, 3)], 1
    stack = jnp.concatenate([row, *got])
    return jnp.sum(stack[(place - jnp.arange(4)) % 4], axis=0)


def transfer(v, axis, pairs):
    if pairs is None:
        return lax.all_to_all(v, axis, split_axis=0, concat_axis=0, tiled=True)
    return lax.ppermute(v, axis, pairs)


def slice_sum(left, right):
    own = yield from group_sum(left_rows(left, right), left.shape[0] // 8)
    return (yield from half_sum(own))


class Moves:
    def __init__(self):
        self.active = []

    def add(self, generator):
        want, turns = next(generator)
        entry = {"gen": generator, "want": want, "turns": turns, "got": None, "value": None}
        self.active.append(entry)
        return entry

    def turn(self, work=None, *values):
        fresh = [e for e in self.active if e["got"] is None]
        arrays, values = tie([[item[0] for item in e["want"]] for e in fresh], values)
        for e, some in zip(fresh, arrays):
            e["got"] = [transfer(v, *item[1:]) for v, item in zip(some, e["want"])]
        results = work(*values) if work else ()
        for e in self.active:
            e["turns"] -= 1
        due = [e for e in self.active if e["turns"] == 0]
        arrived, results = tie([e["got"] for e in due], results)
        for e, got in zip(due, arrived):
            try:
                e["want"], e["turns"] = e["gen"].send(got)
                e["got"] = None
            except StopIteration as stop:
                e["value"] = stop.value
                self.active.remove(e)
        return results

    def after(self, value):
        want = self.active[0]["want"]
        array, *rest = want[-1]
        value, array = tie(value, array)
        want[-1] = (array, *rest)
        return value

    def finish(self):
        while self.active:
            self.turn()


def per_device(tokens, cotangent, lengths, dealing, norm_gain, in_weight, conv_weight, conv_bias, dt_bias, a_log, d_skip, gated_gain, out_weight):
    f32, b16 = jnp.float32, jnp.bfloat16
    groups = lax.axis_size("fsdp")
    tok_rows, width = tokens.shape
    block_rows = tok_rows // groups
    targets = dealing.reshape(groups)
    inverse = jnp.argsort(targets)
    first = lengths.reshape(-1)[:1]
    me = lax.axis_index("fsdp").reshape(1)
    moves = Moves()

    def blocks(values):
        return values.reshape(groups, block_rows, width)[inverse]

    def deal(values):
        return lax.all_to_all(blocks(values), "fsdp", split_axis=0, concat_axis=0, tiled=True).reshape(tok_rows, width)

    def undeal(values):
        blocks = lax.all_to_all(values.reshape(groups, block_rows, width), "fsdp", split_axis=0, concat_axis=0, tiled=True)
        return blocks[targets].reshape(tok_rows, width)

    own_small = [norm_gain[None], conv_weight, conv_bias[None], dt_bias[None], a_log[None], d_skip[None], gated_gain[None]]
    longest = max(v.shape[1] for v in own_small)
    small = jnp.concatenate([pad_lanes(v, longest) for v in own_small])
    small = jnp.pad(small, ((0, SMALL - small.shape[0]), (0, 0)))
    if custom():
        rows, span = in_weight.shape[0], DI + BCD
        w_xb = jnp.pad(in_weight[:, DI:], ((0, SMALL), (0, span + DI - in_weight.shape[1])))
        e_xb = moves.add(gathered_rows(w_xb + jnp.pad(small, ((rows, 0), (0, span - small.shape[1])))))
        moves.turn()
        e_x = moves.add(dealt(blocks(tokens), 1))
        moves.turn()
        out_weight = moves.after(out_weight)
        w_out = lax.all_gather(out_weight, "fsdp", axis=0, tiled=True)
        moves.turn()
        pieces = e_xb["value"]
        x = e_x["value"].reshape(tok_rows, width)
        behind = [[p for p in pieces if p[1] == j][-1] for j in range(8)]
        widths = (norm_gain.size, conv_bias.size, dt_bias.size, gated_gain.size)
        gain, conv, heads, gains = run_unpack(me, behind, rows, widths)
    else:
        x = deal(tokens)
        w_z = lax.all_gather(in_weight[:, :DI], "fsdp", axis=0, tiled=True)
        w_out = lax.all_gather(out_weight, "fsdp", axis=0, tiled=True)
        small_all = lax.all_gather(small, "fsdp", axis=0, tiled=False).astype(f32)
        w_xb = lax.all_gather(pad_lanes(in_weight[:, DI:], DI + BCD), "fsdp", axis=0, tiled=True)
        parts, row = [], 0
        for v in own_small:
            parts.append(small_all[:, row : row + v.shape[0], : v.shape[1]].transpose(1, 0, 2).reshape(v.shape[0], -1))
            row += v.shape[0]
        gain, taps, bias, step_bias, rate, skip, ggain = parts
        conv = jnp.concatenate([taps, bias, jnp.zeros((3, bias.shape[1]), f32)])
        heads = pad_lanes(jnp.concatenate([step_bias, rate, jnp.zeros((6, HEADS), f32)]), 128)
        gains = jnp.concatenate([jnp.repeat(skip, HEAD_DIM, axis=1), ggain, jnp.zeros((6, DI), f32)])
    conv_x, conv_bc = conv[:, :DI], conv[:, DI:]

    if custom():

        def open_up(x):
            normed, sent = run_norm(ORDER, me, x, gain)
            bcd, w_b = run_project(me, normed, pieces, DI, BCD)
            xr, w_x = run_project(me, normed, pieces, 0, DI)
            return normed, sent, bcd, w_b, xr, w_x, run_prep(first, bcd, conv_bc, heads)

        e_z = moves.add(gathered_rows(in_weight[:, :DI]))
        normed, sent, bcd, w_b, xr, w_x, prep = moves.turn(open_up, x)
        e_cot = moves.add(dealt(blocks(cotangent), 1))
        ssm, states = moves.turn(lambda v: run_forward(first, v, conv_x, gains, prep), xr)
        moves.turn()
        z, w_z = run_project(me, normed, e_z["value"], 0, DI)
        gated, r = run_gated(z, ssm, gains)
        cot = e_cot["value"].reshape(tok_rows, width)
        out_term, gated = tie(contract_rows(gated, cot, b16), gated)
        result, rk = run_out(gated, w_out, x, cot, r)
    else:
        normed, sent = run_norm((0,), me * 0, x, gain)
        w_x, w_b = w_xb[:, :DI], w_xb[:, DI:]
        bcd = jnp.dot(normed, w_b, preferred_element_type=f32)
        xr = jnp.dot(normed, w_x, preferred_element_type=f32)
        cot = deal(cotangent)
        prep = run_prep(first, bcd, conv_bc, heads)
        ssm, states = run_forward(first, xr, conv_x, gains, prep)
        z = jnp.dot(normed, w_z, preferred_element_type=f32)
        gated, r = run_gated(z, ssm, gains)
        result, rk = run_out(gated, w_out, x, cot, r)
        out_term = contract_rows(gated, cot, b16)
    s_out = lax.psum_scatter(out_term, "fsdp", scatter_dimension=0, tiled=True)
    dz, ds, ggrads = run_gate(z, ssm, cot, w_out, rk, gains)
    z_term, ds = tie(contract_rows(normed, dz, b16), ds)
    s_z = lax.psum_scatter(z_term, "fsdp", scatter_dimension=0, tiled=True)

    def backward(base, count, ds):
        return run_backward(base, count, first, xr, ssm, ds, conv_x, gains, prep, states)

    def close(backs):
        return run_post(first, bcd, conv_bc, heads, prep, [b[2:] for b in backs])

    def back(backs, d_b):
        pairs = [(dz, 0, w_z, 0, DI)] + [(b[0], 0, w_x, base * LANES, count * LANES) for b, (base, count) in zip(backs, CALLS)]
        return run_back(pairs + [(d_b, 0, w_b, 0, BCD)])

    if custom():
        backs = [backward(*CALLS[0], ds)]
        e_first = moves.add(slice_sum(sent, backs[0][0]))
        e_output = moves.add(dealt(result.reshape(groups, block_rows, width), 1))

        def middle(ds):
            both = backs + [backward(*CALLS[1], ds)]
            return both[1], *close(both)

        s_out, ds = tie(s_out, ds)
        e_rows = moves.add(half_sum(s_out))
        last, d_b, bgrads, hgrads = moves.turn(middle, ds)
        backs.append(last)
        e_last = moves.add(slice_sum(sent, jnp.concatenate([last[0], d_b], axis=1)))
        (d_normed,) = moves.turn(lambda d: (back(backs, d),), d_b)
        s_z, d_normed = tie(s_z, d_normed)
        e_z = moves.add(half_sum(s_z))

        def finish(d_normed):
            d_input, ngrads = run_norm_back(d_normed, x, cot, gain)
            return d_input, run_pack(widths, [b[1] for b in backs], bgrads, hgrads, ggrads, ngrads)

        d_input, packed = moves.turn(finish, d_normed)
    else:
        backs = [backward(*call, ds) for call in CALLS]
        d_b, bgrads, hgrads = close(backs)
        d_normed = back(backs, d_b)
        d_input, ngrads = run_norm_back(d_normed, x, cot, gain)
        s_in = [lax.psum_scatter(contract_rows(normed, d, b16), "fsdp", scatter_dimension=0, tiled=True) for d in [b[0] for b in backs] + [d_b]]
        output, input_grad = undeal(result), undeal(d_input)

    if not custom():
        xgrads = jnp.concatenate([b[1] for b in backs], axis=1)
        g_ggain = ggrads[0]
        g_conv = jnp.concatenate([xgrads[:KW], bgrads[:KW]], axis=1)
        g_cbias = jnp.concatenate([xgrads[KW], bgrads[KW]])
        g_dskip = jnp.sum(xgrads[5].reshape(HEADS, HEAD_DIM), axis=1)
        spread = [
            ngrads[0].reshape(groups, -1),
            g_conv.reshape(KW, groups, -1).transpose(1, 0, 2).reshape(groups, -1),
            g_cbias.reshape(groups, -1),
            hgrads[0, :HEADS].reshape(groups, -1),
            hgrads[1, :HEADS].reshape(groups, -1),
            g_dskip.reshape(groups, -1),
            g_ggain.reshape(groups, -1),
        ]
        packed = jnp.concatenate(spread, axis=1)
        packed = pad_lanes(packed, packed.shape[1] + -packed.shape[1] % 128)
    sizes = [v.size for v in own_small]
    tail = in_weight.shape[1] - 2 * DI
    if custom():
        e_small = moves.add(small_sum(packed))
        e_input = moves.add(dealt(d_input.reshape(groups, block_rows, width), 1))
        moves.finish()
        output, input_grad = (e["value"][targets].reshape(tok_rows, width) for e in (e_output, e_input))
        r_small, r_out = e_small["value"], e_rows["value"]
        r_in = jnp.concatenate([e_z["value"], e_first["value"], e_last["value"][:, : CALLS[-1][1] * LANES + tail]], axis=1)
    else:
        s_small = jnp.sum(lax.all_to_all(packed, "fsdp", split_axis=0, concat_axis=0, tiled=True), axis=0)
        r_small = jnp.sum(lax.all_gather(s_small, "rep", axis=0, tiled=False), axis=0)
        *r_in, r_out = lax.psum((s_z, *s_in, s_out), "rep")
        r_in = jnp.concatenate(r_in, axis=1)[:, : in_weight.shape[1]]
    ends, outs = 0, []
    for size in sizes:
        outs.append(r_small[ends : ends + size])
        ends += size
    return (output, input_grad, outs[0], r_in.astype(f32), outs[1].reshape(conv_weight.shape), outs[2], outs[3], outs[4], outs[5], outs[6], r_out.astype(f32))


def solution(mesh):
    placed = (
        P(("rep", "fsdp"), None),
        P(("rep", "fsdp"), None),
        P("rep", "fsdp", None),
        P("rep", "fsdp", None),
        P("fsdp"),
        P("fsdp", None),
        P(None, "fsdp"),
        P("fsdp"),
        P("fsdp"),
        P("fsdp"),
        P("fsdp"),
        P("fsdp"),
        P("fsdp", None),
    )
    return jax.shard_map(
        per_device,
        mesh=mesh,
        in_specs=placed,
        out_specs=(
            P(("rep", "fsdp"), None),
            P(("rep", "fsdp"), None),
            P("fsdp"),
            P("fsdp", None),
            P(None, "fsdp"),
            P("fsdp"),
            P("fsdp"),
            P("fsdp"),
            P("fsdp"),
            P("fsdp"),
            P("fsdp", None),
        ),
        check_vma=False,
    )
```

```python
import functools

import jax
import jax.numpy as jnp
from jax import lax
from jax.experimental import pallas as pl
from jax.experimental.pallas import tpu as pltpu
from jax.sharding import PartitionSpec as P

DI = 3072
HEAD_DIM = 64
NSTATE = 128
KW = 4
HEADS = 48
BCD = 384

epsilon = 1e-05


Q = 128
GROUP = 8
LANES = GROUP * HEAD_DIM
NEG = -1e30
VMEM = 56 * 1024 * 1024


def dot32(a, b, dims=(((1,), (0,)), ((), ())), precision=None):
    return lax.dot_general(a, b, dims, preferred_element_type=jnp.float32, precision=precision)


NT = (((1,), (1,)), ((), ()))


def row_ids(start, rows, cols):
    return lax.broadcasted_iota(jnp.int32, (rows, cols), 0) + start


def shifted_down(ref, cols, c, first, width):
    if c == 0:
        tall = jnp.concatenate([jnp.zeros((8, width), jnp.float32), ref[0:Q, cols]], axis=0)
    else:
        tall = ref[c * Q - 8 : c * Q + Q, cols]
    place = row_ids(c * Q, Q, width)
    outs = [tall[8:]]
    for j in range(1, KW):
        moved = pltpu.roll(tall, j, 0)[8:]
        keep = (place >= j) & ((place < first) | (place >= first + j))
        outs.append(jnp.where(keep, moved, 0.0))
    return outs


def conv_back(ref, cols, c, first, width, taps):
    tall = ref[c * Q : c * Q + Q + 8, cols]
    place = row_ids(c * Q, Q, width)
    total = taps[KW - 1] * tall[:Q]
    for j in range(1, KW):
        moved = pltpu.roll(tall, Q + 8 - j, 0)[:Q]
        keep = (place < first - j) | (place >= first)
        total = total + taps[KW - 1 - j] * jnp.where(keep, moved, 0.0)
    return total


def sigmoid(v):
    return 0.5 * jnp.tanh(0.5 * v) + 0.5


def sum_rows(v):
    return jnp.sum(v, axis=0, keepdims=True)


def prep_kernel(first_ref, bcd_ref, conv_ref, head_ref, wide_ref, tall_ref, bc_ref, bct_ref):
    first = first_ref[0]
    tri = (row_ids(0, Q, Q) >= lax.broadcasted_iota(jnp.int32, (Q, Q), 1)).astype(jnp.float32)
    rate = -jnp.exp(head_ref[1:2, :])
    lane = lax.broadcasted_iota(jnp.int32, (Q, 128), 1)
    for c in range(bcd_ref.shape[0] // Q):
        rows = slice(c * Q, c * Q + Q)
        moved = shifted_down(bcd_ref, slice(0, 2 * NSTATE), c, first, 2 * NSTATE)
        mixed = conv_ref[4:5, :] + conv_ref[3:4, :] * moved[0]
        for j in range(1, KW):
            mixed = mixed + conv_ref[KW - 1 - j : KW - j, :] * moved[j]
        act = mixed * sigmoid(mixed)
        b32, c32 = act[:, :NSTATE], act[:, NSTATE:]
        b16, c16 = b32.astype(jnp.bfloat16), c32.astype(jnp.bfloat16)
        bc_ref[rows, :] = act.astype(jnp.bfloat16)
        bct_ref[:NSTATE, rows] = b32.T.astype(jnp.bfloat16)
        bct_ref[NSTATE:, rows] = c32.T.astype(jnp.bfloat16)
        wide_ref[rows, :Q] = dot32(c16, b16, NT)
        wide_ref[rows, Q : 2 * Q] = dot32(b16, c16, NT)
        raw = jnp.where(lane < HEADS, bcd_ref[rows, 2 * NSTATE :] + head_ref[0:1, :], 0.0)
        step = jax.nn.softplus(raw)
        cum = dot32(tri, rate * step, precision=lax.Precision.HIGHEST)
        cp = cum - jnp.log(jnp.maximum(step, 1e-37))
        wide_ref[rows, 2 * Q : 3 * Q] = cum
        wide_ref[rows, 3 * Q :] = cp
        tall_ref[:128, rows] = cum.T
        tall_ref[128:, rows] = cp.T


def chunk_masks(first, c, transposed):
    base = c * Q
    row = row_ids(base, Q, Q)
    col = lax.broadcasted_iota(jnp.int32, (Q, Q), 1) + base
    ordered = (col >= row) if transposed else (row >= col)
    inside = ordered & ((row >= first) == (col >= first))
    carry = ((row >= first) == (base - 1 >= first)) & (base > 0)
    last = (row >= first) == (base + Q - 1 >= first)
    through = (base > 0) & ((base + Q - 1 >= first) == (base - 1 >= first))
    return inside, carry, last, through


def lane_column(values, k):
    return jnp.broadcast_to(values[:, k : k + 1], (Q, Q))


def conv_act(x_ref, conv_ref, cols, c, first):
    moved = shifted_down(x_ref, cols, c, first, Q)
    mixed = conv_ref[4:5, cols] + conv_ref[3:4, cols] * moved[0]
    for j in range(1, KW):
        mixed = mixed + conv_ref[KW - 1 - j : KW - j, cols] * moved[j]
    return moved, mixed


def both_heads(left, right, half):
    none = jnp.zeros_like(right)
    stacked = jnp.concatenate([jnp.where(half, right, none), jnp.where(half, none, right)], axis=0)
    return dot32(jnp.concatenate(left, axis=1), stacked)


def forward_kernel(first_ref, x_ref, conv_ref, gain_ref, wide_ref, tall_ref, bc_ref, bct_ref, ssm_ref, states_ref, state):
    first = first_ref[0]
    group = pl.program_id(0)
    half = lax.broadcasted_iota(jnp.int32, (Q, Q), 1) < HEAD_DIM
    state[...] = jnp.zeros_like(state)
    shift = (Q - GROUP * group) % Q
    pairs = range(GROUP // 2)
    for c in range(x_ref.shape[0] // Q):
        rows = slice(c * Q, c * Q + Q)
        inside, carry, last, through = chunk_masks(first, c, False)
        cum = pltpu.roll(wide_ref[rows, 2 * Q : 3 * Q], shift, 1)
        cp = pltpu.roll(wide_ref[rows, 3 * Q :], shift, 1)
        cpt = tall_ref[pl.ds(pl.multiple_of(128 + group * GROUP, GROUP), GROUP), rows]
        scores = wide_ref[rows, :Q]
        old16 = state[...].astype(jnp.bfloat16)
        states_ref[c * NSTATE : (c + 1) * NSTATE, :] = old16
        if c > 0:
            carried = dot32(bc_ref[rows, NSTATE:], old16)
        weighted, ends = [], []
        for p in pairs:
            cols = slice(p * Q, p * Q + Q)
            _, mixed = conv_act(x_ref, conv_ref, cols, c, first)
            xs = mixed * sigmoid(mixed)
            mixing, cums, cps = [], [], []
            for k in (2 * p, 2 * p + 1):
                cum_b = lane_column(cum, k)
                decay = jnp.exp(jnp.where(inside, cum_b - cpt[k : k + 1, :], NEG))
                mixing.append((scores * decay).astype(jnp.bfloat16))
                cums.append(cum_b)
                cps.append(lane_column(cp, k))
            cum_pair = jnp.where(half, cums[0], cums[1])
            cp_pair = jnp.where(half, cps[0], cps[1])
            y = both_heads(mixing, xs.astype(jnp.bfloat16), half)
            if c > 0:
                y = y + jnp.where(carry, jnp.exp(cum_pair), 0.0) * carried[:, cols]
            ssm_ref[rows, cols] = y + gain_ref[0:1, cols] * xs
            end = cum_pair[Q - 1 : Q, :]
            weighted.append((jnp.where(last, jnp.exp(end - cp_pair), 0.0) * xs).astype(jnp.bfloat16))
            ends.append(end)
        fresh = dot32(bct_ref[:NSTATE, rows], jnp.concatenate(weighted, axis=1))
        for p in pairs:
            cols = slice(p * Q, p * Q + Q)
            kept = 0.0 if c == 0 else jnp.where(through, jnp.exp(ends[p]), 0.0) * state[:, cols]
            state[:, cols] = kept + fresh[:, cols]


def gated_kernel(order, me_ref, z_ref, ssm_ref, gain_ref, gated_ref, sent_ref, r_ref):
    squares = jnp.zeros((Q, Q), jnp.float32)
    for p in range(z_ref.shape[1] // Q):
        cols = slice(p * Q, p * Q + Q)
        zv = z_ref[:, cols]
        g = ssm_ref[:, cols] * (zv * sigmoid(zv))
        squares = squares + g * g
    r = lax.rsqrt(jnp.sum(squares, axis=-1, keepdims=True) / DI + epsilon)
    wide = jnp.broadcast_to(r, (Q, Q))
    r_ref[...] = wide
    for p in range(z_ref.shape[1] // Q):
        cols = slice(p * Q, p * Q + Q)
        zv = z_ref[:, cols]
        g = ssm_ref[:, cols] * (zv * sigmoid(zv))
        gated_ref[:, cols] = (g * wide * gain_ref[1:2, cols]).astype(gated_ref.dtype)
    part = gated_ref.shape[1] // 8
    for i, j in enumerate(order):
        sent_ref[:, i * part : (i + 1) * part] = gated_ref[:, pl.ds(pl.multiple_of((me_ref[0] ^ j) * part, 128), part)]


def gate_kernel(z_ref, ssm_ref, cot_ref, weight_ref, rk_ref, gain_ref, dz_ref, ds_ref, grads_ref, d_gated):
    d_gated[...] = dot32(cot_ref[...], weight_ref[...], NT)
    grads_ref[...] = jnp.zeros_like(grads_ref)
    for c in range(z_ref.shape[0] // Q):
        rows = slice(c * Q, c * Q + Q)
        scale = lane_column(rk_ref[rows, :], 0)
        pull = lane_column(rk_ref[rows, :], 1)
        for p in range(z_ref.shape[1] // Q):
            cols = slice(p * Q, p * Q + Q)
            zv = z_ref[rows, cols]
            sz = sigmoid(zv)
            silu_z = zv * sz
            ssm = ssm_ref[rows, cols]
            g = ssm * silu_z
            gs = d_gated[rows, cols] * scale
            grads_ref[0:1, cols] += sum_rows(gs * g)
            d_g = gain_ref[1:2, cols] * gs - g * pull
            dz_ref[rows, cols] = (d_g * ssm * (sz + silu_z * (1.0 - sz))).astype(dz_ref.dtype)
            ds_ref[rows, cols] = (d_g * silu_z).astype(ds_ref.dtype)


def eight_rows(v):
    return functools.reduce(jnp.add, [v[i : i + 8, :] for i in range(0, v.shape[0], 8)])


def backward_kernel(base, first_ref, x_ref, ssm_ref, ds_ref, conv_ref, gain_ref, wide_ref, tall_ref, bc_ref, bct_ref, states_ref, d_ref, grads_ref, sums_ref, flow_ref, dstate, dconv, acc):
    first = first_ref[0]
    group = base + pl.program_id(0)
    half = lax.broadcasted_iota(jnp.int32, (Q, Q), 1) < HEAD_DIM
    dstate[...] = jnp.zeros_like(dstate)
    acc[...] = jnp.zeros_like(acc)
    rows_all = x_ref.shape[0]
    dconv[rows_all : rows_all + 8, :] = jnp.zeros((8, dconv.shape[1]), jnp.float32)
    flow_ref[...] = jnp.zeros_like(flow_ref)

    @pl.when(pl.program_id(0) == 0)
    def _():
        sums_ref[...] = jnp.zeros_like(sums_ref)

    shift = (Q - GROUP * group) % Q
    chunks = rows_all // Q
    pairs = range(GROUP // 2)
    pick = (lax.broadcasted_iota(jnp.int32, (LANES, Q), 1) == GROUP * group + row_ids(0, LANES, Q) // HEAD_DIM).astype(jnp.bfloat16)
    for c in range(chunks - 1, -1, -1):
        rows = slice(c * Q, c * Q + Q)
        inside, carry, last, through = chunk_masks(first, c, True)
        cum = pltpu.roll(wide_ref[rows, 2 * Q : 3 * Q], shift, 1)
        cp = pltpu.roll(wide_ref[rows, 3 * Q :], shift, 1)
        cumt = tall_ref[pl.ds(pl.multiple_of(group * GROUP, GROUP), GROUP), rows]
        scores_t = wide_ref[rows, Q : 2 * Q]
        b16, c16t = bc_ref[rows, :NSTATE], bct_ref[NSTATE:, rows]
        dst = jnp.zeros((Q, Q), jnp.float32)
        if c < chunks - 1:
            later16 = dstate[...].astype(jnp.bfloat16)
            carried = dot32(b16, later16)
        high, low, local, weighted, carries, eys, ends = ([] for _ in range(7))
        for p in pairs:
            cols = slice(p * Q, p * Q + Q)
            moved, mixed = conv_act(x_ref, conv_ref, cols, c, first)
            sx = sigmoid(mixed)
            xs = mixed * sx
            x16 = xs.astype(jnp.bfloat16)
            skip = gain_ref[0:1, cols]
            dy16 = ds_ref[rows, cols]
            d_ssm = dy16.astype(jnp.float32)
            acc[40:48, cols] += eight_rows(d_ssm * xs)
            mixing, cums, cps = [], [], []
            for k in (2 * p, 2 * p + 1):
                cp_b = lane_column(cp, k)
                decay = jnp.exp(jnp.where(inside, cumt[k : k + 1, :] - cp_b, NEG))
                mixing.append((scores_t * decay).astype(jnp.bfloat16))
                x_half = jnp.where(half == (k == 2 * p), x16, jnp.zeros_like(x16))
                dst = dst + decay * dot32(x_half, dy16, NT)
                cums.append(lane_column(cum, k))
                cps.append(cp_b)
            cum_pair = jnp.where(half, cums[0], cums[1])
            cp_pair = jnp.where(half, cps[0], cps[1])
            dx = both_heads(mixing, dy16, half)
            in_dot = x16.astype(jnp.float32) * dx
            u = d_ssm * (ssm_ref[rows, cols] - skip * xs) - in_dot
            high.append(u.astype(jnp.bfloat16))
            low.append((u - high[-1].astype(jnp.float32)).astype(jnp.bfloat16))
            local.append(in_dot.astype(jnp.bfloat16))
            end = cum_pair[Q - 1 : Q, :]
            ends.append(end)
            if c < chunks - 1:
                weight = jnp.where(last, jnp.exp(end - cp_pair), 0.0)
                moved_in = weight * carried[:, cols]
                dx = dx + moved_in
                carries.append((xs * moved_in).astype(jnp.bfloat16))
                weighted.append((weight * xs).astype(jnp.bfloat16))
            if c > 0:
                eys.append((jnp.where(carry, jnp.exp(cum_pair), 0.0) * d_ssm).astype(jnp.bfloat16))
            d_mixed = (dx + skip * d_ssm) * (sx + xs * (1.0 - sx))
            dconv[rows, cols] = d_mixed
            acc[32:40, cols] += eight_rows(d_mixed)
            for j in range(KW):
                acc[8 * (KW - 1 - j) : 8 * (KW - j), cols] += eight_rows(d_mixed * moved[j])
            taps = [conv_ref[i : i + 1, cols] for i in range(KW)]
            d_ref[rows, cols] = conv_back(dconv, cols, c, first, Q, taps).astype(d_ref.dtype)
        join = functools.partial(jnp.concatenate, axis=1)
        sums_ref[rows, :Q] += dst
        sums_ref[rows, 3 * Q : 4 * Q] += dot32(join(high), pick) + dot32(join(low), pick)
        sums_ref[rows, 4 * Q : 5 * Q] += dot32(join(local), pick)
        if c < chunks - 1:
            sums_ref[rows, Q : 2 * Q] += dot32(join(weighted), later16, NT)
            sums_ref[rows, 5 * Q :] += dot32(join(carries), pick)
        if c > 0:
            ey16 = join(eys)
            old16 = states_ref[c * NSTATE : (c + 1) * NSTATE, :]
            sums_ref[rows, 2 * Q : 3 * Q] += dot32(ey16, old16, NT)
            fresh = dot32(c16t, ey16)
            for p in pairs:
                cols = slice(p * Q, p * Q + Q)
                if c < chunks - 1:
                    kept = jnp.where(through, jnp.exp(ends[p]), 0.0) * dstate[:, cols]
                    flow_ref[c : c + 1, cols] = sum_rows(kept * old16[:, cols].astype(jnp.float32))
                    dstate[:, cols] = kept + fresh[:, cols]
                else:
                    dstate[:, cols] = fresh[:, cols]
    for i in range(8):
        grads_ref[i : i + 1, :] = sum_rows(acc[8 * i : 8 * i + 8, :]) if i < 6 else jnp.zeros((1, LANES), jnp.float32)


def post_kernel(calls, first_ref, bcd_ref, conv_ref, head_ref, bc_ref, *refs):
    sums_refs, flow_refs, (d_ref, grads_ref, hgrads_ref, dconv) = refs[:calls], refs[calls:-4], refs[-4:]
    first = first_ref[0]
    rows_all = bcd_ref.shape[0]
    wide = 2 * NSTATE
    dconv[rows_all : rows_all + 8, :] = jnp.zeros((8, wide), jnp.float32)
    grads_ref[...] = jnp.zeros_like(grads_ref)
    hgrads_ref[...] = jnp.zeros_like(hgrads_ref)
    lane = lax.broadcasted_iota(jnp.int32, (Q, 128), 1)
    rate = -jnp.exp(head_ref[1:2, :])
    flow = jnp.zeros((8, 128), jnp.float32)
    start = 0
    for ref in flow_refs:
        width = ref.shape[1]
        spread = (row_ids(start, width, 128) // HEAD_DIM == lax.broadcasted_iota(jnp.int32, (width, 128), 1)).astype(jnp.float32)
        flow = flow + dot32(ref[...], spread, precision=lax.Precision.HIGHEST)
        start += width
    row, col = row_ids(0, Q, Q), lax.broadcasted_iota(jnp.int32, (Q, Q), 1)
    earlier_sum = (col < row).astype(jnp.float32)
    for c in range(rows_all // Q - 1, -1, -1):
        rows = slice(c * Q, c * Q + Q)
        moved = shifted_down(bcd_ref, slice(0, wide), c, first, wide)
        mixed = conv_ref[4:5, :] + conv_ref[3:4, :] * moved[0]
        for j in range(1, KW):
            mixed = mixed + conv_ref[KW - 1 - j : KW - j, :] * moved[j]
        sx = sigmoid(mixed)
        dst, db, dc, us, vs, carried = (functools.reduce(jnp.add, [ref[rows, i * Q : (i + 1) * Q] for ref in sums_refs]) for i in range(6))
        d_b = db + dot32(dst.astype(jnp.bfloat16), bc_ref[rows, NSTATE:])
        d_c = dc + dot32(dst.T.astype(jnp.bfloat16), bc_ref[rows, :NSTATE])
        d_mixed = jnp.concatenate([d_b, d_c], axis=1) * (sx + mixed * sx * (1.0 - sx))
        dconv[rows, :] = d_mixed
        grads_ref[4:5, :] += sum_rows(d_mixed)
        for j in range(KW):
            grads_ref[KW - 1 - j : KW - j, :] += sum_rows(d_mixed * moved[j])
        taps = [conv_ref[i : i + 1, :] for i in range(KW)]
        d_ref[rows, :wide] = conv_back(dconv, slice(0, wide), c, first, wide, taps).astype(d_ref.dtype)
        later_sum = ((col >= row) & ((row + c * Q >= first) == (col + c * Q >= first))).astype(jnp.float32)
        d_la = dot32(later_sum, us, precision=lax.Precision.HIGHEST)
        d_la = d_la + dot32(earlier_sum, carried, precision=lax.Precision.HIGHEST) + flow[c : c + 1, :]
        d_log = vs + carried
        raw = bcd_ref[rows, wide:] + head_ref[0:1, :]
        step = jax.nn.softplus(raw)
        sig = sigmoid(raw)
        ratio = jnp.where(raw < -17.0, 1.0, sig / jnp.maximum(step, 1e-37))
        d_raw = jnp.where(lane < HEADS, d_log * ratio + d_la * rate * sig, 0.0)
        d_ref[rows, wide:] = d_raw.astype(d_ref.dtype)
        hgrads_ref[0:1, :] += sum_rows(d_raw)
        hgrads_ref[1:2, :] += sum_rows(jnp.where(lane < HEADS, d_la * rate * step, 0.0))


def smem():
    return pl.BlockSpec(memory_space=pltpu.SMEM)


def whole(shape):
    return pl.BlockSpec(shape, lambda g: (0,) * len(shape))


def shaped(shape, kind):
    return jax.ShapeDtypeStruct(shape, kind)


def params(limit=VMEM):
    return pltpu.CompilerParams(vmem_limit_bytes=limit)


def cost(flops, size):
    return pl.CostEstimate(flops=flops // 3, bytes_accessed=size // 3, transcendentals=0)


def run_prep(first, bcd, conv, heads):
    rows = bcd.shape[0]
    f32, b16 = jnp.float32, jnp.bfloat16
    shapes = [((rows, 4 * Q), f32), ((256, rows), f32), ((rows, 2 * NSTATE), b16), ((2 * NSTATE, rows), b16)]
    return pl.pallas_call(
        prep_kernel,
        grid=(1,),
        in_specs=[smem(), whole((rows, BCD)), whole((8, 2 * NSTATE)), whole((8, 128))],
        out_specs=[whole(s) for s, _ in shapes],
        out_shape=[shaped(s, d) for s, d in shapes],
        compiler_params=params(),
        cost_estimate=cost(2000000000, 4000000),
    )(first, bcd, conv, heads)


def run_forward(first, x, conv, gains, prep):
    rows, width = x.shape
    chunks = rows // Q
    here = lambda g: (0, g)
    block, eight = pl.BlockSpec((rows, LANES), here), pl.BlockSpec((8, LANES), here)
    return pl.pallas_call(
        forward_kernel,
        grid=(width // LANES,),
        in_specs=[smem(), block, eight, eight] + [whole(v.shape) for v in prep],
        out_specs=[block, pl.BlockSpec((chunks * NSTATE, LANES), here)],
        out_shape=[shaped((rows, width), jnp.float32), shaped((chunks * NSTATE, width), jnp.bfloat16)],
        scratch_shapes=[pltpu.VMEM((NSTATE, LANES), jnp.float32)],
        compiler_params=params(),
        cost_estimate=cost(20000000000, 20000000),
    )(first, x, conv, gains, *prep)


def run_gated(order, me, z, ssm, gains):
    rows, width = z.shape
    b16 = jnp.bfloat16
    block = pl.BlockSpec((Q, width), lambda g: (g, 0))
    thin = pl.BlockSpec((Q, Q), lambda g: (g, 0))
    return pl.pallas_call(
        functools.partial(gated_kernel, order),
        grid=(rows // Q,),
        in_specs=[smem(), block, block, whole(gains.shape)],
        out_specs=[block, block, thin],
        out_shape=[shaped((rows, width), b16), shaped((rows, width), b16), shaped((rows, Q), jnp.float32)],
        compiler_params=params(),
        cost_estimate=cost(4000000000, 16000000),
    )(me, z, ssm, gains)


def run_gate(z, ssm, cot, weight, rk, gains):
    rows, width = cot.shape
    b16 = jnp.bfloat16
    here = lambda g: (0, g)
    block, eight = pl.BlockSpec((rows, LANES), here), pl.BlockSpec((8, LANES), here)
    return pl.pallas_call(
        gate_kernel,
        grid=(DI // LANES,),
        in_specs=[block, block, whole(cot.shape), pl.BlockSpec((LANES, width), lambda g: (g, 0)), whole(rk.shape), eight],
        out_specs=[block, block, eight],
        out_shape=[shaped((rows, DI), b16)] * 2 + [shaped((8, DI), jnp.float32)],
        scratch_shapes=[pltpu.VMEM((rows, LANES), jnp.float32)],
        compiler_params=params(),
        cost_estimate=cost(12000000000, 36000000),
    )(z, ssm, cot, weight, rk, gains)


def run_backward(base, count, first, x, ssm, ds, conv, gains, prep, states):
    rows = x.shape[0]
    f32, b16 = jnp.float32, jnp.bfloat16
    chunks = rows // Q
    at = lambda g: (0, g + base)
    here = lambda g: (0, g)
    block, eight = pl.BlockSpec((rows, LANES), at), pl.BlockSpec((8, LANES), at)
    own = pl.BlockSpec((8, LANES), here)
    return pl.pallas_call(
        functools.partial(backward_kernel, base),
        grid=(count,),
        in_specs=[smem(), block, block, block, eight, eight] + [whole(v.shape) for v in prep] + [pl.BlockSpec((chunks * NSTATE, LANES), at)],
        out_specs=[pl.BlockSpec((rows, LANES), here), own, whole((rows, 6 * Q)), own],
        out_shape=[shaped((rows, count * LANES), b16), shaped((8, count * LANES), f32), shaped((rows, 6 * Q), f32), shaped((8, count * LANES), f32)],
        scratch_shapes=[pltpu.VMEM((NSTATE, LANES), f32), pltpu.VMEM((rows + 8, LANES), f32), pltpu.VMEM((48, LANES), f32)],
        compiler_params=params(),
        cost_estimate=cost(count * 7000000000, count * 8000000),
    )(first, x, ssm, ds, conv, gains, *prep, states)


def run_post(first, bcd, conv, heads, prep, backs):
    rows = bcd.shape[0]
    bc = prep[2]
    f32 = jnp.float32
    sums = [t for some in zip(*backs) for t in some]
    return pl.pallas_call(
        functools.partial(post_kernel, len(backs)),
        grid=(1,),
        in_specs=[smem(), whole((rows, BCD)), whole((8, 2 * NSTATE)), whole((8, 128)), whole(bc.shape)] + [whole(t.shape) for t in sums],
        out_specs=[whole((rows, BCD)), whole((8, 2 * NSTATE)), whole((8, 128))],
        out_shape=[shaped((rows, BCD), jnp.bfloat16), shaped((8, 2 * NSTATE), f32), shaped((8, 128), f32)],
        scratch_shapes=[pltpu.VMEM((rows + 8, 2 * NSTATE), f32)],
        compiler_params=params(),
        cost_estimate=cost(4000000000, 8000000),
    )(first, bcd, conv, heads, bc, *sums)


def contract_rows(left, right, kind=jnp.float32):
    return lax.dot_general(left, right, (((0,), (0,)), ((), ())), preferred_element_type=kind)


def pad_lanes(v, width):
    return jnp.pad(v, ((0, 0), (0, width - v.shape[1])))


ORDER = (7, 3, 5, 1, 6, 2, 4, 0)
WIDE = 512


def project_kernel(places, me_ref, left_ref, *refs):
    pieces, (out_ref, full_ref) = refs[:-2], refs[-2:]
    part = full_ref.shape[0] // 8
    for (j, skip, rows), ref in zip(places, pieces):
        full_ref[pl.ds(pl.multiple_of((me_ref[0] ^ j) * part + skip, 16), rows), :] = ref[:rows, :]
    out_ref[...] = dot32(left_ref[...], full_ref[...])


def run_project(me, left, pieces, skip, cols):
    rows, inner = left.shape
    step = min(WIDE, cols)
    here = lambda g: (0, g)
    places = tuple((j, start, min(v.shape[0], inner // 8 - start)) for v, j, start in pieces)
    return pl.pallas_call(
        functools.partial(project_kernel, places),
        grid=(cols // step,),
        in_specs=[smem(), whole(left.shape)] + [pl.BlockSpec((v.shape[0], step), lambda g: (0, g + skip // step)) for v, _, _ in pieces],
        out_specs=[pl.BlockSpec((rows, step), here), pl.BlockSpec((inner, step), here)],
        out_shape=[shaped((rows, cols), jnp.float32), shaped((inner, cols), left.dtype)],
        compiler_params=params(),
        cost_estimate=cost(2 * rows * inner * cols, 4 * inner * (rows + cols) + 4 * rows * cols),
    )(me, left, *[v for v, _, _ in pieces])


def unpack_kernel(places, widths, me_ref, *refs):
    pieces, (gain_ref, conv_ref, heads_ref, gains_ref, found) = refs[:-5], refs[-5:]
    span = found.shape[2]
    for j, ref in zip(places, pieces):
        found[me_ref[0] ^ j] = ref[:, :span].astype(jnp.float32)
    for ref in (gain_ref, conv_ref, heads_ref, gains_ref):
        ref[...] = jnp.zeros_like(ref)
    wide, taps, few, long = widths
    for i in range(8):
        gain_ref[:, i * wide : (i + 1) * wide] = found[i, 0:1, :wide]
        conv_ref[0:5, i * taps : (i + 1) * taps] = found[i, 1:6, :taps]
        heads_ref[0:3, i * few : (i + 1) * few] = found[i, 6:9, :few]
        gains_ref[1:2, i * long : (i + 1) * long] = found[i, 9:10, :long]
    spread = (row_ids(0, 128, DI) == lax.broadcasted_iota(jnp.int32, (128, DI), 1) // HEAD_DIM).astype(jnp.float32)
    gains_ref[0:1, :] = dot32(heads_ref[...], spread, precision=lax.Precision.HIGHEST)[2:3, :]


def run_unpack(me, pieces, rows, widths):
    f32 = jnp.float32
    wide, taps, few, long = widths
    shapes = [(1, 8 * wide), (8, 8 * taps), (8, 128), (8, 8 * long)]
    return pl.pallas_call(
        functools.partial(unpack_kernel, tuple(j for _, j, _ in pieces), widths),
        grid=(1,),
        in_specs=[smem()] + [pl.BlockSpec((SMALL, 512), lambda g, at=(rows - start) // SMALL: (at, 0)) for _, _, start in pieces],
        out_specs=[whole(s) for s in shapes],
        out_shape=[shaped(s, f32) for s in shapes],
        scratch_shapes=[pltpu.VMEM((8, SMALL, 512), f32)],
        compiler_params=params(),
        cost_estimate=cost(1000000, 1000000),
    )(me, *[v for v, _, _ in pieces])


def out_kernel(gated_ref, weight_ref, x_ref, cot_ref, r_ref, result_ref, rk_ref, acc):
    weight = weight_ref[...]
    branch = dot32(gated_ref[...], weight)
    result_ref[...] = (x_ref[...].astype(jnp.float32) + branch).astype(result_ref.dtype)
    product = cot_ref[...].astype(jnp.float32) * branch
    part = product[:, :Q]
    for p in range(1, product.shape[1] // Q):
        part = part + product[:, p * Q : (p + 1) * Q]

    @pl.when(pl.program_id(0) == 0)
    def _():
        acc[...] = part

    @pl.when(pl.program_id(0) > 0)
    def _():
        acc[...] += part

    @pl.when(pl.program_id(0) == pl.num_programs(0) - 1)
    def _():
        r = r_ref[...]
        pull = r * r * (jnp.sum(acc[...], axis=-1, keepdims=True) / DI)
        lane = lax.broadcasted_iota(jnp.int32, rk_ref.shape, 1)
        rk_ref[...] = jnp.where(lane == 0, r, jnp.where(lane == 1, pull, 0.0))


def run_out(gated, weight, x, cot, r):
    rows, inner = gated.shape
    width = x.shape[1]
    step = width // 3
    here = lambda g: (0, g)
    return pl.pallas_call(
        out_kernel,
        grid=(3,),
        in_specs=[whole(gated.shape)] + [pl.BlockSpec((v.shape[0], step), here) for v in (weight, x, cot)] + [whole(r.shape)],
        out_specs=[pl.BlockSpec((rows, step), here), whole((rows, 128))],
        out_shape=[shaped((rows, width), x.dtype), shaped((rows, 128), jnp.float32)],
        scratch_shapes=[pltpu.VMEM((rows, Q), jnp.float32)],
        compiler_params=params(),
        cost_estimate=cost(4 * rows * inner * width, 4 * inner * width + 8 * rows * width),
    )(gated, weight, x, cot, r)


def pack_kernel(calls, widths, *refs):
    x_refs, (b_ref, h_ref, g_ref, n_ref, out_ref, conv) = refs[:calls], refs[calls:]
    wide, taps, few, long = widths
    start = 0
    for ref in (*x_refs, b_ref):
        conv[:, start : start + ref.shape[1]] = ref[...]
        start += ref.shape[1]
    inner = 8 * long
    spread = (row_ids(0, inner, 128) // HEAD_DIM == lax.broadcasted_iota(jnp.int32, (inner, 128), 1)).astype(jnp.float32)
    skips = dot32(conv[:, :inner], spread, precision=lax.Precision.HIGHEST)
    out_ref[...] = jnp.zeros_like(out_ref)
    for i in range(8):
        fields = [n_ref[0:1, i * wide : (i + 1) * wide]]
        fields += [conv[k : k + 1, i * taps : (i + 1) * taps] for k in range(KW + 1)]
        fields += [h_ref[k : k + 1, i * few : (i + 1) * few] for k in range(2)] + [skips[5:6, i * few : (i + 1) * few]]
        fields += [g_ref[0:1, i * long : (i + 1) * long]]
        start = 0
        for field in fields:
            out_ref[i : i + 1, start : start + field.shape[1]] = field
            start += field.shape[1]


def run_pack(widths, x_grads, b_grads, h_grads, g_grads, n_grads):
    wide, taps, few, long = widths
    width = wide + (KW + 1) * taps + 3 * few + long
    width += -width % 128
    args = (*x_grads, b_grads, h_grads, g_grads, n_grads)
    return pl.pallas_call(
        functools.partial(pack_kernel, len(x_grads), widths),
        grid=(1,),
        in_specs=[whole(v.shape) for v in args],
        out_specs=whole((8, width)),
        out_shape=shaped((8, width), jnp.float32),
        scratch_shapes=[pltpu.VMEM((8, 8 * taps), jnp.float32)],
        compiler_params=params(),
        cost_estimate=cost(1000000, 1000000),
    )(*args)


def back_kernel(spans, based, *refs):
    out_ref = refs[-1]
    grid = pl.program_id(0)

    @pl.when(grid == 0)
    def _():
        out_ref[...] = refs[0][...] if based else jnp.zeros_like(out_ref)

    refs = refs[based:-1]
    for i, (start, stop) in enumerate(spans):

        @pl.when((grid >= start) & (grid < stop))
        def _():
            out_ref[...] += dot32(refs[2 * i][...], refs[2 * i + 1][...], NT)


def run_back(pairs, base=None):
    rows, inner = pairs[0][0].shape[0], pairs[0][2].shape[0]
    spans, specs, args, start = [], [], [], 0
    if base is not None:
        specs, args = [whole((rows, inner))], [base]
    for grad, left_skip, weight, right_skip, width in pairs:
        step = min(WIDE, width)
        steps = width // step
        spans.append((start, start + steps))

        def at(skip, g, start=start, steps=steps):
            return (0, jnp.clip(g - start, 0, steps - 1) + skip)

        specs += [pl.BlockSpec((rows, step), functools.partial(at, left_skip // step)), pl.BlockSpec((inner, step), functools.partial(at, right_skip // step))]
        args += [grad, weight]
        start += steps
    return pl.pallas_call(
        functools.partial(back_kernel, tuple(spans), int(base is not None)),
        grid=(start,),
        in_specs=specs,
        out_specs=whole((rows, inner)),
        out_shape=shaped((rows, inner), jnp.float32),
        input_output_aliases={0: 0} if base is not None else {},
        compiler_params=params(),
        cost_estimate=cost(3000, 3000),
    )(*args)


def terms_kernel(left_ref, right_ref, got_ref, *outs):
    rows = outs[0].shape[0]
    product = dot32(left_ref[...], right_ref[...]) + got_ref[...].astype(jnp.float32)
    for i, ref in enumerate(outs):
        ref[...] = product[i * rows : (i + 1) * rows, :].astype(ref.dtype)


def run_terms(left, right, got):
    rows, inner = left.shape
    cols = right.shape[1]
    step = 512 if cols % 512 == 0 else cols
    here = lambda g: (0, g)
    kinds = [jnp.bfloat16] * 3 + [jnp.float32]
    return pl.pallas_call(
        terms_kernel,
        grid=(cols // step,),
        in_specs=[whole(left.shape), pl.BlockSpec((inner, step), here), pl.BlockSpec((rows, step), here)],
        out_specs=[pl.BlockSpec((rows // 4, step), here)] * 4,
        out_shape=[shaped((rows // 4, cols), kind) for kind in kinds],
        compiler_params=params(),
        cost_estimate=cost(2 * rows * inner * cols, 6 * rows * cols),
    )(left, right, got)


def norm_kernel(order, me_ref, x_ref, gain_ref, out_ref, sent_ref, turned):
    rows, width = x_ref.shape
    for c in range(rows // Q):
        place = slice(c * Q, c * Q + Q)
        v = x_ref[place, :].astype(jnp.float32)
        normed = v * lax.rsqrt(jnp.mean(v * v, axis=-1, keepdims=True) + epsilon) * gain_ref[...]
        out_ref[place, :] = normed.astype(out_ref.dtype)
        for p in range(width // Q):
            turned[p * Q : p * Q + Q, place] = normed[:, p * Q : p * Q + Q].T.astype(turned.dtype)
    part = width // len(order)
    for k, j in enumerate(order):
        sent_ref[k * part : (k + 1) * part, :] = turned[pl.ds(pl.multiple_of((me_ref[0] ^ j) * part, 16), part), :]


def run_norm(order, me, x, gain):
    rows, width = x.shape
    b16 = jnp.bfloat16
    return pl.pallas_call(
        functools.partial(norm_kernel, order),
        grid=(1,),
        in_specs=[smem(), whole(x.shape), whole((1, width))],
        out_specs=[whole(x.shape), whole((width, rows))],
        out_shape=[shaped(x.shape, b16), shaped((width, rows), b16)],
        scratch_shapes=[pltpu.VMEM((width, rows), b16)],
        compiler_params=params(),
        cost_estimate=cost(2000000000, 6 * rows * width),
    )(me, x, gain)


def open_kernel(places, behind, widths, me_ref, first_ref, x_ref, *refs):
    count = len(places)
    tails, pieces, refs = refs[: len(behind)], refs[len(behind) : len(behind) + count], refs[len(behind) + count :]
    gain_ref, conv_ref, heads_ref, gains_ref, out_ref, sent_ref, bcd_ref, full_ref, *prep_refs, found, turned = refs
    unpack_kernel(behind, widths, me_ref, *tails, gain_ref, conv_ref, heads_ref, gains_ref, found)
    norm_kernel(ORDER, me_ref, x_ref, gain_ref, out_ref, sent_ref, turned)
    project_kernel(places, me_ref, out_ref, *pieces, bcd_ref, full_ref)
    prep_kernel(first_ref, bcd_ref, conv_ref.at[:, pl.ds(DI, 2 * NSTATE)], heads_ref, *prep_refs)


def run_open(me, first, x, pieces, rows, widths, skip):
    f32, b16 = jnp.float32, jnp.bfloat16
    toks, width = x.shape
    wide, taps, few, long = widths
    behind = [[p for p in pieces if p[1] == j][-1] for j in range(8)]
    places = tuple((j, start, min(v.shape[0], width // 8 - start)) for v, j, start in pieces)
    shapes = [((1, 8 * wide), f32), ((8, 8 * taps), f32), ((8, 128), f32), ((8, 8 * long), f32)]
    shapes += [((toks, width), b16), ((width, toks), b16), ((toks, BCD), f32), ((width, BCD), b16)]
    shapes += [((toks, 4 * Q), f32), ((256, toks), f32), ((toks, 2 * NSTATE), b16), ((2 * NSTATE, toks), b16)]
    return pl.pallas_call(
        functools.partial(open_kernel, places, tuple(j for _, j, _ in behind), widths),
        grid=(1,),
        in_specs=[smem(), smem(), whole(x.shape)]
        + [pl.BlockSpec((SMALL, 512), lambda g, at=(rows - start) // SMALL: (at, 0)) for _, _, start in behind]
        + [pl.BlockSpec((v.shape[0], BCD), lambda g: (0, skip // BCD)) for v, _, _ in pieces],
        out_specs=[whole(s) for s, _ in shapes],
        out_shape=[shaped(s, d) for s, d in shapes],
        scratch_shapes=[pltpu.VMEM((8, SMALL, 512), f32), pltpu.VMEM((width, toks), b16)],
        compiler_params=params(),
        cost_estimate=cost(6000000000, 10000000),
    )(me, first, x, *[v for v, _, _ in behind], *[v for v, _, _ in pieces])


def norm_back_kernel(d_ref, x_ref, cot_ref, gain_ref, out_ref, grad_ref):
    @pl.when(pl.program_id(0) == 0)
    def _():
        grad_ref[...] = jnp.zeros_like(grad_ref)

    v = x_ref[...].astype(jnp.float32)
    rn = lax.rsqrt(jnp.mean(v * v, axis=-1, keepdims=True) + epsilon)
    d = d_ref[...]
    grad_ref[0:1, :] += sum_rows(d * v * rn)
    scaled = d * gain_ref[...]
    pull = rn * rn * rn * jnp.mean(v * scaled, axis=-1, keepdims=True)
    out_ref[...] = (cot_ref[...].astype(jnp.float32) + rn * scaled - v * pull).astype(out_ref.dtype)


def run_norm_back(d, x, cot, gain):
    rows, width = x.shape
    block = pl.BlockSpec((Q, width), lambda g: (g, 0))
    return pl.pallas_call(
        norm_back_kernel,
        grid=(rows // Q,),
        in_specs=[block, block, block, whole((1, width))],
        out_specs=[block, whole((8, width))],
        out_shape=[shaped(x.shape, x.dtype), shaped((8, width), jnp.float32)],
        compiler_params=params(),
        cost_estimate=cost(3000, 3000),
    )(d, x, cot, gain)


SMALL = 16
CALLS = ((0, 4), (4, 2))


def partners(bit):
    return [(i, i ^ bit) for i in range(8)]


def rotated(step):
    return [(i, (i + step) % 4) for i in range(4)]


def tie(*values):
    return lax.optimization_barrier(values)


def custom():
    return lax.axis_size("fsdp") == 8 and lax.axis_size("rep") == 4


def gathered_rows(w):
    half = w.shape[0] // 32 * 16
    two, four = yield [(w, "fsdp", partners(j)) for j in (2, 4)], 1
    top, bottom, one = yield [(two[:half], "fsdp", partners(4)), (four[half:], "fsdp", partners(2)), (w, "fsdp", partners(1))], 1
    three, five, other_top, other_bottom = yield [(v, "fsdp", partners(1)) for v in (two, four, top, bottom)], 1
    near = [(w, 0, 0), (one, 1, 0), (two, 2, 0), (three, 3, 0), (four, 4, 0), (five, 5, 0)]
    return near + [(top, 6, 0), (bottom, 6, half), (other_top, 7, 0), (other_bottom, 7, half)]


def dealt(v, turns):
    (got,) = yield [(v, "fsdp", None)], turns
    return got


def widen(v):
    return v.astype(jnp.float32)


def group_sum(left, right):
    half = left.shape[0] // 2
    odd = jnp.dot(left[:half], right, preferred_element_type=jnp.float32).astype(jnp.bfloat16)
    (got,) = yield [(odd, "fsdp", partners(1))], 1
    *terms, own = run_terms(left[half:], right, got)
    others = yield [(v, "fsdp", partners(j)) for v, j in zip(terms, ORDER[4:7])], 1
    return own + widen(others[0]) + widen(others[1]) + widen(others[2])


def relayed_sum(left, right):
    b16 = jnp.bfloat16
    rows = left.shape[1] // 8
    half = rows // 2

    def product(start, stop):
        return contract_rows(left[:, start * rows : stop * rows], right)

    (got,) = yield [(product(0, 4).astype(b16), "fsdp", partners(1))], 1
    far = (product(4, 5) + widen(got[:rows])).astype(b16)
    from_x, from_y = yield [(far[:half], "fsdp", partners(2)), (far[half:], "fsdp", partners(4))], 1
    low = jnp.pad(widen(from_y), ((half, 0), (0, 0)))
    high = jnp.pad(widen(from_x), ((0, half), (0, 0)))
    to_x = (product(5, 6) + widen(got[rows : 2 * rows]) + low).astype(b16)
    to_y = (product(6, 7) + widen(got[2 * rows : 3 * rows]) + high).astype(b16)
    got_x, got_y = yield [(to_x, "fsdp", partners(2)), (to_y, "fsdp", partners(4))], 1
    return product(7, 8) + widen(got[3 * rows :]) + widen(got_x) + widen(got_y)


def out_sum(left, right):
    own = yield from relayed_sum(left, right)
    return (yield from half_sum(own))


def half_sum(own):
    b16 = jnp.bfloat16
    place = lax.axis_index("rep")
    odd, late = place % 2 == 1, place >= 2
    across = [(0, 2), (1, 3), (2, 0), (3, 1)]
    beside = [(0, 1), (1, 0), (2, 3), (3, 2)]

    def halves(v, second):
        top, bottom = jnp.split(v, 2)
        return jnp.where(second, bottom, top), jnp.where(second, top, bottom)

    def joined(mine, other, second):
        return jnp.where(second, jnp.concatenate([other, mine]), jnp.concatenate([mine, other]))

    keep, send = halves(own, odd)
    (got,) = yield [(send.astype(b16), "rep", beside)], 1
    keep, send = halves(widen(keep) + widen(got), late)
    (got,) = yield [(send.astype(b16), "rep", across)], 1
    mine = (keep + widen(got)).astype(b16)
    (got,) = yield [(mine, "rep", across)], 1
    mine = joined(mine, got, late)
    (got,) = yield [(mine, "rep", beside)], 1
    return joined(mine, got, odd)


def small_sum(rows):
    me, place = lax.axis_index("fsdp"), lax.axis_index("rep")
    rows = rows[me ^ jnp.array(ORDER, jnp.int32)]
    (got,) = yield [(rows[:4], "fsdp", partners(1))], 1
    rows = rows[4:] + got
    others = yield [(rows[i : i + 1], "fsdp", partners(j)) for i, j in enumerate(ORDER[4:7])], 1
    row = rows[3:] + others[0] + others[1] + others[2]
    got = yield [(row, "rep", rotated(k)) for k in (1, 2, 3)], 1
    stack = jnp.concatenate([row, *got])
    return jnp.sum(stack[(place - jnp.arange(4)) % 4], axis=0)


def transfer(v, axis, pairs):
    if pairs is None:
        return lax.all_to_all(v, axis, split_axis=0, concat_axis=0, tiled=True)
    return lax.ppermute(v, axis, pairs)


def slice_sum(left, right):
    own = yield from group_sum(left, right)
    return (yield from half_sum(own))


class Moves:
    def __init__(self):
        self.active = []

    def add(self, generator):
        want, turns = next(generator)
        entry = {"gen": generator, "want": want, "turns": turns, "got": None, "value": None}
        self.active.append(entry)
        return entry

    def turn(self, work=None, *values):
        fresh = [e for e in self.active if e["got"] is None]
        arrays, values = tie([[item[0] for item in e["want"]] for e in fresh], values)
        for e, some in zip(fresh, arrays):
            e["got"] = [transfer(v, *item[1:]) for v, item in zip(some, e["want"])]
        results = work(*values) if work else ()
        for e in self.active:
            e["turns"] -= 1
        due = [e for e in self.active if e["turns"] == 0]
        arrived, results = tie([e["got"] for e in due], results)
        for e, got in zip(due, arrived):
            try:
                e["want"], e["turns"] = e["gen"].send(got)
                e["got"] = None
            except StopIteration as stop:
                e["value"] = stop.value
                self.active.remove(e)
        return results

    def after(self, value):
        want = self.active[0]["want"]
        array, *rest = want[-1]
        value, array = tie(value, array)
        want[-1] = (array, *rest)
        return value

    def finish(self):
        while self.active:
            self.turn()


def per_device(tokens, cotangent, lengths, dealing, norm_gain, in_weight, conv_weight, conv_bias, dt_bias, a_log, d_skip, gated_gain, out_weight):
    f32, b16 = jnp.float32, jnp.bfloat16
    groups = lax.axis_size("fsdp")
    tok_rows, width = tokens.shape
    block_rows = tok_rows // groups
    targets = dealing.reshape(groups)
    inverse = jnp.argsort(targets)
    first = lengths.reshape(-1)[:1]
    me = lax.axis_index("fsdp").reshape(1)
    moves = Moves()

    def blocks(values):
        return values.reshape(groups, block_rows, width)[inverse]

    def deal(values):
        return lax.all_to_all(blocks(values), "fsdp", split_axis=0, concat_axis=0, tiled=True).reshape(tok_rows, width)

    def undeal(values):
        blocks = lax.all_to_all(values.reshape(groups, block_rows, width), "fsdp", split_axis=0, concat_axis=0, tiled=True)
        return blocks[targets].reshape(tok_rows, width)

    own_small = [norm_gain[None], conv_weight, conv_bias[None], dt_bias[None], a_log[None], d_skip[None], gated_gain[None]]
    longest = max(v.shape[1] for v in own_small)
    small = jnp.concatenate([pad_lanes(v, longest) for v in own_small])
    small = jnp.pad(small, ((0, SMALL - small.shape[0]), (0, 0)))
    if custom():
        rows, span = in_weight.shape[0], DI + BCD
        w_xb = lax.pad(in_weight, jnp.zeros((), b16), ((0, SMALL, 0), (-DI, span + DI - in_weight.shape[1], 0)))
        e_xb = moves.add(gathered_rows(w_xb + jnp.pad(small, ((rows, 0), (0, span - small.shape[1])))))
        moves.turn()
        e_x = moves.add(dealt(blocks(tokens), 1))
        (cot_blocks,) = moves.turn(lambda v: (blocks(v),), cotangent)
        out_weight = moves.after(out_weight)
        w_out = lax.all_gather(out_weight, "fsdp", axis=0, tiled=True)
        moves.turn()
        pieces = e_xb["value"]
        x = e_x["value"].reshape(tok_rows, width)
        widths = (norm_gain.size, conv_bias.size, dt_bias.size, gated_gain.size)
    else:
        x = deal(tokens)
        w_z = lax.all_gather(in_weight[:, :DI], "fsdp", axis=0, tiled=True)
        w_out = lax.all_gather(out_weight, "fsdp", axis=0, tiled=True)
        small_all = lax.all_gather(small, "fsdp", axis=0, tiled=False).astype(f32)
        w_xb = lax.all_gather(pad_lanes(in_weight[:, DI:], DI + BCD), "fsdp", axis=0, tiled=True)
        parts, row = [], 0
        for v in own_small:
            parts.append(small_all[:, row : row + v.shape[0], : v.shape[1]].transpose(1, 0, 2).reshape(v.shape[0], -1))
            row += v.shape[0]
        gain, taps, bias, step_bias, rate, skip, ggain = parts
        conv = jnp.concatenate([taps, bias, jnp.zeros((3, bias.shape[1]), f32)])
        heads = pad_lanes(jnp.concatenate([step_bias, rate, jnp.zeros((6, HEADS), f32)]), 128)
        gains = jnp.concatenate([jnp.repeat(skip, HEAD_DIM, axis=1), ggain, jnp.zeros((6, DI), f32)])
    if custom():

        def open_up(x):
            gain, conv, heads, gains, normed, sent, bcd, w_b, *prep = run_open(me, first, x, pieces, rows, widths, DI)
            return gain, conv, heads, gains, normed, sent, bcd, w_b, prep, *run_project(me, normed, pieces, 0, DI)

        e_z = moves.add(gathered_rows(in_weight[:, :DI]))
        gain, conv, heads, gains, normed, sent, bcd, w_b, prep, xr, w_x = moves.turn(open_up, x)
        conv_x, conv_bc = conv[:, :DI], conv[:, DI:]
        ssm, states = moves.turn(lambda v: run_forward(first, v, conv_x, gains, prep), xr)
        moves.turn()
        e_cot = moves.add(dealt(cot_blocks, 1))

        def close_up(ssm):
            z, full = run_project(me, normed, e_z["value"], 0, DI)
            return z, full, *run_gated(ORDER, me, z, ssm, gains)

        z, w_z, gated, gated_sent, r = moves.turn(close_up, ssm)
        cot = e_cot["value"].reshape(tok_rows, width)
        e_rows = moves.add(out_sum(gated_sent, cot))
        result, rk = moves.turn(lambda v: run_out(v, w_out, x, cot, r), gated)
    else:
        conv_x, conv_bc = conv[:, :DI], conv[:, DI:]
        normed, sent = run_norm((0,), me * 0, x, gain)
        w_x, w_b = w_xb[:, :DI], w_xb[:, DI:]
        bcd = jnp.dot(normed, w_b, preferred_element_type=f32)
        xr = jnp.dot(normed, w_x, preferred_element_type=f32)
        cot = deal(cotangent)
        prep = run_prep(first, bcd, conv_bc, heads)
        ssm, states = run_forward(first, xr, conv_x, gains, prep)
        z = jnp.dot(normed, w_z, preferred_element_type=f32)
        gated, _, r = run_gated(tuple(range(8)), me * 0, z, ssm, gains)
        result, rk = run_out(gated, w_out, x, cot, r)
        s_out = lax.psum_scatter(contract_rows(gated, cot, b16), "fsdp", scatter_dimension=0, tiled=True)

    def gate(rk):
        return run_gate(z, ssm, cot, w_out, rk, gains)

    def backward(base, count, ds):
        return run_backward(base, count, first, xr, ssm, ds, conv_x, gains, prep, states)

    def close(backs):
        return run_post(first, bcd, conv_bc, heads, prep, [b[2:] for b in backs])

    def back(backs, d_b):
        pairs = [(dz, 0, w_z, 0, DI)] + [(b[0], 0, w_x, base * LANES, count * LANES) for b, (base, count) in zip(backs, CALLS)]
        return run_back(pairs + [(d_b, 0, w_b, 0, BCD)])

    if custom():
        dz, ds, ggrads = moves.turn(gate, rk)

        def first_back(dz, ds):
            z_term, ds = tie(contract_rows(normed, dz, b16), ds)
            held.append(lax.psum_scatter(z_term, "fsdp", scatter_dimension=0, tiled=True))
            return backward(*CALLS[0], ds)

        held = []
        backs = [moves.turn(first_back, dz, ds)]
        (s_z,) = held
        e_first = moves.add(slice_sum(sent, backs[0][0]))

        def middle(ds):
            both = backs + [backward(*CALLS[1], ds)]
            return both[1], *close(both)

        last, d_b, bgrads, hgrads = moves.turn(middle, ds)
        backs.append(last)
        s_z, d_b = tie(s_z, d_b)
        e_last = moves.add(slice_sum(sent, jnp.concatenate([last[0], d_b], axis=1)))
        e_z = moves.add(half_sum(s_z))
        (d_normed,) = moves.turn(lambda d: (back(backs, d),), d_b)

        def finish(d_normed):
            d_input, ngrads = run_norm_back(d_normed, x, cot, gain)
            return d_input, run_pack(widths, [b[1] for b in backs], bgrads, hgrads, ggrads, ngrads)

        d_input, packed = moves.turn(finish, d_normed)
    else:
        dz, ds, ggrads = gate(rk)
        s_z = lax.psum_scatter(contract_rows(normed, dz, b16), "fsdp", scatter_dimension=0, tiled=True)
        backs = [backward(*call, ds) for call in CALLS]
        d_b, bgrads, hgrads = close(backs)
        d_normed = back(backs, d_b)
        d_input, ngrads = run_norm_back(d_normed, x, cot, gain)
        s_in = [lax.psum_scatter(contract_rows(normed, d, b16), "fsdp", scatter_dimension=0, tiled=True) for d in [b[0] for b in backs] + [d_b]]
        output, input_grad = undeal(result), undeal(d_input)

    if not custom():
        xgrads = jnp.concatenate([b[1] for b in backs], axis=1)
        g_ggain = ggrads[0]
        g_conv = jnp.concatenate([xgrads[:KW], bgrads[:KW]], axis=1)
        g_cbias = jnp.concatenate([xgrads[KW], bgrads[KW]])
        g_dskip = jnp.sum(xgrads[5].reshape(HEADS, HEAD_DIM), axis=1)
        spread = [
            ngrads[0].reshape(groups, -1),
            g_conv.reshape(KW, groups, -1).transpose(1, 0, 2).reshape(groups, -1),
            g_cbias.reshape(groups, -1),
            hgrads[0, :HEADS].reshape(groups, -1),
            hgrads[1, :HEADS].reshape(groups, -1),
            g_dskip.reshape(groups, -1),
            g_ggain.reshape(groups, -1),
        ]
        packed = jnp.concatenate(spread, axis=1)
        packed = pad_lanes(packed, packed.shape[1] + -packed.shape[1] % 128)
    sizes = [v.size for v in own_small]
    tail = in_weight.shape[1] - 2 * DI

    def cut(row):
        ends, outs = 0, []
        for size in sizes:
            outs.append(row[ends : ends + size])
            ends += size
        return outs

    if custom():
        e_small = moves.add(small_sum(packed))
        e_input = moves.add(dealt(d_input.reshape(groups, block_rows, width), 1))
        moves.turn()
        e_output = moves.add(dealt(result.reshape(groups, block_rows, width), 1))
        moves.turn()

        def restored(entry):
            return entry["value"][targets].reshape(tok_rows, width)

        input_grad, r_out = moves.turn(lambda: (restored(e_input), widen(e_rows["value"])))
        (output,) = moves.turn(lambda: (restored(e_output),))
        last = CALLS[-1][1] * LANES + tail

        def gather_up():
            known = jnp.concatenate([e_z["value"], e_first["value"], jnp.zeros((rows, last), b16)], axis=1)
            return widen(known), *cut(e_small["value"])

        r_in, *outs = moves.turn(gather_up)
        moves.finish()
        r_in = lax.dynamic_update_slice(r_in, widen(e_last["value"][:, :last]), (0, r_in.shape[1] - last))
    else:
        s_small = jnp.sum(lax.all_to_all(packed, "fsdp", split_axis=0, concat_axis=0, tiled=True), axis=0)
        r_small = jnp.sum(lax.all_gather(s_small, "rep", axis=0, tiled=False), axis=0)
        *r_in, r_out = lax.psum((s_z, *s_in, s_out), "rep")
        r_in = jnp.concatenate(r_in, axis=1)[:, : in_weight.shape[1]]
        outs = cut(r_small)
    return (output, input_grad, outs[0], r_in.astype(f32), outs[1].reshape(conv_weight.shape), outs[2], outs[3], outs[4], outs[5], outs[6], r_out.astype(f32))


def solution(mesh):
    placed = (
        P(("rep", "fsdp"), None),
        P(("rep", "fsdp"), None),
        P("rep", "fsdp", None),
        P("rep", "fsdp", None),
        P("fsdp"),
        P("fsdp", None),
        P(None, "fsdp"),
        P("fsdp"),
        P("fsdp"),
        P("fsdp"),
        P("fsdp"),
        P("fsdp"),
        P("fsdp", None),
    )
    return jax.shard_map(
        per_device,
        mesh=mesh,
        in_specs=placed,
        out_specs=(
            P(("rep", "fsdp"), None),
            P(("rep", "fsdp"), None),
            P("fsdp"),
            P("fsdp", None),
            P(None, "fsdp"),
            P("fsdp"),
            P("fsdp"),
            P("fsdp"),
            P("fsdp"),
            P("fsdp"),
            P("fsdp", None),
        ),
        check_vma=False,
    )
```

```python
import functools

import jax
import jax.numpy as jnp
from jax import lax
from jax.experimental import pallas as pl
from jax.experimental.pallas import tpu as pltpu
from jax.sharding import PartitionSpec as P

DI = 3072
HEAD_DIM = 64
NSTATE = 128
KW = 4
HEADS = 48
BCD = 384

epsilon = 1e-05


Q = 128
GROUP = 8
LANES = GROUP * HEAD_DIM
NEG = -1e30
VMEM = 56 * 1024 * 1024


def dot32(a, b, dims=(((1,), (0,)), ((), ())), precision=None):
    return lax.dot_general(a, b, dims, preferred_element_type=jnp.float32, precision=precision)


NT = (((1,), (1,)), ((), ()))


def row_ids(start, rows, cols):
    return lax.broadcasted_iota(jnp.int32, (rows, cols), 0) + start


def shifted_down(ref, cols, c, first, width):
    if c == 0:
        tall = jnp.concatenate([jnp.zeros((8, width), jnp.float32), ref[0:Q, cols]], axis=0)
    else:
        tall = ref[c * Q - 8 : c * Q + Q, cols]
    place = row_ids(c * Q, Q, width)
    outs = [tall[8:]]
    for j in range(1, KW):
        moved = pltpu.roll(tall, j, 0)[8:]
        keep = (place >= j) & ((place < first) | (place >= first + j))
        outs.append(jnp.where(keep, moved, 0.0))
    return outs


def conv_back(ref, cols, c, first, width, taps):
    tall = ref[c * Q : c * Q + Q + 8, cols]
    place = row_ids(c * Q, Q, width)
    total = taps[KW - 1] * tall[:Q]
    for j in range(1, KW):
        moved = pltpu.roll(tall, Q + 8 - j, 0)[:Q]
        keep = (place < first - j) | (place >= first)
        total = total + taps[KW - 1 - j] * jnp.where(keep, moved, 0.0)
    return total


def sigmoid(v):
    return 0.5 * jnp.tanh(0.5 * v) + 0.5


def sum_rows(v):
    return jnp.sum(v, axis=0, keepdims=True)


def prep_kernel(first_ref, bcd_ref, conv_ref, head_ref, wide_ref, tall_ref, bc_ref, bct_ref):
    first = first_ref[0]
    tri = (row_ids(0, Q, Q) >= lax.broadcasted_iota(jnp.int32, (Q, Q), 1)).astype(jnp.float32)
    rate = -jnp.exp(head_ref[1:2, :])
    lane = lax.broadcasted_iota(jnp.int32, (Q, 128), 1)
    for c in range(bcd_ref.shape[0] // Q):
        rows = slice(c * Q, c * Q + Q)
        moved = shifted_down(bcd_ref, slice(0, 2 * NSTATE), c, first, 2 * NSTATE)
        mixed = conv_ref[4:5, :] + conv_ref[3:4, :] * moved[0]
        for j in range(1, KW):
            mixed = mixed + conv_ref[KW - 1 - j : KW - j, :] * moved[j]
        act = mixed * sigmoid(mixed)
        b32, c32 = act[:, :NSTATE], act[:, NSTATE:]
        b16, c16 = b32.astype(jnp.bfloat16), c32.astype(jnp.bfloat16)
        bc_ref[rows, :] = act.astype(jnp.bfloat16)
        bct_ref[:NSTATE, rows] = b32.T.astype(jnp.bfloat16)
        bct_ref[NSTATE:, rows] = c32.T.astype(jnp.bfloat16)
        wide_ref[rows, :Q] = dot32(c16, b16, NT)
        wide_ref[rows, Q : 2 * Q] = dot32(b16, c16, NT)
        raw = jnp.where(lane < HEADS, bcd_ref[rows, 2 * NSTATE :] + head_ref[0:1, :], 0.0)
        step = jax.nn.softplus(raw)
        cum = dot32(tri, rate * step, precision=lax.Precision.HIGHEST)
        cp = cum - jnp.log(jnp.maximum(step, 1e-37))
        wide_ref[rows, 2 * Q : 3 * Q] = cum
        wide_ref[rows, 3 * Q :] = cp
        tall_ref[:128, rows] = cum.T
        tall_ref[128:, rows] = cp.T


def chunk_masks(first, c, transposed):
    base = c * Q
    row = row_ids(base, Q, Q)
    col = lax.broadcasted_iota(jnp.int32, (Q, Q), 1) + base
    ordered = (col >= row) if transposed else (row >= col)
    inside = ordered & ((row >= first) == (col >= first))
    carry = ((row >= first) == (base - 1 >= first)) & (base > 0)
    last = (row >= first) == (base + Q - 1 >= first)
    through = (base > 0) & ((base + Q - 1 >= first) == (base - 1 >= first))
    return inside, carry, last, through


def lane_column(values, k):
    return jnp.broadcast_to(values[:, k : k + 1], (Q, Q))


def conv_act(x_ref, conv_ref, cols, c, first):
    moved = shifted_down(x_ref, cols, c, first, Q)
    mixed = conv_ref[4:5, cols] + conv_ref[3:4, cols] * moved[0]
    for j in range(1, KW):
        mixed = mixed + conv_ref[KW - 1 - j : KW - j, cols] * moved[j]
    return moved, mixed


def both_heads(left, right, half):
    none = jnp.zeros_like(right)
    stacked = jnp.concatenate([jnp.where(half, right, none), jnp.where(half, none, right)], axis=0)
    return dot32(jnp.concatenate(left, axis=1), stacked)


def forward_kernel(first_ref, x_ref, conv_ref, gain_ref, wide_ref, tall_ref, bc_ref, bct_ref, ssm_ref, states_ref, state):
    first = first_ref[0]
    group = pl.program_id(0)
    half = lax.broadcasted_iota(jnp.int32, (Q, Q), 1) < HEAD_DIM
    state[...] = jnp.zeros_like(state)
    shift = (Q - GROUP * group) % Q
    pairs = range(GROUP // 2)
    for c in range(x_ref.shape[0] // Q):
        rows = slice(c * Q, c * Q + Q)
        inside, carry, last, through = chunk_masks(first, c, False)
        cum = pltpu.roll(wide_ref[rows, 2 * Q : 3 * Q], shift, 1)
        cp = pltpu.roll(wide_ref[rows, 3 * Q :], shift, 1)
        cpt = tall_ref[pl.ds(pl.multiple_of(128 + group * GROUP, GROUP), GROUP), rows]
        scores = wide_ref[rows, :Q]
        old16 = state[...].astype(jnp.bfloat16)
        states_ref[c * NSTATE : (c + 1) * NSTATE, :] = old16
        if c > 0:
            carried = dot32(bc_ref[rows, NSTATE:], old16)
        weighted, ends = [], []
        for p in pairs:
            cols = slice(p * Q, p * Q + Q)
            _, mixed = conv_act(x_ref, conv_ref, cols, c, first)
            xs = mixed * sigmoid(mixed)
            mixing, cums, cps = [], [], []
            for k in (2 * p, 2 * p + 1):
                cum_b = lane_column(cum, k)
                decay = jnp.exp(jnp.where(inside, cum_b - cpt[k : k + 1, :], NEG))
                mixing.append((scores * decay).astype(jnp.bfloat16))
                cums.append(cum_b)
                cps.append(lane_column(cp, k))
            cum_pair = jnp.where(half, cums[0], cums[1])
            cp_pair = jnp.where(half, cps[0], cps[1])
            y = both_heads(mixing, xs.astype(jnp.bfloat16), half)
            if c > 0:
                y = y + jnp.where(carry, jnp.exp(cum_pair), 0.0) * carried[:, cols]
            ssm_ref[rows, cols] = y + gain_ref[0:1, cols] * xs
            end = cum_pair[Q - 1 : Q, :]
            weighted.append((jnp.where(last, jnp.exp(end - cp_pair), 0.0) * xs).astype(jnp.bfloat16))
            ends.append(end)
        fresh = dot32(bct_ref[:NSTATE, rows], jnp.concatenate(weighted, axis=1))
        for p in pairs:
            cols = slice(p * Q, p * Q + Q)
            kept = 0.0 if c == 0 else jnp.where(through, jnp.exp(ends[p]), 0.0) * state[:, cols]
            state[:, cols] = kept + fresh[:, cols]


def gated_kernel(order, me_ref, z_ref, ssm_ref, gain_ref, gated_ref, sent_ref, r_ref):
    squares = jnp.zeros((Q, Q), jnp.float32)
    for p in range(z_ref.shape[1] // Q):
        cols = slice(p * Q, p * Q + Q)
        zv = z_ref[:, cols]
        g = ssm_ref[:, cols] * (zv * sigmoid(zv))
        squares = squares + g * g
    r = lax.rsqrt(jnp.sum(squares, axis=-1, keepdims=True) / DI + epsilon)
    wide = jnp.broadcast_to(r, (Q, Q))
    r_ref[...] = wide
    for p in range(z_ref.shape[1] // Q):
        cols = slice(p * Q, p * Q + Q)
        zv = z_ref[:, cols]
        g = ssm_ref[:, cols] * (zv * sigmoid(zv))
        gated_ref[:, cols] = (g * wide * gain_ref[1:2, cols]).astype(gated_ref.dtype)
    part = gated_ref.shape[1] // 8
    for i, j in enumerate(order):
        sent_ref[:, i * part : (i + 1) * part] = gated_ref[:, pl.ds(pl.multiple_of((me_ref[0] ^ j) * part, 128), part)]


def gate_kernel(z_ref, ssm_ref, cot_ref, weight_ref, rk_ref, gain_ref, dz_ref, ds_ref, grads_ref, d_gated):
    d_gated[...] = dot32(cot_ref[...], weight_ref[...], NT)
    grads_ref[...] = jnp.zeros_like(grads_ref)
    for c in range(z_ref.shape[0] // Q):
        rows = slice(c * Q, c * Q + Q)
        scale = lane_column(rk_ref[rows, :], 0)
        pull = lane_column(rk_ref[rows, :], 1)
        for p in range(z_ref.shape[1] // Q):
            cols = slice(p * Q, p * Q + Q)
            zv = z_ref[rows, cols]
            sz = sigmoid(zv)
            silu_z = zv * sz
            ssm = ssm_ref[rows, cols]
            g = ssm * silu_z
            gs = d_gated[rows, cols] * scale
            grads_ref[0:1, cols] += sum_rows(gs * g)
            d_g = gain_ref[1:2, cols] * gs - g * pull
            dz_ref[rows, cols] = (d_g * ssm * (sz + silu_z * (1.0 - sz))).astype(dz_ref.dtype)
            ds_ref[rows, cols] = (d_g * silu_z).astype(ds_ref.dtype)


def eight_rows(v):
    return functools.reduce(jnp.add, [v[i : i + 8, :] for i in range(0, v.shape[0], 8)])


def backward_kernel(base, first_ref, x_ref, ssm_ref, ds_ref, conv_ref, gain_ref, wide_ref, tall_ref, bc_ref, bct_ref, states_ref, d_ref, grads_ref, sums_ref, flow_ref, dstate, dconv, acc):
    first = first_ref[0]
    group = base + pl.program_id(0)
    half = lax.broadcasted_iota(jnp.int32, (Q, Q), 1) < HEAD_DIM
    dstate[...] = jnp.zeros_like(dstate)
    acc[...] = jnp.zeros_like(acc)
    rows_all = x_ref.shape[0]
    dconv[rows_all : rows_all + 8, :] = jnp.zeros((8, dconv.shape[1]), jnp.float32)
    flow_ref[...] = jnp.zeros_like(flow_ref)

    @pl.when(pl.program_id(0) == 0)
    def _():
        sums_ref[...] = jnp.zeros_like(sums_ref)

    shift = (Q - GROUP * group) % Q
    chunks = rows_all // Q
    pairs = range(GROUP // 2)
    pick = (lax.broadcasted_iota(jnp.int32, (LANES, Q), 1) == GROUP * group + row_ids(0, LANES, Q) // HEAD_DIM).astype(jnp.bfloat16)
    for c in range(chunks - 1, -1, -1):
        rows = slice(c * Q, c * Q + Q)
        inside, carry, last, through = chunk_masks(first, c, True)
        cum = pltpu.roll(wide_ref[rows, 2 * Q : 3 * Q], shift, 1)
        cp = pltpu.roll(wide_ref[rows, 3 * Q :], shift, 1)
        cumt = tall_ref[pl.ds(pl.multiple_of(group * GROUP, GROUP), GROUP), rows]
        scores_t = wide_ref[rows, Q : 2 * Q]
        b16, c16t = bc_ref[rows, :NSTATE], bct_ref[NSTATE:, rows]
        dst = jnp.zeros((Q, Q), jnp.float32)
        if c < chunks - 1:
            later16 = dstate[...].astype(jnp.bfloat16)
            carried = dot32(b16, later16)
        high, low, local, weighted, carries, eys, ends = ([] for _ in range(7))
        for p in pairs:
            cols = slice(p * Q, p * Q + Q)
            moved, mixed = conv_act(x_ref, conv_ref, cols, c, first)
            sx = sigmoid(mixed)
            xs = mixed * sx
            x16 = xs.astype(jnp.bfloat16)
            skip = gain_ref[0:1, cols]
            dy16 = ds_ref[rows, cols]
            d_ssm = dy16.astype(jnp.float32)
            acc[40:48, cols] += eight_rows(d_ssm * xs)
            mixing, cums, cps = [], [], []
            for k in (2 * p, 2 * p + 1):
                cp_b = lane_column(cp, k)
                decay = jnp.exp(jnp.where(inside, cumt[k : k + 1, :] - cp_b, NEG))
                mixing.append((scores_t * decay).astype(jnp.bfloat16))
                x_half = jnp.where(half == (k == 2 * p), x16, jnp.zeros_like(x16))
                dst = dst + decay * dot32(x_half, dy16, NT)
                cums.append(lane_column(cum, k))
                cps.append(cp_b)
            cum_pair = jnp.where(half, cums[0], cums[1])
            cp_pair = jnp.where(half, cps[0], cps[1])
            dx = both_heads(mixing, dy16, half)
            in_dot = x16.astype(jnp.float32) * dx
            u = d_ssm * (ssm_ref[rows, cols] - skip * xs) - in_dot
            high.append(u.astype(jnp.bfloat16))
            low.append((u - high[-1].astype(jnp.float32)).astype(jnp.bfloat16))
            local.append(in_dot.astype(jnp.bfloat16))
            end = cum_pair[Q - 1 : Q, :]
            ends.append(end)
            if c < chunks - 1:
                weight = jnp.where(last, jnp.exp(end - cp_pair), 0.0)
                moved_in = weight * carried[:, cols]
                dx = dx + moved_in
                carries.append((xs * moved_in).astype(jnp.bfloat16))
                weighted.append((weight * xs).astype(jnp.bfloat16))
            if c > 0:
                eys.append((jnp.where(carry, jnp.exp(cum_pair), 0.0) * d_ssm).astype(jnp.bfloat16))
            d_mixed = (dx + skip * d_ssm) * (sx + xs * (1.0 - sx))
            dconv[rows, cols] = d_mixed
            acc[32:40, cols] += eight_rows(d_mixed)
            for j in range(KW):
                acc[8 * (KW - 1 - j) : 8 * (KW - j), cols] += eight_rows(d_mixed * moved[j])
            taps = [conv_ref[i : i + 1, cols] for i in range(KW)]
            d_ref[rows, cols] = conv_back(dconv, cols, c, first, Q, taps).astype(d_ref.dtype)
        join = functools.partial(jnp.concatenate, axis=1)
        sums_ref[rows, :Q] += dst
        sums_ref[rows, 3 * Q : 4 * Q] += dot32(join(high), pick) + dot32(join(low), pick)
        sums_ref[rows, 4 * Q : 5 * Q] += dot32(join(local), pick)
        if c < chunks - 1:
            sums_ref[rows, Q : 2 * Q] += dot32(join(weighted), later16, NT)
            sums_ref[rows, 5 * Q :] += dot32(join(carries), pick)
        if c > 0:
            ey16 = join(eys)
            old16 = states_ref[c * NSTATE : (c + 1) * NSTATE, :]
            sums_ref[rows, 2 * Q : 3 * Q] += dot32(ey16, old16, NT)
            fresh = dot32(c16t, ey16)
            for p in pairs:
                cols = slice(p * Q, p * Q + Q)
                if c < chunks - 1:
                    kept = jnp.where(through, jnp.exp(ends[p]), 0.0) * dstate[:, cols]
                    flow_ref[c : c + 1, cols] = sum_rows(kept * old16[:, cols].astype(jnp.float32))
                    dstate[:, cols] = kept + fresh[:, cols]
                else:
                    dstate[:, cols] = fresh[:, cols]
    for i in range(8):
        grads_ref[i : i + 1, :] = sum_rows(acc[8 * i : 8 * i + 8, :]) if i < 6 else jnp.zeros((1, LANES), jnp.float32)


def post_kernel(calls, first_ref, bcd_ref, conv_ref, head_ref, bc_ref, *refs):
    sums_refs, flow_refs, (d_ref, grads_ref, hgrads_ref, dconv) = refs[:calls], refs[calls:-4], refs[-4:]
    first = first_ref[0]
    rows_all = bcd_ref.shape[0]
    wide = 2 * NSTATE
    dconv[rows_all : rows_all + 8, :] = jnp.zeros((8, wide), jnp.float32)
    grads_ref[...] = jnp.zeros_like(grads_ref)
    hgrads_ref[...] = jnp.zeros_like(hgrads_ref)
    lane = lax.broadcasted_iota(jnp.int32, (Q, 128), 1)
    rate = -jnp.exp(head_ref[1:2, :])
    flow = jnp.zeros((8, 128), jnp.float32)
    start = 0
    for ref in flow_refs:
        width = ref.shape[1]
        spread = (row_ids(start, width, 128) // HEAD_DIM == lax.broadcasted_iota(jnp.int32, (width, 128), 1)).astype(jnp.float32)
        flow = flow + dot32(ref[...], spread, precision=lax.Precision.HIGHEST)
        start += width
    row, col = row_ids(0, Q, Q), lax.broadcasted_iota(jnp.int32, (Q, Q), 1)
    earlier_sum = (col < row).astype(jnp.float32)
    for c in range(rows_all // Q - 1, -1, -1):
        rows = slice(c * Q, c * Q + Q)
        moved = shifted_down(bcd_ref, slice(0, wide), c, first, wide)
        mixed = conv_ref[4:5, :] + conv_ref[3:4, :] * moved[0]
        for j in range(1, KW):
            mixed = mixed + conv_ref[KW - 1 - j : KW - j, :] * moved[j]
        sx = sigmoid(mixed)
        dst, db, dc, us, vs, carried = (functools.reduce(jnp.add, [ref[rows, i * Q : (i + 1) * Q] for ref in sums_refs]) for i in range(6))
        d_b = db + dot32(dst.astype(jnp.bfloat16), bc_ref[rows, NSTATE:])
        d_c = dc + dot32(dst.T.astype(jnp.bfloat16), bc_ref[rows, :NSTATE])
        d_mixed = jnp.concatenate([d_b, d_c], axis=1) * (sx + mixed * sx * (1.0 - sx))
        dconv[rows, :] = d_mixed
        grads_ref[4:5, :] += sum_rows(d_mixed)
        for j in range(KW):
            grads_ref[KW - 1 - j : KW - j, :] += sum_rows(d_mixed * moved[j])
        taps = [conv_ref[i : i + 1, :] for i in range(KW)]
        d_ref[rows, :wide] = conv_back(dconv, slice(0, wide), c, first, wide, taps).astype(d_ref.dtype)
        later_sum = ((col >= row) & ((row + c * Q >= first) == (col + c * Q >= first))).astype(jnp.float32)
        d_la = dot32(later_sum, us, precision=lax.Precision.HIGHEST)
        d_la = d_la + dot32(earlier_sum, carried, precision=lax.Precision.HIGHEST) + flow[c : c + 1, :]
        d_log = vs + carried
        raw = bcd_ref[rows, wide:] + head_ref[0:1, :]
        step = jax.nn.softplus(raw)
        sig = sigmoid(raw)
        ratio = jnp.where(raw < -17.0, 1.0, sig / jnp.maximum(step, 1e-37))
        d_raw = jnp.where(lane < HEADS, d_log * ratio + d_la * rate * sig, 0.0)
        d_ref[rows, wide:] = d_raw.astype(d_ref.dtype)
        hgrads_ref[0:1, :] += sum_rows(d_raw)
        hgrads_ref[1:2, :] += sum_rows(jnp.where(lane < HEADS, d_la * rate * step, 0.0))


def smem():
    return pl.BlockSpec(memory_space=pltpu.SMEM)


def whole(shape):
    return pl.BlockSpec(shape, lambda g: (0,) * len(shape))


def shaped(shape, kind):
    return jax.ShapeDtypeStruct(shape, kind)


def params(limit=VMEM):
    return pltpu.CompilerParams(vmem_limit_bytes=limit)


def cost(flops, size):
    return pl.CostEstimate(flops=flops // 3, bytes_accessed=size // 3, transcendentals=0)


def run_prep(first, bcd, conv, heads):
    rows = bcd.shape[0]
    f32, b16 = jnp.float32, jnp.bfloat16
    shapes = [((rows, 4 * Q), f32), ((256, rows), f32), ((rows, 2 * NSTATE), b16), ((2 * NSTATE, rows), b16)]
    return pl.pallas_call(
        prep_kernel,
        grid=(1,),
        in_specs=[smem(), whole((rows, BCD)), whole((8, 2 * NSTATE)), whole((8, 128))],
        out_specs=[whole(s) for s, _ in shapes],
        out_shape=[shaped(s, d) for s, d in shapes],
        compiler_params=params(),
        cost_estimate=cost(2000000000, 4000000),
    )(first, bcd, conv, heads)


def run_forward(first, x, conv, gains, prep):
    rows, width = x.shape
    chunks = rows // Q
    here = lambda g: (0, g)
    block, eight = pl.BlockSpec((rows, LANES), here), pl.BlockSpec((8, LANES), here)
    return pl.pallas_call(
        forward_kernel,
        grid=(width // LANES,),
        in_specs=[smem(), block, eight, eight] + [whole(v.shape) for v in prep],
        out_specs=[block, pl.BlockSpec((chunks * NSTATE, LANES), here)],
        out_shape=[shaped((rows, width), jnp.float32), shaped((chunks * NSTATE, width), jnp.bfloat16)],
        scratch_shapes=[pltpu.VMEM((NSTATE, LANES), jnp.float32)],
        compiler_params=params(),
        cost_estimate=cost(20000000000, 20000000),
    )(first, x, conv, gains, *prep)


def run_gated(order, me, z, ssm, gains):
    rows, width = z.shape
    b16 = jnp.bfloat16
    block = pl.BlockSpec((Q, width), lambda g: (g, 0))
    thin = pl.BlockSpec((Q, Q), lambda g: (g, 0))
    return pl.pallas_call(
        functools.partial(gated_kernel, order),
        grid=(rows // Q,),
        in_specs=[smem(), block, block, whole(gains.shape)],
        out_specs=[block, block, thin],
        out_shape=[shaped((rows, width), b16), shaped((rows, width), b16), shaped((rows, Q), jnp.float32)],
        compiler_params=params(),
        cost_estimate=cost(4000000000, 16000000),
    )(me, z, ssm, gains)


def run_gate(z, ssm, cot, weight, rk, gains):
    rows, width = cot.shape
    b16 = jnp.bfloat16
    here = lambda g: (0, g)
    block, eight = pl.BlockSpec((rows, LANES), here), pl.BlockSpec((8, LANES), here)
    return pl.pallas_call(
        gate_kernel,
        grid=(DI // LANES,),
        in_specs=[block, block, whole(cot.shape), pl.BlockSpec((LANES, width), lambda g: (g, 0)), whole(rk.shape), eight],
        out_specs=[block, block, eight],
        out_shape=[shaped((rows, DI), b16)] * 2 + [shaped((8, DI), jnp.float32)],
        scratch_shapes=[pltpu.VMEM((rows, LANES), jnp.float32)],
        compiler_params=params(),
        cost_estimate=cost(12000000000, 36000000),
    )(z, ssm, cot, weight, rk, gains)


def run_backward(base, count, first, x, ssm, ds, conv, gains, prep, states):
    rows = x.shape[0]
    f32, b16 = jnp.float32, jnp.bfloat16
    chunks = rows // Q
    at = lambda g: (0, g + base)
    here = lambda g: (0, g)
    block, eight = pl.BlockSpec((rows, LANES), at), pl.BlockSpec((8, LANES), at)
    own = pl.BlockSpec((8, LANES), here)
    return pl.pallas_call(
        functools.partial(backward_kernel, base),
        grid=(count,),
        in_specs=[smem(), block, block, block, eight, eight] + [whole(v.shape) for v in prep] + [pl.BlockSpec((chunks * NSTATE, LANES), at)],
        out_specs=[pl.BlockSpec((rows, LANES), here), own, whole((rows, 6 * Q)), own],
        out_shape=[shaped((rows, count * LANES), b16), shaped((8, count * LANES), f32), shaped((rows, 6 * Q), f32), shaped((8, count * LANES), f32)],
        scratch_shapes=[pltpu.VMEM((NSTATE, LANES), f32), pltpu.VMEM((rows + 8, LANES), f32), pltpu.VMEM((48, LANES), f32)],
        compiler_params=params(),
        cost_estimate=cost(count * 7000000000, count * 8000000),
    )(first, x, ssm, ds, conv, gains, *prep, states)


def run_post(first, bcd, conv, heads, prep, backs):
    rows = bcd.shape[0]
    bc = prep[2]
    f32 = jnp.float32
    sums = [t for some in zip(*backs) for t in some]
    return pl.pallas_call(
        functools.partial(post_kernel, len(backs)),
        grid=(1,),
        in_specs=[smem(), whole((rows, BCD)), whole((8, 2 * NSTATE)), whole((8, 128)), whole(bc.shape)] + [whole(t.shape) for t in sums],
        out_specs=[whole((rows, BCD)), whole((8, 2 * NSTATE)), whole((8, 128))],
        out_shape=[shaped((rows, BCD), jnp.bfloat16), shaped((8, 2 * NSTATE), f32), shaped((8, 128), f32)],
        scratch_shapes=[pltpu.VMEM((rows + 8, 2 * NSTATE), f32)],
        compiler_params=params(),
        cost_estimate=cost(4000000000, 8000000),
    )(first, bcd, conv, heads, bc, *sums)


def contract_rows(left, right, kind=jnp.float32):
    return lax.dot_general(left, right, (((0,), (0,)), ((), ())), preferred_element_type=kind)


def pad_lanes(v, width):
    return jnp.pad(v, ((0, 0), (0, width - v.shape[1])))


ORDER = (7, 3, 5, 1, 6, 2, 4, 0)
DOUBLED = (0, 2, 4, 6, 1, 3, 5, 7)
WIDE = 512


def project_kernel(places, me_ref, left_ref, *refs):
    pieces, (out_ref, full_ref) = refs[:-2], refs[-2:]
    part = full_ref.shape[0] // 8
    for (j, skip, rows), ref in zip(places, pieces):
        full_ref[pl.ds(pl.multiple_of((me_ref[0] ^ j) * part + skip, 16), rows), :] = ref[:rows, :]
    out_ref[...] = dot32(left_ref[...], full_ref[...])


def run_project(me, left, pieces, skip, cols):
    rows, inner = left.shape
    step = min(WIDE, cols)
    here = lambda g: (0, g)
    places = tuple((j, start, min(v.shape[0], inner // 8 - start)) for v, j, start in pieces)
    return pl.pallas_call(
        functools.partial(project_kernel, places),
        grid=(cols // step,),
        in_specs=[smem(), whole(left.shape)] + [pl.BlockSpec((v.shape[0], step), lambda g: (0, g + skip // step)) for v, _, _ in pieces],
        out_specs=[pl.BlockSpec((rows, step), here), pl.BlockSpec((inner, step), here)],
        out_shape=[shaped((rows, cols), jnp.float32), shaped((inner, cols), left.dtype)],
        compiler_params=params(),
        cost_estimate=cost(2 * rows * inner * cols, 4 * inner * (rows + cols) + 4 * rows * cols),
    )(me, left, *[v for v, _, _ in pieces])


def unpack_kernel(widths, me_ref, small_ref, gain_ref, conv_ref, heads_ref, gains_ref, found):
    for k, j in enumerate(DOUBLED):
        found[me_ref[0] ^ j] = small_ref[k * SMALL : (k + 1) * SMALL, :].astype(jnp.float32)
    for ref in (gain_ref, conv_ref, heads_ref, gains_ref):
        ref[...] = jnp.zeros_like(ref)
    wide, taps, few, long = widths
    for i in range(8):
        gain_ref[:, i * wide : (i + 1) * wide] = found[i, 0:1, :wide]
        conv_ref[0:5, i * taps : (i + 1) * taps] = found[i, 1:6, :taps]
        heads_ref[0:3, i * few : (i + 1) * few] = found[i, 6:9, :few]
        gains_ref[1:2, i * long : (i + 1) * long] = found[i, 9:10, :long]
    spread = (row_ids(0, 128, DI) == lax.broadcasted_iota(jnp.int32, (128, DI), 1) // HEAD_DIM).astype(jnp.float32)
    gains_ref[0:1, :] = dot32(heads_ref[...], spread, precision=lax.Precision.HIGHEST)[2:3, :]


def out_kernel(gated_ref, weight_ref, x_ref, cot_ref, r_ref, result_ref, rk_ref, acc):
    weight = weight_ref[...]
    branch = dot32(gated_ref[...], weight)
    result_ref[...] = (x_ref[...].astype(jnp.float32) + branch).astype(result_ref.dtype)
    product = cot_ref[...].astype(jnp.float32) * branch
    part = product[:, :Q]
    for p in range(1, product.shape[1] // Q):
        part = part + product[:, p * Q : (p + 1) * Q]

    @pl.when(pl.program_id(0) == 0)
    def _():
        acc[...] = part

    @pl.when(pl.program_id(0) > 0)
    def _():
        acc[...] += part

    @pl.when(pl.program_id(0) == pl.num_programs(0) - 1)
    def _():
        r = r_ref[...]
        pull = r * r * (jnp.sum(acc[...], axis=-1, keepdims=True) / DI)
        lane = lax.broadcasted_iota(jnp.int32, rk_ref.shape, 1)
        rk_ref[...] = jnp.where(lane == 0, r, jnp.where(lane == 1, pull, 0.0))


def run_out(gated, weight, x, cot, r):
    rows, inner = gated.shape
    width = x.shape[1]
    step = width // 3
    here = lambda g: (0, g)
    return pl.pallas_call(
        out_kernel,
        grid=(3,),
        in_specs=[whole(gated.shape)] + [pl.BlockSpec((v.shape[0], step), here) for v in (weight, x, cot)] + [whole(r.shape)],
        out_specs=[pl.BlockSpec((rows, step), here), whole((rows, 128))],
        out_shape=[shaped((rows, width), x.dtype), shaped((rows, 128), jnp.float32)],
        scratch_shapes=[pltpu.VMEM((rows, Q), jnp.float32)],
        compiler_params=params(),
        cost_estimate=cost(4 * rows * inner * width, 4 * inner * width + 8 * rows * width),
    )(gated, weight, x, cot, r)


def pack_kernel(calls, widths, *refs):
    x_refs, (b_ref, h_ref, g_ref, n_ref, out_ref, conv) = refs[:calls], refs[calls:]
    wide, taps, few, long = widths
    start = 0
    for ref in (*x_refs, b_ref):
        conv[:, start : start + ref.shape[1]] = ref[...]
        start += ref.shape[1]
    inner = 8 * long
    spread = (row_ids(0, inner, 128) // HEAD_DIM == lax.broadcasted_iota(jnp.int32, (inner, 128), 1)).astype(jnp.float32)
    skips = dot32(conv[:, :inner], spread, precision=lax.Precision.HIGHEST)
    out_ref[...] = jnp.zeros_like(out_ref)
    for i in range(8):
        fields = [n_ref[0:1, i * wide : (i + 1) * wide]]
        fields += [conv[k : k + 1, i * taps : (i + 1) * taps] for k in range(KW + 1)]
        fields += [h_ref[k : k + 1, i * few : (i + 1) * few] for k in range(2)] + [skips[5:6, i * few : (i + 1) * few]]
        fields += [g_ref[0:1, i * long : (i + 1) * long]]
        start = 0
        for field in fields:
            out_ref[i : i + 1, start : start + field.shape[1]] = field
            start += field.shape[1]


def run_pack(widths, x_grads, b_grads, h_grads, g_grads, n_grads):
    wide, taps, few, long = widths
    width = wide + (KW + 1) * taps + 3 * few + long
    width += -width % 128
    args = (*x_grads, b_grads, h_grads, g_grads, n_grads)
    return pl.pallas_call(
        functools.partial(pack_kernel, len(x_grads), widths),
        grid=(1,),
        in_specs=[whole(v.shape) for v in args],
        out_specs=whole((8, width)),
        out_shape=shaped((8, width), jnp.float32),
        scratch_shapes=[pltpu.VMEM((8, 8 * taps), jnp.float32)],
        compiler_params=params(),
        cost_estimate=cost(1000000, 1000000),
    )(*args)


def back_kernel(spans, based, *refs):
    out_ref = refs[-1]
    grid = pl.program_id(0)

    @pl.when(grid == 0)
    def _():
        out_ref[...] = refs[0][...] if based else jnp.zeros_like(out_ref)

    refs = refs[based:-1]
    for i, (start, stop) in enumerate(spans):

        @pl.when((grid >= start) & (grid < stop))
        def _():
            out_ref[...] += dot32(refs[2 * i][...], refs[2 * i + 1][...], NT)


def run_back(pairs, base=None):
    rows, inner = pairs[0][0].shape[0], pairs[0][2].shape[0]
    spans, specs, args, start = [], [], [], 0
    if base is not None:
        specs, args = [whole((rows, inner))], [base]
    for grad, left_skip, weight, right_skip, width in pairs:
        step = min(WIDE, width)
        steps = width // step
        spans.append((start, start + steps))

        def at(skip, g, start=start, steps=steps):
            return (0, jnp.clip(g - start, 0, steps - 1) + skip)

        specs += [pl.BlockSpec((rows, step), functools.partial(at, left_skip // step)), pl.BlockSpec((inner, step), functools.partial(at, right_skip // step))]
        args += [grad, weight]
        start += steps
    return pl.pallas_call(
        functools.partial(back_kernel, tuple(spans), int(base is not None)),
        grid=(start,),
        in_specs=specs,
        out_specs=whole((rows, inner)),
        out_shape=shaped((rows, inner), jnp.float32),
        input_output_aliases={0: 0} if base is not None else {},
        compiler_params=params(),
        cost_estimate=cost(3000, 3000),
    )(*args)


TN = (((0,), (0,)), ((), ()))


def terms_kernel(turned, left_ref, right_ref, got_ref, *outs):
    rows = outs[0].shape[0]
    if turned:
        product = dot32(left_ref[...], right_ref[...], TN)
    else:
        product = dot32(left_ref[...], right_ref[...])
    product = product + got_ref[...].astype(jnp.float32)
    for i, ref in enumerate(outs):
        ref[...] = product[i * rows : (i + 1) * rows, :].astype(ref.dtype)


def run_terms(left, right, got, turned=False):
    rows, cols = got.shape
    inner = right.shape[0]
    step = 512 if cols % 512 == 0 else cols
    here = lambda g: (0, g)
    kinds = [jnp.bfloat16] * 3 + [jnp.float32]
    half = pl.BlockSpec((inner, rows), lambda g: (0, 1)) if turned else pl.BlockSpec((rows, inner), lambda g: (1, 0))
    return pl.pallas_call(
        functools.partial(terms_kernel, turned),
        grid=(cols // step,),
        in_specs=[half, pl.BlockSpec((inner, step), here), pl.BlockSpec((rows, step), here)],
        out_specs=[pl.BlockSpec((rows // 4, step), here)] * 4,
        out_shape=[shaped((rows // 4, cols), kind) for kind in kinds],
        compiler_params=params(),
        cost_estimate=cost(2 * rows * inner * cols, 6 * rows * cols),
    )(left, right, got)


def norm_kernel(order, me_ref, x_ref, gain_ref, out_ref, sent_ref, turned):
    rows, width = x_ref.shape
    for c in range(rows // Q):
        place = slice(c * Q, c * Q + Q)
        v = x_ref[place, :].astype(jnp.float32)
        normed = v * lax.rsqrt(jnp.mean(v * v, axis=-1, keepdims=True) + epsilon) * gain_ref[...]
        out_ref[place, :] = normed.astype(out_ref.dtype)
        for p in range(width // Q):
            turned[p * Q : p * Q + Q, place] = normed[:, p * Q : p * Q + Q].T.astype(turned.dtype)
    part = width // len(order)
    for k, j in enumerate(order):
        sent_ref[k * part : (k + 1) * part, :] = turned[pl.ds(pl.multiple_of((me_ref[0] ^ j) * part, 16), part), :]


def run_norm(order, me, x, gain):
    rows, width = x.shape
    b16 = jnp.bfloat16
    return pl.pallas_call(
        functools.partial(norm_kernel, order),
        grid=(1,),
        in_specs=[smem(), whole(x.shape), whole((1, width))],
        out_specs=[whole(x.shape), whole((width, rows))],
        out_shape=[shaped(x.shape, b16), shaped((width, rows), b16)],
        scratch_shapes=[pltpu.VMEM((width, rows), b16)],
        compiler_params=params(),
        cost_estimate=cost(2000000000, 6 * rows * width),
    )(me, x, gain)


def open_kernel(places, widths, me_ref, first_ref, x_ref, small_ref, *refs):
    pieces, refs = refs[: len(places)], refs[len(places) :]
    gain_ref, conv_ref, heads_ref, gains_ref, out_ref, sent_ref, bcd_ref, full_ref, *prep_refs, found, turned = refs
    unpack_kernel(widths, me_ref, small_ref, gain_ref, conv_ref, heads_ref, gains_ref, found)
    norm_kernel(ORDER, me_ref, x_ref, gain_ref, out_ref, sent_ref, turned)
    project_kernel(places, me_ref, out_ref, *pieces, bcd_ref, full_ref)
    prep_kernel(first_ref, bcd_ref, conv_ref.at[:, pl.ds(DI, 2 * NSTATE)], heads_ref, *prep_refs)


def run_open(me, first, x, small, pieces, widths, skip):
    f32, b16 = jnp.float32, jnp.bfloat16
    toks, width = x.shape
    wide, taps, few, long = widths
    places = tuple((j, start, min(v.shape[0], width // 8 - start)) for v, j, start in pieces)
    shapes = [((1, 8 * wide), f32), ((8, 8 * taps), f32), ((8, 128), f32), ((8, 8 * long), f32)]
    shapes += [((toks, width), b16), ((width, toks), b16), ((toks, BCD), f32), ((width, BCD), b16)]
    shapes += [((toks, 4 * Q), f32), ((256, toks), f32), ((toks, 2 * NSTATE), b16), ((2 * NSTATE, toks), b16)]
    return pl.pallas_call(
        functools.partial(open_kernel, places, widths),
        grid=(1,),
        in_specs=[smem(), smem(), whole(x.shape), whole(small.shape)] + [pl.BlockSpec((v.shape[0], BCD), lambda g: (0, skip // BCD)) for v, _, _ in pieces],
        out_specs=[whole(s) for s, _ in shapes],
        out_shape=[shaped(s, d) for s, d in shapes],
        scratch_shapes=[pltpu.VMEM((8, SMALL, small.shape[1]), f32), pltpu.VMEM((width, toks), b16)],
        compiler_params=params(),
        cost_estimate=cost(6000000000, 10000000),
    )(me, first, x, small, *[v for v, _, _ in pieces])


def norm_back_kernel(d_ref, x_ref, cot_ref, gain_ref, out_ref, grad_ref):
    @pl.when(pl.program_id(0) == 0)
    def _():
        grad_ref[...] = jnp.zeros_like(grad_ref)

    v = x_ref[...].astype(jnp.float32)
    rn = lax.rsqrt(jnp.mean(v * v, axis=-1, keepdims=True) + epsilon)
    d = d_ref[...]
    grad_ref[0:1, :] += sum_rows(d * v * rn)
    scaled = d * gain_ref[...]
    pull = rn * rn * rn * jnp.mean(v * scaled, axis=-1, keepdims=True)
    out_ref[...] = (cot_ref[...].astype(jnp.float32) + rn * scaled - v * pull).astype(out_ref.dtype)


def run_norm_back(d, x, cot, gain):
    rows, width = x.shape
    block = pl.BlockSpec((Q, width), lambda g: (g, 0))
    return pl.pallas_call(
        norm_back_kernel,
        grid=(rows // Q,),
        in_specs=[block, block, block, whole((1, width))],
        out_specs=[block, whole((8, width))],
        out_shape=[shaped(x.shape, x.dtype), shaped((8, width), jnp.float32)],
        compiler_params=params(),
        cost_estimate=cost(3000, 3000),
    )(d, x, cot, gain)


SMALL = 16
CALLS = ((0, 4), (4, 2))


def partners(bit):
    return [(i, i ^ bit) for i in range(8)]


def rotated(step):
    return [(i, (i + step) % 4) for i in range(4)]


def tie(*values):
    return lax.optimization_barrier(values)


def custom():
    return lax.axis_size("fsdp") == 8 and lax.axis_size("rep") == 4


def gathered_rows(w, late=False):
    half = w.shape[0] // 32 * 16
    two, four = yield [(w, "fsdp", partners(j)) for j in (2, 4)], 1
    sent = [(two[:half], "fsdp", partners(4)), (four[half:], "fsdp", partners(2))]
    if late:
        top, bottom, one, three = yield sent + [(v, "fsdp", partners(1)) for v in (w, two)], 1
        five, other_top, other_bottom = yield [(v, "fsdp", partners(1)) for v in (four, top, bottom)], 1
    else:
        top, bottom, one, three, five = yield sent + [(v, "fsdp", partners(1)) for v in (w, two, four)], 1
        other_top, other_bottom = yield [(v, "fsdp", partners(1)) for v in (top, bottom)], 1
    near = [(w, 0, 0), (one, 1, 0), (two, 2, 0), (three, 3, 0), (four, 4, 0), (five, 5, 0)]
    return near + [(top, 6, 0), (bottom, 6, half), (other_top, 7, 0), (other_bottom, 7, half)]


def dealt(v, turns):
    (got,) = yield [(v, "fsdp", None)], turns
    return got


def widen(v):
    return v.astype(jnp.float32)


def group_sum(left, right):
    half = left.shape[0] // 2
    odd = jnp.dot(left[:half], right, preferred_element_type=jnp.float32).astype(jnp.bfloat16)
    (got,) = yield [(odd, "fsdp", partners(1))], 1
    *terms, own = run_terms(left, right, got)
    others = yield [(v, "fsdp", partners(j)) for v, j in zip(terms, ORDER[4:7])], 1
    return own + widen(others[0]) + widen(others[1]) + widen(others[2])


def relayed_sum(left, right):
    b16 = jnp.bfloat16
    rows = left.shape[1] // 8
    half = rows // 2

    def product(start, stop):
        return contract_rows(left[:, start * rows : stop * rows], right)

    (got,) = yield [(product(0, 4).astype(b16), "fsdp", partners(1))], 1
    far = (product(4, 5) + widen(got[:rows])).astype(b16)
    from_x, from_y = yield [(far[:half], "fsdp", partners(2)), (far[half:], "fsdp", partners(4))], 1
    low = jnp.pad(widen(from_y), ((half, 0), (0, 0)))
    high = jnp.pad(widen(from_x), ((0, half), (0, 0)))
    to_x = (product(5, 6) + widen(got[rows : 2 * rows]) + low).astype(b16)
    to_y = (product(6, 7) + widen(got[2 * rows : 3 * rows]) + high).astype(b16)
    got_x, got_y = yield [(to_x, "fsdp", partners(2)), (to_y, "fsdp", partners(4))], 1
    return product(7, 8) + widen(got[3 * rows :]) + widen(got_x) + widen(got_y)


def out_sum(left, right):
    own = yield from relayed_sum(left, right)
    return (yield from half_sum(own))


def half_sum(own):
    b16 = jnp.bfloat16
    place = lax.axis_index("rep")
    odd, late = place % 2 == 1, place >= 2
    across = [(0, 2), (1, 3), (2, 0), (3, 1)]
    beside = [(0, 1), (1, 0), (2, 3), (3, 2)]

    def halves(v, second):
        top, bottom = jnp.split(v, 2)
        return jnp.where(second, bottom, top), jnp.where(second, top, bottom)

    def joined(mine, other, second):
        return jnp.where(second, jnp.concatenate([other, mine]), jnp.concatenate([mine, other]))

    keep, send = halves(own, odd)
    (got,) = yield [(send.astype(b16), "rep", beside)], 1
    keep, send = halves(widen(keep) + widen(got), late)
    (got,) = yield [(send.astype(b16), "rep", across)], 1
    mine = (keep + widen(got)).astype(b16)
    (got,) = yield [(mine, "rep", across)], 1
    mine = joined(mine, got, late)
    (got,) = yield [(mine, "rep", beside)], 1
    return joined(mine, got, odd)


def small_sum(rows):
    me, place = lax.axis_index("fsdp"), lax.axis_index("rep")
    rows = rows[me ^ jnp.array(ORDER, jnp.int32)]
    (got,) = yield [(rows[:4], "fsdp", partners(1))], 1
    rows = rows[4:] + got
    others = yield [(rows[i : i + 1], "fsdp", partners(j)) for i, j in enumerate(ORDER[4:7])], 1
    row = rows[3:] + others[0] + others[1] + others[2]
    got = yield [(row, "rep", rotated(k)) for k in (1, 2, 3)], 1
    stack = jnp.concatenate([row, *got])
    return jnp.sum(stack[(place - jnp.arange(4)) % 4], axis=0)


def transfer(v, axis, pairs):
    if pairs is None:
        return lax.all_to_all(v, axis, split_axis=0, concat_axis=0, tiled=True)
    return lax.ppermute(v, axis, pairs)


def slice_sum(left, right):
    own = yield from group_sum(left, right)
    return (yield from half_sum(own))


class Moves:
    def __init__(self):
        self.active = []

    def add(self, generator):
        want, turns = next(generator)
        entry = {"gen": generator, "want": want, "turns": turns, "got": None, "value": None}
        self.active.append(entry)
        return entry

    def turn(self, work=None, *values):
        fresh = [e for e in self.active if e["got"] is None]
        arrays, values = tie([[item[0] for item in e["want"]] for e in fresh], values)
        for e, some in zip(fresh, arrays):
            e["got"] = [None] * len(some)
        alike = {}
        for e, some in zip(fresh, arrays):
            for i, (v, item) in enumerate(zip(some, e["want"])):
                kind = (item[1], str(item[2]), v.shape[0], v.dtype.name) if item[1] == "rep" else (id(e), i)
                alike.setdefault(kind, []).append((e, i, v, item))
        for group in alike.values():
            moved = transfer(jnp.concatenate([g[2] for g in group], axis=1) if len(group) > 1 else group[0][2], *group[0][3][1:])
            start = 0
            for e, i, v, _ in group:
                e["got"][i] = moved[:, start : start + v.shape[1]] if len(group) > 1 else moved
                start += v.shape[1]
        results = work(*values) if work else ()
        for e in self.active:
            e["turns"] -= 1
        due = [e for e in self.active if e["turns"] == 0]
        arrived, results = tie([e["got"] for e in due], results)
        for e, got in zip(due, arrived):
            try:
                e["want"], e["turns"] = e["gen"].send(got)
                e["got"] = None
            except StopIteration as stop:
                e["value"] = stop.value
                self.active.remove(e)
        return results

    def after(self, value):
        want = self.active[0]["want"]
        array, *rest = want[-1]
        value, array = tie(value, array)
        want[-1] = (array, *rest)
        return value

    def finish(self):
        while self.active:
            self.turn()


def per_device(tokens, cotangent, lengths, dealing, norm_gain, in_weight, conv_weight, conv_bias, dt_bias, a_log, d_skip, gated_gain, out_weight):
    f32, b16 = jnp.float32, jnp.bfloat16
    groups = lax.axis_size("fsdp")
    tok_rows, width = tokens.shape
    block_rows = tok_rows // groups
    targets = dealing.reshape(groups)
    inverse = jnp.argsort(targets)
    first = lengths.reshape(-1)[:1]
    me = lax.axis_index("fsdp").reshape(1)
    moves = Moves()

    def blocks(values):
        return values.reshape(groups, block_rows, width)[inverse]

    def deal(values):
        return lax.all_to_all(blocks(values), "fsdp", split_axis=0, concat_axis=0, tiled=True).reshape(tok_rows, width)

    def undeal(values):
        blocks = lax.all_to_all(values.reshape(groups, block_rows, width), "fsdp", split_axis=0, concat_axis=0, tiled=True)
        return blocks[targets].reshape(tok_rows, width)

    own_small = [norm_gain, conv_weight, conv_bias, dt_bias, a_log, d_skip, gated_gain]

    def rows_of(values):
        values = [v if v.ndim == 2 else v[None] for v in values]
        longest = max(v.shape[1] for v in values)
        packed = jnp.concatenate([pad_lanes(v, longest) for v in values])
        return jnp.pad(packed, ((0, SMALL - packed.shape[0]), (0, 0)))

    def doubled(v, bit):
        return (jnp.concatenate([v, lax.ppermute(v, "fsdp", partners(bit))]),)

    if custom():
        rows, span = in_weight.shape[0], DI + BCD
        w_xb = lax.pad(in_weight, jnp.zeros((), b16), ((0, 0, 0), (-DI, span + DI - in_weight.shape[1], 0)))
        e_xb = moves.add(gathered_rows(w_xb, True))
        e_x = moves.add(dealt(blocks(tokens), 2))
        (small,) = moves.turn(lambda *v: doubled(rows_of(v), 2), *own_small)
        small, cot_blocks = moves.turn(lambda v, c: (*doubled(v, 4), blocks(c)), small, cotangent)
        out_weight = moves.after(out_weight)
        w_out = lax.all_gather(out_weight, "fsdp", axis=0, tiled=True)
        (small,) = moves.turn(lambda v: doubled(v, 1), small)
        pieces = e_xb["value"]
        x = e_x["value"].reshape(tok_rows, width)
        widths = (norm_gain.size, conv_bias.size, dt_bias.size, gated_gain.size)
    else:
        x = deal(tokens)
        w_z = lax.all_gather(in_weight[:, :DI], "fsdp", axis=0, tiled=True)
        w_out = lax.all_gather(out_weight, "fsdp", axis=0, tiled=True)
        small_all = lax.all_gather(rows_of(own_small), "fsdp", axis=0, tiled=False).astype(f32)
        w_xb = lax.all_gather(pad_lanes(in_weight[:, DI:], DI + BCD), "fsdp", axis=0, tiled=True)
        parts, row = [], 0
        for v in (u if u.ndim == 2 else u[None] for u in own_small):
            parts.append(small_all[:, row : row + v.shape[0], : v.shape[1]].transpose(1, 0, 2).reshape(v.shape[0], -1))
            row += v.shape[0]
        gain, taps, bias, step_bias, rate, skip, ggain = parts
        conv = jnp.concatenate([taps, bias, jnp.zeros((3, bias.shape[1]), f32)])
        heads = pad_lanes(jnp.concatenate([step_bias, rate, jnp.zeros((6, HEADS), f32)]), 128)
        gains = jnp.concatenate([jnp.repeat(skip, HEAD_DIM, axis=1), ggain, jnp.zeros((6, DI), f32)])
    if custom():

        def open_up(x):
            gain, conv, heads, gains, normed, sent, bcd, w_b, *prep = run_open(me, first, x, small, pieces, widths, DI)
            return gain, conv, heads, gains, normed, sent, bcd, w_b, prep, *run_project(me, normed, pieces, 0, DI)

        e_z = moves.add(gathered_rows(in_weight[:, :DI]))
        gain, conv, heads, gains, normed, sent, bcd, w_b, prep, xr, w_x = moves.turn(open_up, x)
        conv_x, conv_bc = conv[:, :DI], conv[:, DI:]
        ssm, states = moves.turn(lambda v: run_forward(first, v, conv_x, gains, prep), xr)
        moves.turn()
        e_cot = moves.add(dealt(cot_blocks, 1))

        def close_up(ssm):
            z, full = run_project(me, normed, e_z["value"], 0, DI)
            return z, full, *run_gated(ORDER, me, z, ssm, gains)

        z, w_z, gated, gated_sent, r = moves.turn(close_up, ssm)
        cot = e_cot["value"].reshape(tok_rows, width)
        e_rows = moves.add(out_sum(gated_sent, cot))
        result, rk = moves.turn(lambda v: run_out(v, w_out, x, cot, r), gated)
    else:
        conv_x, conv_bc = conv[:, :DI], conv[:, DI:]
        normed, sent = run_norm((0,), me * 0, x, gain)
        w_x, w_b = w_xb[:, :DI], w_xb[:, DI:]
        bcd = jnp.dot(normed, w_b, preferred_element_type=f32)
        xr = jnp.dot(normed, w_x, preferred_element_type=f32)
        cot = deal(cotangent)
        prep = run_prep(first, bcd, conv_bc, heads)
        ssm, states = run_forward(first, xr, conv_x, gains, prep)
        z = jnp.dot(normed, w_z, preferred_element_type=f32)
        gated, _, r = run_gated(tuple(range(8)), me * 0, z, ssm, gains)
        result, rk = run_out(gated, w_out, x, cot, r)
        s_out = lax.psum_scatter(contract_rows(gated, cot, b16), "fsdp", scatter_dimension=0, tiled=True)

    def gate(rk):
        return run_gate(z, ssm, cot, w_out, rk, gains)

    def backward(base, count, ds):
        return run_backward(base, count, first, xr, ssm, ds, conv_x, gains, prep, states)

    def close(backs):
        return run_post(first, bcd, conv_bc, heads, prep, [b[2:] for b in backs])

    def back(backs, d_b):
        pairs = [(dz, 0, w_z, 0, DI)] + [(b[0], 0, w_x, base * LANES, count * LANES) for b, (base, count) in zip(backs, CALLS)]
        return run_back(pairs + [(d_b, 0, w_b, 0, BCD)])

    if custom():
        dz, ds, ggrads = moves.turn(gate, rk)

        def first_back(dz, ds):
            z_term, ds = tie(contract_rows(normed, dz, b16), ds)
            held.append(lax.psum_scatter(z_term, "fsdp", scatter_dimension=0, tiled=True))
            return backward(*CALLS[0], ds)

        held = []
        backs = [moves.turn(first_back, dz, ds)]
        (s_z,) = held
        e_first = moves.add(slice_sum(sent, backs[0][0]))

        def middle(ds):
            both = backs + [backward(*CALLS[1], ds)]
            return both[1], *close(both)

        last, d_b, bgrads, hgrads = moves.turn(middle, ds)
        backs.append(last)
        s_z, d_b = tie(s_z, d_b)
        e_last = moves.add(slice_sum(sent, jnp.concatenate([last[0], d_b], axis=1)))
        e_z = moves.add(half_sum(s_z))
        (d_normed,) = moves.turn(lambda d: (back(backs, d),), d_b)

        def finish(d_normed):
            d_input, ngrads = run_norm_back(d_normed, x, cot, gain)
            return d_input, run_pack(widths, [b[1] for b in backs], bgrads, hgrads, ggrads, ngrads)

        d_input, packed = moves.turn(finish, d_normed)
    else:
        dz, ds, ggrads = gate(rk)
        s_z = lax.psum_scatter(contract_rows(normed, dz, b16), "fsdp", scatter_dimension=0, tiled=True)
        backs = [backward(*call, ds) for call in CALLS]
        d_b, bgrads, hgrads = close(backs)
        d_normed = back(backs, d_b)
        d_input, ngrads = run_norm_back(d_normed, x, cot, gain)
        s_in = [lax.psum_scatter(contract_rows(normed, d, b16), "fsdp", scatter_dimension=0, tiled=True) for d in [b[0] for b in backs] + [d_b]]
        output, input_grad = undeal(result), undeal(d_input)

    if not custom():
        xgrads = jnp.concatenate([b[1] for b in backs], axis=1)
        g_ggain = ggrads[0]
        g_conv = jnp.concatenate([xgrads[:KW], bgrads[:KW]], axis=1)
        g_cbias = jnp.concatenate([xgrads[KW], bgrads[KW]])
        g_dskip = jnp.sum(xgrads[5].reshape(HEADS, HEAD_DIM), axis=1)
        spread = [
            ngrads[0].reshape(groups, -1),
            g_conv.reshape(KW, groups, -1).transpose(1, 0, 2).reshape(groups, -1),
            g_cbias.reshape(groups, -1),
            hgrads[0, :HEADS].reshape(groups, -1),
            hgrads[1, :HEADS].reshape(groups, -1),
            g_dskip.reshape(groups, -1),
            g_ggain.reshape(groups, -1),
        ]
        packed = jnp.concatenate(spread, axis=1)
        packed = pad_lanes(packed, packed.shape[1] + -packed.shape[1] % 128)
    sizes = [v.size for v in own_small]
    tail = in_weight.shape[1] - 2 * DI

    def cut(row):
        ends, outs = 0, []
        for size in sizes:
            outs.append(row[ends : ends + size])
            ends += size
        return outs

    if custom():
        e_small = moves.add(small_sum(packed))
        e_input = moves.add(dealt(d_input.reshape(groups, block_rows, width), 1))
        moves.turn()
        e_output = moves.add(dealt(result.reshape(groups, block_rows, width), 1))
        moves.turn()

        def restored(entry):
            return entry["value"][targets].reshape(tok_rows, width)

        input_grad, r_out = moves.turn(lambda: (restored(e_input), widen(e_rows["value"])))
        (output,) = moves.turn(lambda: (restored(e_output),))
        last = CALLS[-1][1] * LANES + tail

        def gather_up():
            known = jnp.concatenate([e_z["value"], e_first["value"], jnp.zeros((rows, last), b16)], axis=1)
            return widen(known), *cut(e_small["value"])

        r_in, *outs = moves.turn(gather_up)
        moves.finish()
        r_in = lax.dynamic_update_slice(r_in, widen(e_last["value"][:, :last]), (0, r_in.shape[1] - last))
    else:
        s_small = jnp.sum(lax.all_to_all(packed, "fsdp", split_axis=0, concat_axis=0, tiled=True), axis=0)
        r_small = jnp.sum(lax.all_gather(s_small, "rep", axis=0, tiled=False), axis=0)
        *r_in, r_out = lax.psum((s_z, *s_in, s_out), "rep")
        r_in = jnp.concatenate(r_in, axis=1)[:, : in_weight.shape[1]]
        outs = cut(r_small)
    return (output, input_grad, outs[0], r_in.astype(f32), outs[1].reshape(conv_weight.shape), outs[2], outs[3], outs[4], outs[5], outs[6], r_out.astype(f32))


def solution(mesh):
    placed = (
        P(("rep", "fsdp"), None),
        P(("rep", "fsdp"), None),
        P("rep", "fsdp", None),
        P("rep", "fsdp", None),
        P("fsdp"),
        P("fsdp", None),
        P(None, "fsdp"),
        P("fsdp"),
        P("fsdp"),
        P("fsdp"),
        P("fsdp"),
        P("fsdp"),
        P("fsdp", None),
    )
    return jax.shard_map(
        per_device,
        mesh=mesh,
        in_specs=placed,
        out_specs=(
            P(("rep", "fsdp"), None),
            P(("rep", "fsdp"), None),
            P("fsdp"),
            P("fsdp", None),
            P(None, "fsdp"),
            P("fsdp"),
            P("fsdp"),
            P("fsdp"),
            P("fsdp"),
            P("fsdp"),
            P("fsdp", None),
        ),
        check_vma=False,
    )
```

```python
import functools

import jax
import jax.numpy as jnp
from jax import lax
from jax.experimental import pallas as pl
from jax.experimental.pallas import tpu as pltpu
from jax.sharding import PartitionSpec as P

DI = 3072
HEAD_DIM = 64
NSTATE = 128
KW = 4
HEADS = 48
BCD = 384

epsilon = 1e-05


Q = 128
GROUP = 8
LANES = GROUP * HEAD_DIM
NEG = -1e30
VMEM = 56 * 1024 * 1024


def dot32(a, b, dims=(((1,), (0,)), ((), ())), precision=None):
    return lax.dot_general(a, b, dims, preferred_element_type=jnp.float32, precision=precision)


NT = (((1,), (1,)), ((), ()))


def row_ids(start, rows, cols):
    return lax.broadcasted_iota(jnp.int32, (rows, cols), 0) + start


def shifted_down(ref, cols, c, first, width):
    if c == 0:
        tall = jnp.concatenate([jnp.zeros((8, width), jnp.float32), ref[0:Q, cols]], axis=0)
    else:
        tall = ref[c * Q - 8 : c * Q + Q, cols]
    place = row_ids(c * Q, Q, width)
    outs = [tall[8:]]
    for j in range(1, KW):
        moved = pltpu.roll(tall, j, 0)[8:]
        keep = (place >= j) & ((place < first) | (place >= first + j))
        outs.append(jnp.where(keep, moved, 0.0))
    return outs


def conv_back(ref, cols, c, first, width, taps):
    tall = ref[c * Q : c * Q + Q + 8, cols]
    place = row_ids(c * Q, Q, width)
    total = taps[KW - 1] * tall[:Q]
    for j in range(1, KW):
        moved = pltpu.roll(tall, Q + 8 - j, 0)[:Q]
        keep = (place < first - j) | (place >= first)
        total = total + taps[KW - 1 - j] * jnp.where(keep, moved, 0.0)
    return total


def sigmoid(v):
    return 0.5 * jnp.tanh(0.5 * v) + 0.5


def sum_rows(v):
    return jnp.sum(v, axis=0, keepdims=True)


def prep_kernel(first_ref, bcd_ref, conv_ref, head_ref, wide_ref, tall_ref, bc_ref, bct_ref):
    first = first_ref[0]
    tri = (row_ids(0, Q, Q) >= lax.broadcasted_iota(jnp.int32, (Q, Q), 1)).astype(jnp.float32)
    rate = -jnp.exp(head_ref[1:2, :])
    lane = lax.broadcasted_iota(jnp.int32, (Q, 128), 1)
    for c in range(bcd_ref.shape[0] // Q):
        rows = slice(c * Q, c * Q + Q)
        moved = shifted_down(bcd_ref, slice(0, 2 * NSTATE), c, first, 2 * NSTATE)
        mixed = conv_ref[4:5, :] + conv_ref[3:4, :] * moved[0]
        for j in range(1, KW):
            mixed = mixed + conv_ref[KW - 1 - j : KW - j, :] * moved[j]
        act = mixed * sigmoid(mixed)
        b32, c32 = act[:, :NSTATE], act[:, NSTATE:]
        b16, c16 = b32.astype(jnp.bfloat16), c32.astype(jnp.bfloat16)
        bc_ref[rows, :] = act.astype(jnp.bfloat16)
        bct_ref[:NSTATE, rows] = b32.T.astype(jnp.bfloat16)
        bct_ref[NSTATE:, rows] = c32.T.astype(jnp.bfloat16)
        wide_ref[rows, :Q] = dot32(c16, b16, NT)
        wide_ref[rows, Q : 2 * Q] = dot32(b16, c16, NT)
        raw = jnp.where(lane < HEADS, bcd_ref[rows, 2 * NSTATE :] + head_ref[0:1, :], 0.0)
        step = jax.nn.softplus(raw)
        cum = dot32(tri, rate * step, precision=lax.Precision.HIGHEST)
        cp = cum - jnp.log(jnp.maximum(step, 1e-37))
        wide_ref[rows, 2 * Q : 3 * Q] = cum
        wide_ref[rows, 3 * Q :] = cp
        tall_ref[:128, rows] = cum.T
        tall_ref[128:, rows] = cp.T


def chunk_masks(first, c, transposed):
    base = c * Q
    row = row_ids(base, Q, Q)
    col = lax.broadcasted_iota(jnp.int32, (Q, Q), 1) + base
    ordered = (col >= row) if transposed else (row >= col)
    inside = ordered & ((row >= first) == (col >= first))
    carry = ((row >= first) == (base - 1 >= first)) & (base > 0)
    last = (row >= first) == (base + Q - 1 >= first)
    through = (base > 0) & ((base + Q - 1 >= first) == (base - 1 >= first))
    return inside, carry, last, through


def lane_column(values, k):
    return jnp.broadcast_to(values[:, k : k + 1], (Q, Q))


def conv_act(x_ref, conv_ref, cols, c, first):
    moved = shifted_down(x_ref, cols, c, first, Q)
    mixed = conv_ref[4:5, cols] + conv_ref[3:4, cols] * moved[0]
    for j in range(1, KW):
        mixed = mixed + conv_ref[KW - 1 - j : KW - j, cols] * moved[j]
    return moved, mixed


def both_heads(left, right, half):
    none = jnp.zeros_like(right)
    stacked = jnp.concatenate([jnp.where(half, right, none), jnp.where(half, none, right)], axis=0)
    return dot32(jnp.concatenate(left, axis=1), stacked)


def forward_kernel(first_ref, x_ref, conv_ref, gain_ref, wide_ref, tall_ref, bc_ref, bct_ref, ssm_ref, states_ref, state):
    first = first_ref[0]
    group = pl.program_id(0)
    half = lax.broadcasted_iota(jnp.int32, (Q, Q), 1) < HEAD_DIM
    state[...] = jnp.zeros_like(state)
    shift = (Q - GROUP * group) % Q
    pairs = range(GROUP // 2)
    for c in range(x_ref.shape[0] // Q):
        rows = slice(c * Q, c * Q + Q)
        inside, carry, last, through = chunk_masks(first, c, False)
        cum = pltpu.roll(wide_ref[rows, 2 * Q : 3 * Q], shift, 1)
        cp = pltpu.roll(wide_ref[rows, 3 * Q :], shift, 1)
        cpt = tall_ref[pl.ds(pl.multiple_of(128 + group * GROUP, GROUP), GROUP), rows]
        scores = wide_ref[rows, :Q]
        old16 = state[...].astype(jnp.bfloat16)
        states_ref[c * NSTATE : (c + 1) * NSTATE, :] = old16
        if c > 0:
            carried = dot32(bc_ref[rows, NSTATE:], old16)
        weighted, ends = [], []
        for p in pairs:
            cols = slice(p * Q, p * Q + Q)
            _, mixed = conv_act(x_ref, conv_ref, cols, c, first)
            xs = mixed * sigmoid(mixed)
            mixing, cums, cps = [], [], []
            for k in (2 * p, 2 * p + 1):
                cum_b = lane_column(cum, k)
                decay = jnp.exp(jnp.where(inside, cum_b - cpt[k : k + 1, :], NEG))
                mixing.append((scores * decay).astype(jnp.bfloat16))
                cums.append(cum_b)
                cps.append(lane_column(cp, k))
            cum_pair = jnp.where(half, cums[0], cums[1])
            cp_pair = jnp.where(half, cps[0], cps[1])
            y = both_heads(mixing, xs.astype(jnp.bfloat16), half)
            if c > 0:
                y = y + jnp.where(carry, jnp.exp(cum_pair), 0.0) * carried[:, cols]
            ssm_ref[rows, cols] = y + gain_ref[0:1, cols] * xs
            end = cum_pair[Q - 1 : Q, :]
            weighted.append((jnp.where(last, jnp.exp(end - cp_pair), 0.0) * xs).astype(jnp.bfloat16))
            ends.append(end)
        fresh = dot32(bct_ref[:NSTATE, rows], jnp.concatenate(weighted, axis=1))
        for p in pairs:
            cols = slice(p * Q, p * Q + Q)
            kept = 0.0 if c == 0 else jnp.where(through, jnp.exp(ends[p]), 0.0) * state[:, cols]
            state[:, cols] = kept + fresh[:, cols]


def gated_kernel(order, me_ref, z_ref, ssm_ref, gain_ref, gated_ref, sent_ref, r_ref):
    squares = jnp.zeros((Q, Q), jnp.float32)
    for p in range(z_ref.shape[1] // Q):
        cols = slice(p * Q, p * Q + Q)
        zv = z_ref[:, cols]
        g = ssm_ref[:, cols] * (zv * sigmoid(zv))
        squares = squares + g * g
    r = lax.rsqrt(jnp.sum(squares, axis=-1, keepdims=True) / DI + epsilon)
    wide = jnp.broadcast_to(r, (Q, Q))
    r_ref[...] = wide
    for p in range(z_ref.shape[1] // Q):
        cols = slice(p * Q, p * Q + Q)
        zv = z_ref[:, cols]
        g = ssm_ref[:, cols] * (zv * sigmoid(zv))
        gated_ref[:, cols] = (g * wide * gain_ref[1:2, cols]).astype(gated_ref.dtype)
    part = gated_ref.shape[1] // 8
    for i, j in enumerate(order):
        sent_ref[:, i * part : (i + 1) * part] = gated_ref[:, pl.ds(pl.multiple_of((me_ref[0] ^ j) * part, 128), part)]


def gate_kernel(z_ref, ssm_ref, cot_ref, weight_ref, rk_ref, gain_ref, dz_ref, ds_ref, grads_ref, d_gated):
    d_gated[...] = dot32(cot_ref[...], weight_ref[...], NT)
    grads_ref[...] = jnp.zeros_like(grads_ref)
    for c in range(z_ref.shape[0] // Q):
        rows = slice(c * Q, c * Q + Q)
        scale = lane_column(rk_ref[rows, :], 0)
        pull = lane_column(rk_ref[rows, :], 1)
        for p in range(z_ref.shape[1] // Q):
            cols = slice(p * Q, p * Q + Q)
            zv = z_ref[rows, cols]
            sz = sigmoid(zv)
            silu_z = zv * sz
            ssm = ssm_ref[rows, cols]
            g = ssm * silu_z
            gs = d_gated[rows, cols] * scale
            grads_ref[0:1, cols] += sum_rows(gs * g)
            d_g = gain_ref[1:2, cols] * gs - g * pull
            dz_ref[rows, cols] = (d_g * ssm * (sz + silu_z * (1.0 - sz))).astype(dz_ref.dtype)
            ds_ref[rows, cols] = (d_g * silu_z).astype(ds_ref.dtype)


def eight_rows(v):
    return functools.reduce(jnp.add, [v[i : i + 8, :] for i in range(0, v.shape[0], 8)])


def backward_kernel(base, first_ref, x_ref, ssm_ref, ds_ref, conv_ref, gain_ref, wide_ref, tall_ref, bc_ref, bct_ref, states_ref, d_ref, grads_ref, sums_ref, flow_ref, dstate, dconv, acc):
    first = first_ref[0]
    group = base + pl.program_id(0)
    half = lax.broadcasted_iota(jnp.int32, (Q, Q), 1) < HEAD_DIM
    dstate[...] = jnp.zeros_like(dstate)
    acc[...] = jnp.zeros_like(acc)
    rows_all = x_ref.shape[0]
    dconv[rows_all : rows_all + 8, :] = jnp.zeros((8, dconv.shape[1]), jnp.float32)
    flow_ref[...] = jnp.zeros_like(flow_ref)

    @pl.when(pl.program_id(0) == 0)
    def _():
        sums_ref[...] = jnp.zeros_like(sums_ref)

    shift = (Q - GROUP * group) % Q
    chunks = rows_all // Q
    pairs = range(GROUP // 2)
    pick = (lax.broadcasted_iota(jnp.int32, (LANES, Q), 1) == GROUP * group + row_ids(0, LANES, Q) // HEAD_DIM).astype(jnp.bfloat16)
    for c in range(chunks - 1, -1, -1):
        rows = slice(c * Q, c * Q + Q)
        inside, carry, last, through = chunk_masks(first, c, True)
        cum = pltpu.roll(wide_ref[rows, 2 * Q : 3 * Q], shift, 1)
        cp = pltpu.roll(wide_ref[rows, 3 * Q :], shift, 1)
        cumt = tall_ref[pl.ds(pl.multiple_of(group * GROUP, GROUP), GROUP), rows]
        scores_t = wide_ref[rows, Q : 2 * Q]
        b16, c16t = bc_ref[rows, :NSTATE], bct_ref[NSTATE:, rows]
        dst = jnp.zeros((Q, Q), jnp.float32)
        if c < chunks - 1:
            later16 = dstate[...].astype(jnp.bfloat16)
            carried = dot32(b16, later16)
        high, low, local, weighted, carries, eys, ends = ([] for _ in range(7))
        for p in pairs:
            cols = slice(p * Q, p * Q + Q)
            moved, mixed = conv_act(x_ref, conv_ref, cols, c, first)
            sx = sigmoid(mixed)
            xs = mixed * sx
            x16 = xs.astype(jnp.bfloat16)
            skip = gain_ref[0:1, cols]
            dy16 = ds_ref[rows, cols]
            d_ssm = dy16.astype(jnp.float32)
            acc[40:48, cols] += eight_rows(d_ssm * xs)
            mixing, cums, cps = [], [], []
            for k in (2 * p, 2 * p + 1):
                cp_b = lane_column(cp, k)
                decay = jnp.exp(jnp.where(inside, cumt[k : k + 1, :] - cp_b, NEG))
                mixing.append((scores_t * decay).astype(jnp.bfloat16))
                x_half = jnp.where(half == (k == 2 * p), x16, jnp.zeros_like(x16))
                dst = dst + decay * dot32(x_half, dy16, NT)
                cums.append(lane_column(cum, k))
                cps.append(cp_b)
            cum_pair = jnp.where(half, cums[0], cums[1])
            cp_pair = jnp.where(half, cps[0], cps[1])
            dx = both_heads(mixing, dy16, half)
            in_dot = x16.astype(jnp.float32) * dx
            u = d_ssm * (ssm_ref[rows, cols] - skip * xs) - in_dot
            high.append(u.astype(jnp.bfloat16))
            low.append((u - high[-1].astype(jnp.float32)).astype(jnp.bfloat16))
            local.append(in_dot.astype(jnp.bfloat16))
            end = cum_pair[Q - 1 : Q, :]
            ends.append(end)
            if c < chunks - 1:
                weight = jnp.where(last, jnp.exp(end - cp_pair), 0.0)
                moved_in = weight * carried[:, cols]
                dx = dx + moved_in
                carries.append((xs * moved_in).astype(jnp.bfloat16))
                weighted.append((weight * xs).astype(jnp.bfloat16))
            if c > 0:
                eys.append((jnp.where(carry, jnp.exp(cum_pair), 0.0) * d_ssm).astype(jnp.bfloat16))
            d_mixed = (dx + skip * d_ssm) * (sx + xs * (1.0 - sx))
            dconv[rows, cols] = d_mixed
            acc[32:40, cols] += eight_rows(d_mixed)
            for j in range(KW):
                acc[8 * (KW - 1 - j) : 8 * (KW - j), cols] += eight_rows(d_mixed * moved[j])
            taps = [conv_ref[i : i + 1, cols] for i in range(KW)]
            d_ref[rows, cols] = conv_back(dconv, cols, c, first, Q, taps).astype(d_ref.dtype)
        join = functools.partial(jnp.concatenate, axis=1)
        sums_ref[rows, :Q] += dst
        sums_ref[rows, 3 * Q : 4 * Q] += dot32(join(high), pick) + dot32(join(low), pick)
        sums_ref[rows, 4 * Q : 5 * Q] += dot32(join(local), pick)
        if c < chunks - 1:
            sums_ref[rows, Q : 2 * Q] += dot32(join(weighted), later16, NT)
            sums_ref[rows, 5 * Q :] += dot32(join(carries), pick)
        if c > 0:
            ey16 = join(eys)
            old16 = states_ref[c * NSTATE : (c + 1) * NSTATE, :]
            sums_ref[rows, 2 * Q : 3 * Q] += dot32(ey16, old16, NT)
            fresh = dot32(c16t, ey16)
            for p in pairs:
                cols = slice(p * Q, p * Q + Q)
                if c < chunks - 1:
                    kept = jnp.where(through, jnp.exp(ends[p]), 0.0) * dstate[:, cols]
                    flow_ref[c : c + 1, cols] = sum_rows(kept * old16[:, cols].astype(jnp.float32))
                    dstate[:, cols] = kept + fresh[:, cols]
                else:
                    dstate[:, cols] = fresh[:, cols]
    for i in range(8):
        grads_ref[i : i + 1, :] = sum_rows(acc[8 * i : 8 * i + 8, :]) if i < 6 else jnp.zeros((1, LANES), jnp.float32)


def post_kernel(calls, first_ref, bcd_ref, conv_ref, head_ref, bc_ref, *refs):
    sums_refs, flow_refs, (d_ref, grads_ref, hgrads_ref, dconv) = refs[:calls], refs[calls:-4], refs[-4:]
    first = first_ref[0]
    rows_all = bcd_ref.shape[0]
    wide = 2 * NSTATE
    dconv[rows_all : rows_all + 8, :] = jnp.zeros((8, wide), jnp.float32)
    grads_ref[...] = jnp.zeros_like(grads_ref)
    hgrads_ref[...] = jnp.zeros_like(hgrads_ref)
    lane = lax.broadcasted_iota(jnp.int32, (Q, 128), 1)
    rate = -jnp.exp(head_ref[1:2, :])
    flow = jnp.zeros((8, 128), jnp.float32)
    start = 0
    for ref in flow_refs:
        width = ref.shape[1]
        spread = (row_ids(start, width, 128) // HEAD_DIM == lax.broadcasted_iota(jnp.int32, (width, 128), 1)).astype(jnp.float32)
        flow = flow + dot32(ref[...], spread, precision=lax.Precision.HIGHEST)
        start += width
    row, col = row_ids(0, Q, Q), lax.broadcasted_iota(jnp.int32, (Q, Q), 1)
    earlier_sum = (col < row).astype(jnp.float32)
    for c in range(rows_all // Q - 1, -1, -1):
        rows = slice(c * Q, c * Q + Q)
        moved = shifted_down(bcd_ref, slice(0, wide), c, first, wide)
        mixed = conv_ref[4:5, :] + conv_ref[3:4, :] * moved[0]
        for j in range(1, KW):
            mixed = mixed + conv_ref[KW - 1 - j : KW - j, :] * moved[j]
        sx = sigmoid(mixed)
        dst, db, dc, us, vs, carried = (functools.reduce(jnp.add, [ref[rows, i * Q : (i + 1) * Q] for ref in sums_refs]) for i in range(6))
        d_b = db + dot32(dst.astype(jnp.bfloat16), bc_ref[rows, NSTATE:])
        d_c = dc + dot32(dst.T.astype(jnp.bfloat16), bc_ref[rows, :NSTATE])
        d_mixed = jnp.concatenate([d_b, d_c], axis=1) * (sx + mixed * sx * (1.0 - sx))
        dconv[rows, :] = d_mixed
        grads_ref[4:5, :] += sum_rows(d_mixed)
        for j in range(KW):
            grads_ref[KW - 1 - j : KW - j, :] += sum_rows(d_mixed * moved[j])
        taps = [conv_ref[i : i + 1, :] for i in range(KW)]
        d_ref[rows, :wide] = conv_back(dconv, slice(0, wide), c, first, wide, taps).astype(d_ref.dtype)
        later_sum = ((col >= row) & ((row + c * Q >= first) == (col + c * Q >= first))).astype(jnp.float32)
        d_la = dot32(later_sum, us, precision=lax.Precision.HIGHEST)
        d_la = d_la + dot32(earlier_sum, carried, precision=lax.Precision.HIGHEST) + flow[c : c + 1, :]
        d_log = vs + carried
        raw = bcd_ref[rows, wide:] + head_ref[0:1, :]
        step = jax.nn.softplus(raw)
        sig = sigmoid(raw)
        ratio = jnp.where(raw < -17.0, 1.0, sig / jnp.maximum(step, 1e-37))
        d_raw = jnp.where(lane < HEADS, d_log * ratio + d_la * rate * sig, 0.0)
        d_ref[rows, wide:] = d_raw.astype(d_ref.dtype)
        hgrads_ref[0:1, :] += sum_rows(d_raw)
        hgrads_ref[1:2, :] += sum_rows(jnp.where(lane < HEADS, d_la * rate * step, 0.0))


def smem():
    return pl.BlockSpec(memory_space=pltpu.SMEM)


def whole(shape):
    return pl.BlockSpec(shape, lambda g: (0,) * len(shape))


def shaped(shape, kind):
    return jax.ShapeDtypeStruct(shape, kind)


def params(limit=VMEM):
    return pltpu.CompilerParams(vmem_limit_bytes=limit)


def cost(flops, size):
    return pl.CostEstimate(flops=flops // 3, bytes_accessed=size // 3, transcendentals=0)


def run_prep(first, bcd, conv, heads):
    rows = bcd.shape[0]
    f32, b16 = jnp.float32, jnp.bfloat16
    shapes = [((rows, 4 * Q), f32), ((256, rows), f32), ((rows, 2 * NSTATE), b16), ((2 * NSTATE, rows), b16)]
    return pl.pallas_call(
        prep_kernel,
        grid=(1,),
        in_specs=[smem(), whole((rows, BCD)), whole((8, 2 * NSTATE)), whole((8, 128))],
        out_specs=[whole(s) for s, _ in shapes],
        out_shape=[shaped(s, d) for s, d in shapes],
        compiler_params=params(),
        cost_estimate=cost(2000000000, 4000000),
    )(first, bcd, conv, heads)


def run_forward(first, x, conv, gains, prep):
    rows, width = x.shape
    chunks = rows // Q
    here = lambda g: (0, g)
    block, eight = pl.BlockSpec((rows, LANES), here), pl.BlockSpec((8, LANES), here)
    return pl.pallas_call(
        forward_kernel,
        grid=(width // LANES,),
        in_specs=[smem(), block, eight, eight] + [whole(v.shape) for v in prep],
        out_specs=[block, pl.BlockSpec((chunks * NSTATE, LANES), here)],
        out_shape=[shaped((rows, width), jnp.float32), shaped((chunks * NSTATE, width), jnp.bfloat16)],
        scratch_shapes=[pltpu.VMEM((NSTATE, LANES), jnp.float32)],
        compiler_params=params(),
        cost_estimate=cost(20000000000, 20000000),
    )(first, x, conv, gains, *prep)


def run_gated(order, me, z, ssm, gains):
    rows, width = z.shape
    b16 = jnp.bfloat16
    block = pl.BlockSpec((Q, width), lambda g: (g, 0))
    thin = pl.BlockSpec((Q, Q), lambda g: (g, 0))
    return pl.pallas_call(
        functools.partial(gated_kernel, order),
        grid=(rows // Q,),
        in_specs=[smem(), block, block, whole(gains.shape)],
        out_specs=[block, block, thin],
        out_shape=[shaped((rows, width), b16), shaped((rows, width), b16), shaped((rows, Q), jnp.float32)],
        compiler_params=params(),
        cost_estimate=cost(4000000000, 16000000),
    )(me, z, ssm, gains)


def run_gate(z, ssm, cot, weight, rk, gains):
    rows, width = cot.shape
    b16 = jnp.bfloat16
    here = lambda g: (0, g)
    block, eight = pl.BlockSpec((rows, LANES), here), pl.BlockSpec((8, LANES), here)
    return pl.pallas_call(
        gate_kernel,
        grid=(DI // LANES,),
        in_specs=[block, block, whole(cot.shape), pl.BlockSpec((LANES, width), lambda g: (g, 0)), whole(rk.shape), eight],
        out_specs=[block, block, eight],
        out_shape=[shaped((rows, DI), b16)] * 2 + [shaped((8, DI), jnp.float32)],
        scratch_shapes=[pltpu.VMEM((rows, LANES), jnp.float32)],
        compiler_params=params(),
        cost_estimate=cost(12000000000, 36000000),
    )(z, ssm, cot, weight, rk, gains)


def run_backward(base, count, first, x, ssm, ds, conv, gains, prep, states):
    rows = x.shape[0]
    f32, b16 = jnp.float32, jnp.bfloat16
    chunks = rows // Q
    at = lambda g: (0, g + base)
    here = lambda g: (0, g)
    block, eight = pl.BlockSpec((rows, LANES), at), pl.BlockSpec((8, LANES), at)
    own = pl.BlockSpec((8, LANES), here)
    return pl.pallas_call(
        functools.partial(backward_kernel, base),
        grid=(count,),
        in_specs=[smem(), block, block, block, eight, eight] + [whole(v.shape) for v in prep] + [pl.BlockSpec((chunks * NSTATE, LANES), at)],
        out_specs=[pl.BlockSpec((rows, LANES), here), own, whole((rows, 6 * Q)), own],
        out_shape=[shaped((rows, count * LANES), b16), shaped((8, count * LANES), f32), shaped((rows, 6 * Q), f32), shaped((8, count * LANES), f32)],
        scratch_shapes=[pltpu.VMEM((NSTATE, LANES), f32), pltpu.VMEM((rows + 8, LANES), f32), pltpu.VMEM((48, LANES), f32)],
        compiler_params=params(),
        cost_estimate=cost(count * 7000000000, count * 8000000),
    )(first, x, ssm, ds, conv, gains, *prep, states)


def run_post(first, bcd, conv, heads, prep, backs):
    rows = bcd.shape[0]
    bc = prep[2]
    f32 = jnp.float32
    sums = [t for some in zip(*backs) for t in some]
    return pl.pallas_call(
        functools.partial(post_kernel, len(backs)),
        grid=(1,),
        in_specs=[smem(), whole((rows, BCD)), whole((8, 2 * NSTATE)), whole((8, 128)), whole(bc.shape)] + [whole(t.shape) for t in sums],
        out_specs=[whole((rows, BCD)), whole((8, 2 * NSTATE)), whole((8, 128))],
        out_shape=[shaped((rows, BCD), jnp.bfloat16), shaped((8, 2 * NSTATE), f32), shaped((8, 128), f32)],
        scratch_shapes=[pltpu.VMEM((rows + 8, 2 * NSTATE), f32)],
        compiler_params=params(),
        cost_estimate=cost(4000000000, 8000000),
    )(first, bcd, conv, heads, bc, *sums)


def contract_rows(left, right, kind=jnp.float32):
    return lax.dot_general(left, right, (((0,), (0,)), ((), ())), preferred_element_type=kind)


def pad_lanes(v, width):
    return jnp.pad(v, ((0, 0), (0, width - v.shape[1])))


ORDER = (7, 3, 5, 1, 6, 2, 4, 0)
DOUBLED = (0, 2, 4, 6, 1, 3, 5, 7)
WIDE = 512


def project_kernel(places, me_ref, left_ref, *refs):
    pieces, (out_ref, full_ref) = refs[:-2], refs[-2:]
    part = full_ref.shape[0] // 8
    for (j, skip, rows), ref in zip(places, pieces):
        full_ref[pl.ds(pl.multiple_of((me_ref[0] ^ j) * part + skip, 16), rows), :] = ref[:rows, :]
    out_ref[...] = dot32(left_ref[...], full_ref[...])


def run_project(me, left, pieces, skip, cols):
    rows, inner = left.shape
    step = min(WIDE, cols)
    here = lambda g: (0, g)
    places = tuple((j, start, min(v.shape[0], inner // 8 - start)) for v, j, start in pieces)
    return pl.pallas_call(
        functools.partial(project_kernel, places),
        grid=(cols // step,),
        in_specs=[smem(), whole(left.shape)] + [pl.BlockSpec((v.shape[0], step), lambda g: (0, g + skip // step)) for v, _, _ in pieces],
        out_specs=[pl.BlockSpec((rows, step), here), pl.BlockSpec((inner, step), here)],
        out_shape=[shaped((rows, cols), jnp.float32), shaped((inner, cols), left.dtype)],
        compiler_params=params(),
        cost_estimate=cost(2 * rows * inner * cols, 4 * inner * (rows + cols) + 4 * rows * cols),
    )(me, left, *[v for v, _, _ in pieces])


def unpack_kernel(widths, me_ref, small_ref, gain_ref, conv_ref, heads_ref, gains_ref, found):
    for k, j in enumerate(DOUBLED):
        found[me_ref[0] ^ j] = small_ref[k * SMALL : (k + 1) * SMALL, :].astype(jnp.float32)
    for ref in (gain_ref, conv_ref, heads_ref, gains_ref):
        ref[...] = jnp.zeros_like(ref)
    wide, taps, few, long = widths
    for i in range(8):
        gain_ref[:, i * wide : (i + 1) * wide] = found[i, 0:1, :wide]
        conv_ref[0:5, i * taps : (i + 1) * taps] = found[i, 1:6, :taps]
        heads_ref[0:3, i * few : (i + 1) * few] = found[i, 6:9, :few]
        gains_ref[1:2, i * long : (i + 1) * long] = found[i, 9:10, :long]
    spread = (row_ids(0, 128, DI) == lax.broadcasted_iota(jnp.int32, (128, DI), 1) // HEAD_DIM).astype(jnp.float32)
    gains_ref[0:1, :] = dot32(heads_ref[...], spread, precision=lax.Precision.HIGHEST)[2:3, :]


def out_kernel(gated_ref, weight_ref, x_ref, cot_ref, r_ref, result_ref, rk_ref, acc):
    weight = weight_ref[...]
    branch = dot32(gated_ref[...], weight)
    result_ref[...] = (x_ref[...].astype(jnp.float32) + branch).astype(result_ref.dtype)
    product = cot_ref[...].astype(jnp.float32) * branch
    part = product[:, :Q]
    for p in range(1, product.shape[1] // Q):
        part = part + product[:, p * Q : (p + 1) * Q]

    @pl.when(pl.program_id(0) == 0)
    def _():
        acc[...] = part

    @pl.when(pl.program_id(0) > 0)
    def _():
        acc[...] += part

    @pl.when(pl.program_id(0) == pl.num_programs(0) - 1)
    def _():
        r = r_ref[...]
        pull = r * r * (jnp.sum(acc[...], axis=-1, keepdims=True) / DI)
        lane = lax.broadcasted_iota(jnp.int32, rk_ref.shape, 1)
        rk_ref[...] = jnp.where(lane == 0, r, jnp.where(lane == 1, pull, 0.0))


def run_out(gated, weight, x, cot, r):
    rows, inner = gated.shape
    width = x.shape[1]
    step = width // 3
    here = lambda g: (0, g)
    return pl.pallas_call(
        out_kernel,
        grid=(3,),
        in_specs=[whole(gated.shape)] + [pl.BlockSpec((v.shape[0], step), here) for v in (weight, x, cot)] + [whole(r.shape)],
        out_specs=[pl.BlockSpec((rows, step), here), whole((rows, 128))],
        out_shape=[shaped((rows, width), x.dtype), shaped((rows, 128), jnp.float32)],
        scratch_shapes=[pltpu.VMEM((rows, Q), jnp.float32)],
        compiler_params=params(),
        cost_estimate=cost(4 * rows * inner * width, 4 * inner * width + 8 * rows * width),
    )(gated, weight, x, cot, r)


def pack_kernel(calls, widths, *refs):
    x_refs, (b_ref, h_ref, g_ref, n_ref, out_ref, conv) = refs[:calls], refs[calls:]
    wide, taps, few, long = widths
    start = 0
    for ref in (*x_refs, b_ref):
        conv[:, start : start + ref.shape[1]] = ref[...]
        start += ref.shape[1]
    inner = 8 * long
    spread = (row_ids(0, inner, 128) // HEAD_DIM == lax.broadcasted_iota(jnp.int32, (inner, 128), 1)).astype(jnp.float32)
    skips = dot32(conv[:, :inner], spread, precision=lax.Precision.HIGHEST)
    out_ref[...] = jnp.zeros_like(out_ref)
    for i in range(8):
        fields = [n_ref[0:1, i * wide : (i + 1) * wide]]
        fields += [conv[k : k + 1, i * taps : (i + 1) * taps] for k in range(KW + 1)]
        fields += [h_ref[k : k + 1, i * few : (i + 1) * few] for k in range(2)] + [skips[5:6, i * few : (i + 1) * few]]
        fields += [g_ref[0:1, i * long : (i + 1) * long]]
        start = 0
        for field in fields:
            out_ref[i : i + 1, start : start + field.shape[1]] = field
            start += field.shape[1]


def run_pack(widths, x_grads, b_grads, h_grads, g_grads, n_grads):
    wide, taps, few, long = widths
    width = wide + (KW + 1) * taps + 3 * few + long
    width += -width % 128
    args = (*x_grads, b_grads, h_grads, g_grads, n_grads)
    return pl.pallas_call(
        functools.partial(pack_kernel, len(x_grads), widths),
        grid=(1,),
        in_specs=[whole(v.shape) for v in args],
        out_specs=whole((8, width)),
        out_shape=shaped((8, width), jnp.float32),
        scratch_shapes=[pltpu.VMEM((8, 8 * taps), jnp.float32)],
        compiler_params=params(),
        cost_estimate=cost(1000000, 1000000),
    )(*args)


def back_kernel(spans, based, *refs):
    out_ref = refs[-1]
    grid = pl.program_id(0)

    @pl.when(grid == 0)
    def _():
        out_ref[...] = refs[0][...] if based else jnp.zeros_like(out_ref)

    refs = refs[based:-1]
    for i, (start, stop) in enumerate(spans):

        @pl.when((grid >= start) & (grid < stop))
        def _():
            out_ref[...] += dot32(refs[2 * i][...], refs[2 * i + 1][...], NT)


def run_back(pairs, base=None):
    rows, inner = pairs[0][0].shape[0], pairs[0][2].shape[0]
    spans, specs, args, start = [], [], [], 0
    if base is not None:
        specs, args = [whole((rows, inner))], [base]
    for grad, left_skip, weight, right_skip, width in pairs:
        step = min(WIDE, width)
        steps = width // step
        spans.append((start, start + steps))

        def at(skip, g, start=start, steps=steps):
            return (0, jnp.clip(g - start, 0, steps - 1) + skip)

        specs += [pl.BlockSpec((rows, step), functools.partial(at, left_skip // step)), pl.BlockSpec((inner, step), functools.partial(at, right_skip // step))]
        args += [grad, weight]
        start += steps
    return pl.pallas_call(
        functools.partial(back_kernel, tuple(spans), int(base is not None)),
        grid=(start,),
        in_specs=specs,
        out_specs=whole((rows, inner)),
        out_shape=shaped((rows, inner), jnp.float32),
        input_output_aliases={0: 0} if base is not None else {},
        compiler_params=params(),
        cost_estimate=cost(3000, 3000),
    )(*args)


TN = (((0,), (0,)), ((), ()))


def restore_kernel(targets_ref, blocks_ref, out_ref):
    count, rows, _ = blocks_ref.shape
    for i in range(count):
        out_ref[i * rows : (i + 1) * rows, :] = blocks_ref[targets_ref[i]]


def run_restore(targets, blocks):
    count, rows, width = blocks.shape
    return pl.pallas_call(
        restore_kernel,
        grid=(1,),
        in_specs=[smem(), whole(blocks.shape)],
        out_specs=whole((count * rows, width)),
        out_shape=shaped((count * rows, width), blocks.dtype),
        compiler_params=params(),
        cost_estimate=cost(6000000000, 12000000),
    )(targets, blocks)


def terms_kernel(turned, left_ref, right_ref, got_ref, *outs):
    rows = outs[0].shape[0]
    if turned:
        product = dot32(left_ref[...], right_ref[...], TN)
    else:
        product = dot32(left_ref[...], right_ref[...])
    product = product + got_ref[...].astype(jnp.float32)
    for i, ref in enumerate(outs):
        ref[...] = product[i * rows : (i + 1) * rows, :].astype(ref.dtype)


def run_terms(left, right, got, turned=False):
    rows, cols = got.shape
    inner = right.shape[0]
    step = 512 if cols % 512 == 0 else cols
    here = lambda g: (0, g)
    kinds = [jnp.bfloat16] * 3 + [jnp.float32]
    half = pl.BlockSpec((inner, rows), lambda g: (0, 1)) if turned else pl.BlockSpec((rows, inner), lambda g: (1, 0))
    return pl.pallas_call(
        functools.partial(terms_kernel, turned),
        grid=(cols // step,),
        in_specs=[half, pl.BlockSpec((inner, step), here), pl.BlockSpec((rows, step), here)],
        out_specs=[pl.BlockSpec((rows // 4, step), here)] * 4,
        out_shape=[shaped((rows // 4, cols), kind) for kind in kinds],
        compiler_params=params(),
        cost_estimate=cost(2 * rows * inner * cols, 6 * rows * cols),
    )(left, right, got)


def norm_kernel(order, me_ref, x_ref, gain_ref, out_ref, sent_ref, turned):
    rows, width = x_ref.shape
    for c in range(rows // Q):
        place = slice(c * Q, c * Q + Q)
        v = x_ref[place, :].astype(jnp.float32)
        normed = v * lax.rsqrt(jnp.mean(v * v, axis=-1, keepdims=True) + epsilon) * gain_ref[...]
        out_ref[place, :] = normed.astype(out_ref.dtype)
        for p in range(width // Q):
            turned[p * Q : p * Q + Q, place] = normed[:, p * Q : p * Q + Q].T.astype(turned.dtype)
    part = width // len(order)
    for k, j in enumerate(order):
        sent_ref[k * part : (k + 1) * part, :] = turned[pl.ds(pl.multiple_of((me_ref[0] ^ j) * part, 16), part), :]


def run_norm(order, me, x, gain):
    rows, width = x.shape
    b16 = jnp.bfloat16
    return pl.pallas_call(
        functools.partial(norm_kernel, order),
        grid=(1,),
        in_specs=[smem(), whole(x.shape), whole((1, width))],
        out_specs=[whole(x.shape), whole((width, rows))],
        out_shape=[shaped(x.shape, b16), shaped((width, rows), b16)],
        scratch_shapes=[pltpu.VMEM((width, rows), b16)],
        compiler_params=params(),
        cost_estimate=cost(2000000000, 6 * rows * width),
    )(me, x, gain)


def open_kernel(places, widths, me_ref, first_ref, x_ref, small_ref, *refs):
    pieces, refs = refs[: len(places)], refs[len(places) :]
    gain_ref, conv_ref, heads_ref, gains_ref, out_ref, sent_ref, bcd_ref, full_ref, *prep_refs, found, turned = refs
    unpack_kernel(widths, me_ref, small_ref, gain_ref, conv_ref, heads_ref, gains_ref, found)
    norm_kernel(ORDER, me_ref, x_ref, gain_ref, out_ref, sent_ref, turned)
    project_kernel(places, me_ref, out_ref, *pieces, bcd_ref, full_ref)
    prep_kernel(first_ref, bcd_ref, conv_ref.at[:, pl.ds(DI, 2 * NSTATE)], heads_ref, *prep_refs)


def run_open(me, first, x, small, pieces, widths, skip):
    f32, b16 = jnp.float32, jnp.bfloat16
    toks, width = x.shape
    wide, taps, few, long = widths
    places = tuple((j, start, min(v.shape[0], width // 8 - start)) for v, j, start in pieces)
    shapes = [((1, 8 * wide), f32), ((8, 8 * taps), f32), ((8, 128), f32), ((8, 8 * long), f32)]
    shapes += [((toks, width), b16), ((width, toks), b16), ((toks, BCD), f32), ((width, BCD), b16)]
    shapes += [((toks, 4 * Q), f32), ((256, toks), f32), ((toks, 2 * NSTATE), b16), ((2 * NSTATE, toks), b16)]
    return pl.pallas_call(
        functools.partial(open_kernel, places, widths),
        grid=(1,),
        in_specs=[smem(), smem(), whole(x.shape), whole(small.shape)] + [pl.BlockSpec((v.shape[0], BCD), lambda g: (0, skip // BCD)) for v, _, _ in pieces],
        out_specs=[whole(s) for s, _ in shapes],
        out_shape=[shaped(s, d) for s, d in shapes],
        scratch_shapes=[pltpu.VMEM((8, SMALL, small.shape[1]), f32), pltpu.VMEM((width, toks), b16)],
        compiler_params=params(),
        cost_estimate=cost(6000000000, 10000000),
    )(me, first, x, small, *[v for v, _, _ in pieces])


def norm_back_kernel(d_ref, x_ref, cot_ref, gain_ref, out_ref, grad_ref):
    @pl.when(pl.program_id(0) == 0)
    def _():
        grad_ref[...] = jnp.zeros_like(grad_ref)

    v = x_ref[...].astype(jnp.float32)
    rn = lax.rsqrt(jnp.mean(v * v, axis=-1, keepdims=True) + epsilon)
    d = d_ref[...]
    grad_ref[0:1, :] += sum_rows(d * v * rn)
    scaled = d * gain_ref[...]
    pull = rn * rn * rn * jnp.mean(v * scaled, axis=-1, keepdims=True)
    out_ref[...] = (cot_ref[...].astype(jnp.float32) + rn * scaled - v * pull).astype(out_ref.dtype)


def run_norm_back(d, x, cot, gain):
    rows, width = x.shape
    block = pl.BlockSpec((Q, width), lambda g: (g, 0))
    return pl.pallas_call(
        norm_back_kernel,
        grid=(rows // Q,),
        in_specs=[block, block, block, whole((1, width))],
        out_specs=[block, whole((8, width))],
        out_shape=[shaped(x.shape, x.dtype), shaped((8, width), jnp.float32)],
        compiler_params=params(),
        cost_estimate=cost(3000, 3000),
    )(d, x, cot, gain)


SMALL = 16
CALLS = ((0, 4), (4, 2))


def partners(bit):
    return [(i, i ^ bit) for i in range(8)]


def rotated(step):
    return [(i, (i + step) % 4) for i in range(4)]


def tie(*values):
    return lax.optimization_barrier(values)


def custom():
    return lax.axis_size("fsdp") == 8 and lax.axis_size("rep") == 4


def gathered_rows(w, late=False):
    half = w.shape[0] // 32 * 16
    two, four = yield [(w, "fsdp", partners(j)) for j in (2, 4)], 1
    sent = [(two[:half], "fsdp", partners(4)), (four[half:], "fsdp", partners(2))]
    if late:
        top, bottom, one, three = yield sent + [(v, "fsdp", partners(1)) for v in (w, two)], 1
        five, other_top, other_bottom = yield [(v, "fsdp", partners(1)) for v in (four, top, bottom)], 1
    else:
        top, bottom, one, three, five = yield sent + [(v, "fsdp", partners(1)) for v in (w, two, four)], 1
        other_top, other_bottom = yield [(v, "fsdp", partners(1)) for v in (top, bottom)], 1
    near = [(w, 0, 0), (one, 1, 0), (two, 2, 0), (three, 3, 0), (four, 4, 0), (five, 5, 0)]
    return near + [(top, 6, 0), (bottom, 6, half), (other_top, 7, 0), (other_bottom, 7, half)]


def dealt(v, turns):
    (got,) = yield [(v, "fsdp", None)], turns
    return got


def widen(v):
    return v.astype(jnp.float32)


def group_sum(left, right):
    half = left.shape[0] // 2
    odd = jnp.dot(left[:half], right, preferred_element_type=jnp.float32).astype(jnp.bfloat16)
    (got,) = yield [(odd, "fsdp", partners(1))], 1
    *terms, own = run_terms(left, right, got)
    others = yield [(v, "fsdp", partners(j)) for v, j in zip(terms, ORDER[4:7])], 1
    return own + widen(others[0]) + widen(others[1]) + widen(others[2])


def relayed_sum(left, right):
    b16 = jnp.bfloat16
    rows = left.shape[1] // 8
    half = rows // 2

    def product(start, stop):
        return contract_rows(left[:, start * rows : stop * rows], right)

    (got,) = yield [(product(0, 4).astype(b16), "fsdp", partners(1))], 1
    far = (product(4, 5) + widen(got[:rows])).astype(b16)
    from_x, from_y = yield [(far[:half], "fsdp", partners(2)), (far[half:], "fsdp", partners(4))], 1
    low = jnp.pad(widen(from_y), ((half, 0), (0, 0)))
    high = jnp.pad(widen(from_x), ((0, half), (0, 0)))
    to_x = (product(5, 6) + widen(got[rows : 2 * rows]) + low).astype(b16)
    to_y = (product(6, 7) + widen(got[2 * rows : 3 * rows]) + high).astype(b16)
    got_x, got_y = yield [(to_x, "fsdp", partners(2)), (to_y, "fsdp", partners(4))], 1
    return product(7, 8) + widen(got[3 * rows :]) + widen(got_x) + widen(got_y)


def out_sum(left, right):
    own = yield from relayed_sum(left, right)
    return (yield from half_sum(own))


def half_sum(own):
    b16 = jnp.bfloat16
    place = lax.axis_index("rep")
    odd, late = place % 2 == 1, place >= 2
    across = [(0, 2), (1, 3), (2, 0), (3, 1)]
    beside = [(0, 1), (1, 0), (2, 3), (3, 2)]

    def halves(v, second):
        top, bottom = jnp.split(v, 2)
        return jnp.where(second, bottom, top), jnp.where(second, top, bottom)

    def joined(mine, other, second):
        return jnp.where(second, jnp.concatenate([other, mine]), jnp.concatenate([mine, other]))

    keep, send = halves(own, odd)
    (got,) = yield [(send.astype(b16), "rep", beside)], 1
    keep, send = halves(widen(keep) + widen(got), late)
    (got,) = yield [(send.astype(b16), "rep", across)], 1
    mine = (keep + widen(got)).astype(b16)
    (got,) = yield [(mine, "rep", across)], 1
    mine = joined(mine, got, late)
    (got,) = yield [(mine, "rep", beside)], 1
    return joined(mine, got, odd)


def small_sum(rows):
    me, place = lax.axis_index("fsdp"), lax.axis_index("rep")
    rows = rows[me ^ jnp.array(ORDER, jnp.int32)]
    (got,) = yield [(rows[:4], "fsdp", partners(1))], 1
    rows = rows[4:] + got
    others = yield [(rows[i : i + 1], "fsdp", partners(j)) for i, j in enumerate(ORDER[4:7])], 1
    row = rows[3:] + others[0] + others[1] + others[2]
    got = yield [(row, "rep", rotated(k)) for k in (1, 2, 3)], 1
    stack = jnp.concatenate([row, *got])
    return jnp.sum(stack[(place - jnp.arange(4)) % 4], axis=0)


def transfer(v, axis, pairs):
    if pairs is None:
        return lax.all_to_all(v, axis, split_axis=0, concat_axis=0, tiled=True)
    return lax.ppermute(v, axis, pairs)


def slice_sum(left, right):
    own = yield from group_sum(left, right)
    return (yield from half_sum(own))


class Moves:
    def __init__(self):
        self.active = []

    def add(self, generator):
        want, turns = next(generator)
        entry = {"gen": generator, "want": want, "turns": turns, "got": None, "value": None}
        self.active.append(entry)
        return entry

    def turn(self, work=None, *values):
        fresh = [e for e in self.active if e["got"] is None]
        arrays, values = tie([[item[0] for item in e["want"]] for e in fresh], values)
        for e, some in zip(fresh, arrays):
            e["got"] = [None] * len(some)
        alike = {}
        for e, some in zip(fresh, arrays):
            for i, (v, item) in enumerate(zip(some, e["want"])):
                kind = (item[1], str(item[2]), v.shape[0], v.dtype.name) if item[1] == "rep" else (id(e), i)
                alike.setdefault(kind, []).append((e, i, v, item))
        for group in alike.values():
            moved = transfer(jnp.concatenate([g[2] for g in group], axis=1) if len(group) > 1 else group[0][2], *group[0][3][1:])
            start = 0
            for e, i, v, _ in group:
                e["got"][i] = moved[:, start : start + v.shape[1]] if len(group) > 1 else moved
                start += v.shape[1]
        results = work(*values) if work else ()
        for e in self.active:
            e["turns"] -= 1
        due = [e for e in self.active if e["turns"] == 0]
        arrived, results = tie([e["got"] for e in due], results)
        for e, got in zip(due, arrived):
            try:
                e["want"], e["turns"] = e["gen"].send(got)
                e["got"] = None
            except StopIteration as stop:
                e["value"] = stop.value
                self.active.remove(e)
        return results

    def after(self, value):
        want = self.active[0]["want"]
        array, *rest = want[-1]
        value, array = tie(value, array)
        want[-1] = (array, *rest)
        return value

    def finish(self):
        while self.active:
            self.turn()


def per_device(tokens, cotangent, lengths, dealing, norm_gain, in_weight, conv_weight, conv_bias, dt_bias, a_log, d_skip, gated_gain, out_weight):
    f32, b16 = jnp.float32, jnp.bfloat16
    groups = lax.axis_size("fsdp")
    tok_rows, width = tokens.shape
    block_rows = tok_rows // groups
    targets = dealing.reshape(groups)
    inverse = jnp.argsort(targets)
    first = lengths.reshape(-1)[:1]
    me = lax.axis_index("fsdp").reshape(1)
    moves = Moves()

    def blocks(values):
        return values.reshape(groups, block_rows, width)[inverse]

    def deal(values):
        return lax.all_to_all(blocks(values), "fsdp", split_axis=0, concat_axis=0, tiled=True).reshape(tok_rows, width)

    def undeal(values):
        blocks = lax.all_to_all(values.reshape(groups, block_rows, width), "fsdp", split_axis=0, concat_axis=0, tiled=True)
        return blocks[targets].reshape(tok_rows, width)

    own_small = [norm_gain, conv_weight, conv_bias, dt_bias, a_log, d_skip, gated_gain]

    def rows_of(values):
        values = [v if v.ndim == 2 else v[None] for v in values]
        longest = max(v.shape[1] for v in values)
        packed = jnp.concatenate([pad_lanes(v, longest) for v in values])
        return jnp.pad(packed, ((0, SMALL - packed.shape[0]), (0, 0)))

    def doubled(v, bit):
        return (jnp.concatenate([v, lax.ppermute(v, "fsdp", partners(bit))]),)

    if custom():
        rows, span = in_weight.shape[0], DI + BCD
        w_xb = lax.pad(in_weight, jnp.zeros((), b16), ((0, 0, 0), (-DI, span + DI - in_weight.shape[1], 0)))
        e_xb = moves.add(gathered_rows(w_xb, True))
        e_x = moves.add(dealt(blocks(tokens), 2))
        (small,) = moves.turn(lambda *v: doubled(rows_of(v), 2), *own_small)
        small, cot_blocks = moves.turn(lambda v, c: (*doubled(v, 4), blocks(c)), small, cotangent)
        out_weight = moves.after(out_weight)
        w_out = lax.all_gather(out_weight, "fsdp", axis=0, tiled=True)
        (small,) = moves.turn(lambda v: doubled(v, 1), small)
        pieces = e_xb["value"]
        x = e_x["value"].reshape(tok_rows, width)
        widths = (norm_gain.size, conv_bias.size, dt_bias.size, gated_gain.size)
    else:
        x = deal(tokens)
        w_z = lax.all_gather(in_weight[:, :DI], "fsdp", axis=0, tiled=True)
        w_out = lax.all_gather(out_weight, "fsdp", axis=0, tiled=True)
        small_all = lax.all_gather(rows_of(own_small), "fsdp", axis=0, tiled=False).astype(f32)
        w_xb = lax.all_gather(pad_lanes(in_weight[:, DI:], DI + BCD), "fsdp", axis=0, tiled=True)
        parts, row = [], 0
        for v in (u if u.ndim == 2 else u[None] for u in own_small):
            parts.append(small_all[:, row : row + v.shape[0], : v.shape[1]].transpose(1, 0, 2).reshape(v.shape[0], -1))
            row += v.shape[0]
        gain, taps, bias, step_bias, rate, skip, ggain = parts
        conv = jnp.concatenate([taps, bias, jnp.zeros((3, bias.shape[1]), f32)])
        heads = pad_lanes(jnp.concatenate([step_bias, rate, jnp.zeros((6, HEADS), f32)]), 128)
        gains = jnp.concatenate([jnp.repeat(skip, HEAD_DIM, axis=1), ggain, jnp.zeros((6, DI), f32)])
    if custom():

        def open_up(x):
            gain, conv, heads, gains, normed, sent, bcd, w_b, *prep = run_open(me, first, x, small, pieces, widths, DI)
            return gain, conv, heads, gains, normed, sent, bcd, w_b, prep, *run_project(me, normed, pieces, 0, DI)

        e_z = moves.add(gathered_rows(in_weight[:, :DI]))
        gain, conv, heads, gains, normed, sent, bcd, w_b, prep, xr, w_x = moves.turn(open_up, x)
        conv_x, conv_bc = conv[:, :DI], conv[:, DI:]
        ssm, states = moves.turn(lambda v: run_forward(first, v, conv_x, gains, prep), xr)
        moves.turn()
        e_cot = moves.add(dealt(cot_blocks, 1))

        def close_up(ssm):
            z, full = run_project(me, normed, e_z["value"], 0, DI)
            return z, full, *run_gated(ORDER, me, z, ssm, gains)

        z, w_z, gated, gated_sent, r = moves.turn(close_up, ssm)
        cot = e_cot["value"].reshape(tok_rows, width)
        e_rows = moves.add(out_sum(gated_sent, cot))
        result, rk = moves.turn(lambda v: run_out(v, w_out, x, cot, r), gated)
    else:
        conv_x, conv_bc = conv[:, :DI], conv[:, DI:]
        normed, sent = run_norm((0,), me * 0, x, gain)
        w_x, w_b = w_xb[:, :DI], w_xb[:, DI:]
        bcd = jnp.dot(normed, w_b, preferred_element_type=f32)
        xr = jnp.dot(normed, w_x, preferred_element_type=f32)
        cot = deal(cotangent)
        prep = run_prep(first, bcd, conv_bc, heads)
        ssm, states = run_forward(first, xr, conv_x, gains, prep)
        z = jnp.dot(normed, w_z, preferred_element_type=f32)
        gated, _, r = run_gated(tuple(range(8)), me * 0, z, ssm, gains)
        result, rk = run_out(gated, w_out, x, cot, r)
        s_out = lax.psum_scatter(contract_rows(gated, cot, b16), "fsdp", scatter_dimension=0, tiled=True)

    def gate(rk):
        return run_gate(z, ssm, cot, w_out, rk, gains)

    def backward(base, count, ds):
        return run_backward(base, count, first, xr, ssm, ds, conv_x, gains, prep, states)

    def close(backs):
        return run_post(first, bcd, conv_bc, heads, prep, [b[2:] for b in backs])

    def back(backs, d_b):
        pairs = [(dz, 0, w_z, 0, DI)] + [(b[0], 0, w_x, base * LANES, count * LANES) for b, (base, count) in zip(backs, CALLS)]
        return run_back(pairs + [(d_b, 0, w_b, 0, BCD)])

    if custom():
        dz, ds, ggrads = moves.turn(gate, rk)

        def first_back(dz, ds):
            z_term, ds = tie(contract_rows(normed, dz, b16), ds)
            held.append(lax.psum_scatter(z_term, "fsdp", scatter_dimension=0, tiled=True))
            return backward(*CALLS[0], ds)

        held = []
        backs = [moves.turn(first_back, dz, ds)]
        (s_z,) = held
        e_first = moves.add(slice_sum(sent, backs[0][0]))

        def middle(ds):
            both = backs + [backward(*CALLS[1], ds)]
            return both[1], *close(both)

        last, d_b, bgrads, hgrads = moves.turn(middle, ds)
        backs.append(last)
        e_last = moves.add(slice_sum(sent, jnp.concatenate([last[0], d_b], axis=1)))
        e_z = moves.add(half_sum(s_z))
        (d_normed,) = moves.turn(lambda d: (back(backs, d),), d_b)

        def finish(d_normed):
            d_input, ngrads = run_norm_back(d_normed, x, cot, gain)
            return d_input, run_pack(widths, [b[1] for b in backs], bgrads, hgrads, ggrads, ngrads)

        d_input, packed = moves.turn(finish, d_normed)
    else:
        dz, ds, ggrads = gate(rk)
        s_z = lax.psum_scatter(contract_rows(normed, dz, b16), "fsdp", scatter_dimension=0, tiled=True)
        backs = [backward(*call, ds) for call in CALLS]
        d_b, bgrads, hgrads = close(backs)
        d_normed = back(backs, d_b)
        d_input, ngrads = run_norm_back(d_normed, x, cot, gain)
        s_in = [lax.psum_scatter(contract_rows(normed, d, b16), "fsdp", scatter_dimension=0, tiled=True) for d in [b[0] for b in backs] + [d_b]]
        output, input_grad = undeal(result), undeal(d_input)

    if not custom():
        xgrads = jnp.concatenate([b[1] for b in backs], axis=1)
        g_ggain = ggrads[0]
        g_conv = jnp.concatenate([xgrads[:KW], bgrads[:KW]], axis=1)
        g_cbias = jnp.concatenate([xgrads[KW], bgrads[KW]])
        g_dskip = jnp.sum(xgrads[5].reshape(HEADS, HEAD_DIM), axis=1)
        spread = [
            ngrads[0].reshape(groups, -1),
            g_conv.reshape(KW, groups, -1).transpose(1, 0, 2).reshape(groups, -1),
            g_cbias.reshape(groups, -1),
            hgrads[0, :HEADS].reshape(groups, -1),
            hgrads[1, :HEADS].reshape(groups, -1),
            g_dskip.reshape(groups, -1),
            g_ggain.reshape(groups, -1),
        ]
        packed = jnp.concatenate(spread, axis=1)
        packed = pad_lanes(packed, packed.shape[1] + -packed.shape[1] % 128)
    sizes = [v.size for v in own_small]
    tail = in_weight.shape[1] - 2 * DI

    def cut(row):
        ends, outs = 0, []
        for size in sizes:
            outs.append(row[ends : ends + size])
            ends += size
        return outs

    if custom():
        e_small = moves.add(small_sum(packed))
        e_input = moves.add(dealt(d_input.reshape(groups, block_rows, width), 1))
        moves.turn()
        e_output = moves.add(dealt(result.reshape(groups, block_rows, width), 1))
        moves.turn()

        def restored(entry):
            return run_restore(targets, entry["value"])

        input_grad, r_out = moves.turn(lambda: (restored(e_input), widen(e_rows["value"])))
        (output,) = moves.turn(lambda: (restored(e_output),))
        last = CALLS[-1][1] * LANES + tail

        def gather_up():
            known = jnp.concatenate([e_z["value"], e_first["value"], jnp.zeros((rows, last), b16)], axis=1)
            return widen(known), *cut(e_small["value"])

        r_in, *outs = moves.turn(gather_up)
        moves.finish()
        r_in = lax.dynamic_update_slice(r_in, widen(e_last["value"][:, :last]), (0, r_in.shape[1] - last))
    else:
        s_small = jnp.sum(lax.all_to_all(packed, "fsdp", split_axis=0, concat_axis=0, tiled=True), axis=0)
        r_small = jnp.sum(lax.all_gather(s_small, "rep", axis=0, tiled=False), axis=0)
        *r_in, r_out = lax.psum((s_z, *s_in, s_out), "rep")
        r_in = jnp.concatenate(r_in, axis=1)[:, : in_weight.shape[1]]
        outs = cut(r_small)
    return (output, input_grad, outs[0], r_in.astype(f32), outs[1].reshape(conv_weight.shape), outs[2], outs[3], outs[4], outs[5], outs[6], r_out.astype(f32))


def solution(mesh):
    placed = (
        P(("rep", "fsdp"), None),
        P(("rep", "fsdp"), None),
        P("rep", "fsdp", None),
        P("rep", "fsdp", None),
        P("fsdp"),
        P("fsdp", None),
        P(None, "fsdp"),
        P("fsdp"),
        P("fsdp"),
        P("fsdp"),
        P("fsdp"),
        P("fsdp"),
        P("fsdp", None),
    )
    return jax.shard_map(
        per_device,
        mesh=mesh,
        in_specs=placed,
        out_specs=(
            P(("rep", "fsdp"), None),
            P(("rep", "fsdp"), None),
            P("fsdp"),
            P("fsdp", None),
            P(None, "fsdp"),
            P("fsdp"),
            P("fsdp"),
            P("fsdp"),
            P("fsdp"),
            P("fsdp"),
            P("fsdp", None),
        ),
        check_vma=False,
    )
```

```python
import functools

import jax
import jax.numpy as jnp
from jax import lax
from jax.experimental import pallas as pl
from jax.experimental.pallas import tpu as pltpu
from jax.sharding import PartitionSpec as P

DI = 3072
HEAD_DIM = 64
NSTATE = 128
KW = 4
HEADS = 48
BCD = 384

epsilon = 1e-05


Q = 128
GROUP = 8
LANES = GROUP * HEAD_DIM
NEG = -1e30
VMEM = 56 * 1024 * 1024


def dot32(a, b, dims=(((1,), (0,)), ((), ())), precision=None):
    return lax.dot_general(a, b, dims, preferred_element_type=jnp.float32, precision=precision)


NT = (((1,), (1,)), ((), ()))


def row_ids(start, rows, cols):
    return lax.broadcasted_iota(jnp.int32, (rows, cols), 0) + start


def shifted_down(ref, cols, c, first, width):
    if c == 0:
        tall = jnp.concatenate([jnp.zeros((8, width), jnp.float32), ref[0:Q, cols]], axis=0)
    else:
        tall = ref[c * Q - 8 : c * Q + Q, cols]
    place = row_ids(c * Q, Q, width)
    outs = [tall[8:]]
    for j in range(1, KW):
        moved = pltpu.roll(tall, j, 0)[8:]
        keep = (place >= j) & ((place < first) | (place >= first + j))
        outs.append(jnp.where(keep, moved, 0.0))
    return outs


def conv_back(ref, cols, c, first, width, taps):
    tall = ref[c * Q : c * Q + Q + 8, cols]
    place = row_ids(c * Q, Q, width)
    total = taps[KW - 1] * tall[:Q]
    for j in range(1, KW):
        moved = pltpu.roll(tall, Q + 8 - j, 0)[:Q]
        keep = (place < first - j) | (place >= first)
        total = total + taps[KW - 1 - j] * jnp.where(keep, moved, 0.0)
    return total


def sigmoid(v):
    return 0.5 * jnp.tanh(0.5 * v) + 0.5


def sum_rows(v):
    return jnp.sum(v, axis=0, keepdims=True)


def prep_kernel(first_ref, bcd_ref, conv_ref, head_ref, wide_ref, tall_ref, bc_ref, bct_ref):
    first = first_ref[0]
    tri = (row_ids(0, Q, Q) >= lax.broadcasted_iota(jnp.int32, (Q, Q), 1)).astype(jnp.float32)
    rate = -jnp.exp(head_ref[1:2, :])
    lane = lax.broadcasted_iota(jnp.int32, (Q, 128), 1)
    for c in range(bcd_ref.shape[0] // Q):
        rows = slice(c * Q, c * Q + Q)
        moved = shifted_down(bcd_ref, slice(0, 2 * NSTATE), c, first, 2 * NSTATE)
        mixed = conv_ref[4:5, :] + conv_ref[3:4, :] * moved[0]
        for j in range(1, KW):
            mixed = mixed + conv_ref[KW - 1 - j : KW - j, :] * moved[j]
        act = mixed * sigmoid(mixed)
        b32, c32 = act[:, :NSTATE], act[:, NSTATE:]
        b16, c16 = b32.astype(jnp.bfloat16), c32.astype(jnp.bfloat16)
        bc_ref[rows, :] = act.astype(jnp.bfloat16)
        bct_ref[:NSTATE, rows] = b32.T.astype(jnp.bfloat16)
        bct_ref[NSTATE:, rows] = c32.T.astype(jnp.bfloat16)
        wide_ref[rows, :Q] = dot32(c16, b16, NT)
        wide_ref[rows, Q : 2 * Q] = dot32(b16, c16, NT)
        raw = jnp.where(lane < HEADS, bcd_ref[rows, 2 * NSTATE :] + head_ref[0:1, :], 0.0)
        step = jax.nn.softplus(raw)
        cum = dot32(tri, rate * step, precision=lax.Precision.HIGHEST)
        cp = cum - jnp.log(jnp.maximum(step, 1e-37))
        wide_ref[rows, 2 * Q : 3 * Q] = cum
        wide_ref[rows, 3 * Q :] = cp
        tall_ref[:128, rows] = cum.T
        tall_ref[128:, rows] = cp.T


def chunk_masks(first, c, transposed):
    base = c * Q
    row = row_ids(base, Q, Q)
    col = lax.broadcasted_iota(jnp.int32, (Q, Q), 1) + base
    ordered = (col >= row) if transposed else (row >= col)
    inside = ordered & ((row >= first) == (col >= first))
    carry = ((row >= first) == (base - 1 >= first)) & (base > 0)
    last = (row >= first) == (base + Q - 1 >= first)
    through = (base > 0) & ((base + Q - 1 >= first) == (base - 1 >= first))
    return inside, carry, last, through


def lane_column(values, k):
    return jnp.broadcast_to(values[:, k : k + 1], (Q, Q))


def conv_act(x_ref, conv_ref, cols, c, first):
    moved = shifted_down(x_ref, cols, c, first, Q)
    mixed = conv_ref[4:5, cols] + conv_ref[3:4, cols] * moved[0]
    for j in range(1, KW):
        mixed = mixed + conv_ref[KW - 1 - j : KW - j, cols] * moved[j]
    return moved, mixed


def both_heads(left, right, half):
    none = jnp.zeros_like(right)
    stacked = jnp.concatenate([jnp.where(half, right, none), jnp.where(half, none, right)], axis=0)
    return dot32(jnp.concatenate(left, axis=1), stacked)


def forward_kernel(first_ref, x_ref, conv_ref, gain_ref, wide_ref, tall_ref, bc_ref, bct_ref, ssm_ref, states_ref, state):
    first = first_ref[0]
    group = pl.program_id(0)
    half = lax.broadcasted_iota(jnp.int32, (Q, Q), 1) < HEAD_DIM
    state[...] = jnp.zeros_like(state)
    shift = (Q - GROUP * group) % Q
    pairs = range(GROUP // 2)
    for c in range(x_ref.shape[0] // Q):
        rows = slice(c * Q, c * Q + Q)
        inside, carry, last, through = chunk_masks(first, c, False)
        cum = pltpu.roll(wide_ref[rows, 2 * Q : 3 * Q], shift, 1)
        cp = pltpu.roll(wide_ref[rows, 3 * Q :], shift, 1)
        cpt = tall_ref[pl.ds(pl.multiple_of(128 + group * GROUP, GROUP), GROUP), rows]
        scores = wide_ref[rows, :Q]
        old16 = state[...].astype(jnp.bfloat16)
        states_ref[c * NSTATE : (c + 1) * NSTATE, :] = old16
        if c > 0:
            carried = dot32(bc_ref[rows, NSTATE:], old16)
        weighted, ends = [], []
        for p in pairs:
            cols = slice(p * Q, p * Q + Q)
            _, mixed = conv_act(x_ref, conv_ref, cols, c, first)
            xs = mixed * sigmoid(mixed)
            mixing, cums, cps = [], [], []
            for k in (2 * p, 2 * p + 1):
                cum_b = lane_column(cum, k)
                decay = jnp.exp(jnp.where(inside, cum_b - cpt[k : k + 1, :], NEG))
                mixing.append((scores * decay).astype(jnp.bfloat16))
                cums.append(cum_b)
                cps.append(lane_column(cp, k))
            cum_pair = jnp.where(half, cums[0], cums[1])
            cp_pair = jnp.where(half, cps[0], cps[1])
            y = both_heads(mixing, xs.astype(jnp.bfloat16), half)
            if c > 0:
                y = y + jnp.where(carry, jnp.exp(cum_pair), 0.0) * carried[:, cols]
            ssm_ref[rows, cols] = y + gain_ref[0:1, cols] * xs
            end = cum_pair[Q - 1 : Q, :]
            weighted.append((jnp.where(last, jnp.exp(end - cp_pair), 0.0) * xs).astype(jnp.bfloat16))
            ends.append(end)
        fresh = dot32(bct_ref[:NSTATE, rows], jnp.concatenate(weighted, axis=1))
        for p in pairs:
            cols = slice(p * Q, p * Q + Q)
            kept = 0.0 if c == 0 else jnp.where(through, jnp.exp(ends[p]), 0.0) * state[:, cols]
            state[:, cols] = kept + fresh[:, cols]


def gated_kernel(order, me_ref, z_ref, ssm_ref, gain_ref, gated_ref, sent_ref, r_ref):
    squares = jnp.zeros((Q, Q), jnp.float32)
    for p in range(z_ref.shape[1] // Q):
        cols = slice(p * Q, p * Q + Q)
        zv = z_ref[:, cols]
        g = ssm_ref[:, cols] * (zv * sigmoid(zv))
        squares = squares + g * g
    r = lax.rsqrt(jnp.sum(squares, axis=-1, keepdims=True) / DI + epsilon)
    wide = jnp.broadcast_to(r, (Q, Q))
    r_ref[...] = wide
    for p in range(z_ref.shape[1] // Q):
        cols = slice(p * Q, p * Q + Q)
        zv = z_ref[:, cols]
        g = ssm_ref[:, cols] * (zv * sigmoid(zv))
        gated_ref[:, cols] = (g * wide * gain_ref[1:2, cols]).astype(gated_ref.dtype)
    part = gated_ref.shape[1] // 8
    for i, j in enumerate(order):
        sent_ref[:, i * part : (i + 1) * part] = gated_ref[:, pl.ds(pl.multiple_of((me_ref[0] ^ j) * part, 128), part)]


def gate_kernel(z_ref, ssm_ref, cot_ref, weight_ref, rk_ref, gain_ref, dz_ref, ds_ref, grads_ref, d_gated):
    d_gated[...] = dot32(cot_ref[...], weight_ref[...], NT)
    grads_ref[...] = jnp.zeros_like(grads_ref)
    for c in range(z_ref.shape[0] // Q):
        rows = slice(c * Q, c * Q + Q)
        scale = lane_column(rk_ref[rows, :], 0)
        pull = lane_column(rk_ref[rows, :], 1)
        for p in range(z_ref.shape[1] // Q):
            cols = slice(p * Q, p * Q + Q)
            zv = z_ref[rows, cols]
            sz = sigmoid(zv)
            silu_z = zv * sz
            ssm = ssm_ref[rows, cols]
            g = ssm * silu_z
            gs = d_gated[rows, cols] * scale
            grads_ref[0:1, cols] += sum_rows(gs * g)
            d_g = gain_ref[1:2, cols] * gs - g * pull
            dz_ref[rows, cols] = (d_g * ssm * (sz + silu_z * (1.0 - sz))).astype(dz_ref.dtype)
            ds_ref[rows, cols] = (d_g * silu_z).astype(ds_ref.dtype)


def eight_rows(v):
    return functools.reduce(jnp.add, [v[i : i + 8, :] for i in range(0, v.shape[0], 8)])


def backward_kernel(base, first_ref, x_ref, ssm_ref, ds_ref, conv_ref, gain_ref, wide_ref, tall_ref, bc_ref, bct_ref, states_ref, d_ref, grads_ref, sums_ref, flow_ref, dstate, dconv, acc):
    first = first_ref[0]
    group = base + pl.program_id(0)
    half = lax.broadcasted_iota(jnp.int32, (Q, Q), 1) < HEAD_DIM
    dstate[...] = jnp.zeros_like(dstate)
    acc[...] = jnp.zeros_like(acc)
    rows_all = x_ref.shape[0]
    dconv[rows_all : rows_all + 8, :] = jnp.zeros((8, dconv.shape[1]), jnp.float32)
    flow_ref[...] = jnp.zeros_like(flow_ref)

    @pl.when(pl.program_id(0) == 0)
    def _():
        sums_ref[...] = jnp.zeros_like(sums_ref)

    shift = (Q - GROUP * group) % Q
    chunks = rows_all // Q
    pairs = range(GROUP // 2)
    pick = (lax.broadcasted_iota(jnp.int32, (LANES, Q), 1) == GROUP * group + row_ids(0, LANES, Q) // HEAD_DIM).astype(jnp.bfloat16)
    for c in range(chunks - 1, -1, -1):
        rows = slice(c * Q, c * Q + Q)
        inside, carry, last, through = chunk_masks(first, c, True)
        cum = pltpu.roll(wide_ref[rows, 2 * Q : 3 * Q], shift, 1)
        cp = pltpu.roll(wide_ref[rows, 3 * Q :], shift, 1)
        cumt = tall_ref[pl.ds(pl.multiple_of(group * GROUP, GROUP), GROUP), rows]
        scores_t = wide_ref[rows, Q : 2 * Q]
        b16, c16t = bc_ref[rows, :NSTATE], bct_ref[NSTATE:, rows]
        dst = jnp.zeros((Q, Q), jnp.float32)
        if c < chunks - 1:
            later16 = dstate[...].astype(jnp.bfloat16)
            carried = dot32(b16, later16)
        high, low, local, weighted, carries, eys, ends = ([] for _ in range(7))
        for p in pairs:
            cols = slice(p * Q, p * Q + Q)
            moved, mixed = conv_act(x_ref, conv_ref, cols, c, first)
            sx = sigmoid(mixed)
            xs = mixed * sx
            x16 = xs.astype(jnp.bfloat16)
            skip = gain_ref[0:1, cols]
            dy16 = ds_ref[rows, cols]
            d_ssm = dy16.astype(jnp.float32)
            acc[40:48, cols] += eight_rows(d_ssm * xs)
            mixing, cums, cps = [], [], []
            for k in (2 * p, 2 * p + 1):
                cp_b = lane_column(cp, k)
                decay = jnp.exp(jnp.where(inside, cumt[k : k + 1, :] - cp_b, NEG))
                mixing.append((scores_t * decay).astype(jnp.bfloat16))
                x_half = jnp.where(half == (k == 2 * p), x16, jnp.zeros_like(x16))
                dst = dst + decay * dot32(x_half, dy16, NT)
                cums.append(lane_column(cum, k))
                cps.append(cp_b)
            cum_pair = jnp.where(half, cums[0], cums[1])
            cp_pair = jnp.where(half, cps[0], cps[1])
            dx = both_heads(mixing, dy16, half)
            in_dot = x16.astype(jnp.float32) * dx
            u = d_ssm * (ssm_ref[rows, cols] - skip * xs) - in_dot
            high.append(u.astype(jnp.bfloat16))
            low.append((u - high[-1].astype(jnp.float32)).astype(jnp.bfloat16))
            local.append(in_dot.astype(jnp.bfloat16))
            end = cum_pair[Q - 1 : Q, :]
            ends.append(end)
            if c < chunks - 1:
                weight = jnp.where(last, jnp.exp(end - cp_pair), 0.0)
                moved_in = weight * carried[:, cols]
                dx = dx + moved_in
                carries.append((xs * moved_in).astype(jnp.bfloat16))
                weighted.append((weight * xs).astype(jnp.bfloat16))
            if c > 0:
                eys.append((jnp.where(carry, jnp.exp(cum_pair), 0.0) * d_ssm).astype(jnp.bfloat16))
            d_mixed = (dx + skip * d_ssm) * (sx + xs * (1.0 - sx))
            dconv[rows, cols] = d_mixed
            acc[32:40, cols] += eight_rows(d_mixed)
            for j in range(KW):
                acc[8 * (KW - 1 - j) : 8 * (KW - j), cols] += eight_rows(d_mixed * moved[j])
            taps = [conv_ref[i : i + 1, cols] for i in range(KW)]
            d_ref[rows, cols] = conv_back(dconv, cols, c, first, Q, taps).astype(d_ref.dtype)
        join = functools.partial(jnp.concatenate, axis=1)
        sums_ref[rows, :Q] += dst
        sums_ref[rows, 3 * Q : 4 * Q] += dot32(join(high), pick) + dot32(join(low), pick)
        sums_ref[rows, 4 * Q : 5 * Q] += dot32(join(local), pick)
        if c < chunks - 1:
            sums_ref[rows, Q : 2 * Q] += dot32(join(weighted), later16, NT)
            sums_ref[rows, 5 * Q :] += dot32(join(carries), pick)
        if c > 0:
            ey16 = join(eys)
            old16 = states_ref[c * NSTATE : (c + 1) * NSTATE, :]
            sums_ref[rows, 2 * Q : 3 * Q] += dot32(ey16, old16, NT)
            fresh = dot32(c16t, ey16)
            for p in pairs:
                cols = slice(p * Q, p * Q + Q)
                if c < chunks - 1:
                    kept = jnp.where(through, jnp.exp(ends[p]), 0.0) * dstate[:, cols]
                    flow_ref[c : c + 1, cols] = sum_rows(kept * old16[:, cols].astype(jnp.float32))
                    dstate[:, cols] = kept + fresh[:, cols]
                else:
                    dstate[:, cols] = fresh[:, cols]
    for i in range(8):
        grads_ref[i : i + 1, :] = sum_rows(acc[8 * i : 8 * i + 8, :]) if i < 6 else jnp.zeros((1, LANES), jnp.float32)


def post_kernel(calls, first_ref, bcd_ref, conv_ref, head_ref, bc_ref, *refs):
    sums_refs, flow_refs, (d_ref, grads_ref, hgrads_ref, dconv) = refs[:calls], refs[calls:-4], refs[-4:]
    first = first_ref[0]
    rows_all = bcd_ref.shape[0]
    wide = 2 * NSTATE
    dconv[rows_all : rows_all + 8, :] = jnp.zeros((8, wide), jnp.float32)
    grads_ref[...] = jnp.zeros_like(grads_ref)
    hgrads_ref[...] = jnp.zeros_like(hgrads_ref)
    lane = lax.broadcasted_iota(jnp.int32, (Q, 128), 1)
    rate = -jnp.exp(head_ref[1:2, :])
    flow = jnp.zeros((8, 128), jnp.float32)
    start = 0
    for ref in flow_refs:
        width = ref.shape[1]
        spread = (row_ids(start, width, 128) // HEAD_DIM == lax.broadcasted_iota(jnp.int32, (width, 128), 1)).astype(jnp.float32)
        flow = flow + dot32(ref[...], spread, precision=lax.Precision.HIGHEST)
        start += width
    row, col = row_ids(0, Q, Q), lax.broadcasted_iota(jnp.int32, (Q, Q), 1)
    earlier_sum = (col < row).astype(jnp.float32)
    for c in range(rows_all // Q - 1, -1, -1):
        rows = slice(c * Q, c * Q + Q)
        moved = shifted_down(bcd_ref, slice(0, wide), c, first, wide)
        mixed = conv_ref[4:5, :] + conv_ref[3:4, :] * moved[0]
        for j in range(1, KW):
            mixed = mixed + conv_ref[KW - 1 - j : KW - j, :] * moved[j]
        sx = sigmoid(mixed)
        dst, db, dc, us, vs, carried = (functools.reduce(jnp.add, [ref[rows, i * Q : (i + 1) * Q] for ref in sums_refs]) for i in range(6))
        d_b = db + dot32(dst.astype(jnp.bfloat16), bc_ref[rows, NSTATE:])
        d_c = dc + dot32(dst.T.astype(jnp.bfloat16), bc_ref[rows, :NSTATE])
        d_mixed = jnp.concatenate([d_b, d_c], axis=1) * (sx + mixed * sx * (1.0 - sx))
        dconv[rows, :] = d_mixed
        grads_ref[4:5, :] += sum_rows(d_mixed)
        for j in range(KW):
            grads_ref[KW - 1 - j : KW - j, :] += sum_rows(d_mixed * moved[j])
        taps = [conv_ref[i : i + 1, :] for i in range(KW)]
        d_ref[rows, :wide] = conv_back(dconv, slice(0, wide), c, first, wide, taps).astype(d_ref.dtype)
        later_sum = ((col >= row) & ((row + c * Q >= first) == (col + c * Q >= first))).astype(jnp.float32)
        d_la = dot32(later_sum, us, precision=lax.Precision.HIGHEST)
        d_la = d_la + dot32(earlier_sum, carried, precision=lax.Precision.HIGHEST) + flow[c : c + 1, :]
        d_log = vs + carried
        raw = bcd_ref[rows, wide:] + head_ref[0:1, :]
        step = jax.nn.softplus(raw)
        sig = sigmoid(raw)
        ratio = jnp.where(raw < -17.0, 1.0, sig / jnp.maximum(step, 1e-37))
        d_raw = jnp.where(lane < HEADS, d_log * ratio + d_la * rate * sig, 0.0)
        d_ref[rows, wide:] = d_raw.astype(d_ref.dtype)
        hgrads_ref[0:1, :] += sum_rows(d_raw)
        hgrads_ref[1:2, :] += sum_rows(jnp.where(lane < HEADS, d_la * rate * step, 0.0))


def smem():
    return pl.BlockSpec(memory_space=pltpu.SMEM)


def whole(shape):
    return pl.BlockSpec(shape, lambda g: (0,) * len(shape))


def shaped(shape, kind):
    return jax.ShapeDtypeStruct(shape, kind)


def params(limit=VMEM):
    return pltpu.CompilerParams(vmem_limit_bytes=limit)


def cost(flops, size):
    return pl.CostEstimate(flops=flops // 3, bytes_accessed=size // 3, transcendentals=0)


def run_prep(first, bcd, conv, heads):
    rows = bcd.shape[0]
    f32, b16 = jnp.float32, jnp.bfloat16
    shapes = [((rows, 4 * Q), f32), ((256, rows), f32), ((rows, 2 * NSTATE), b16), ((2 * NSTATE, rows), b16)]
    return pl.pallas_call(
        prep_kernel,
        grid=(1,),
        in_specs=[smem(), whole((rows, BCD)), whole((8, 2 * NSTATE)), whole((8, 128))],
        out_specs=[whole(s) for s, _ in shapes],
        out_shape=[shaped(s, d) for s, d in shapes],
        compiler_params=params(),
        cost_estimate=cost(2000000000, 4000000),
    )(first, bcd, conv, heads)


def run_forward(first, x, conv, gains, prep):
    rows, width = x.shape
    chunks = rows // Q
    here = lambda g: (0, g)
    block, eight = pl.BlockSpec((rows, LANES), here), pl.BlockSpec((8, LANES), here)
    return pl.pallas_call(
        forward_kernel,
        grid=(width // LANES,),
        in_specs=[smem(), block, eight, eight] + [whole(v.shape) for v in prep],
        out_specs=[block, pl.BlockSpec((chunks * NSTATE, LANES), here)],
        out_shape=[shaped((rows, width), jnp.float32), shaped((chunks * NSTATE, width), jnp.bfloat16)],
        scratch_shapes=[pltpu.VMEM((NSTATE, LANES), jnp.float32)],
        compiler_params=params(),
        cost_estimate=cost(20000000000, 20000000),
    )(first, x, conv, gains, *prep)


def run_gated(order, me, z, ssm, gains):
    rows, width = z.shape
    b16 = jnp.bfloat16
    block = pl.BlockSpec((Q, width), lambda g: (g, 0))
    thin = pl.BlockSpec((Q, Q), lambda g: (g, 0))
    return pl.pallas_call(
        functools.partial(gated_kernel, order),
        grid=(rows // Q,),
        in_specs=[smem(), block, block, whole(gains.shape)],
        out_specs=[block, block, thin],
        out_shape=[shaped((rows, width), b16), shaped((rows, width), b16), shaped((rows, Q), jnp.float32)],
        compiler_params=params(),
        cost_estimate=cost(4000000000, 16000000),
    )(me, z, ssm, gains)


def run_gate(z, ssm, cot, weight, rk, gains):
    rows, width = cot.shape
    b16 = jnp.bfloat16
    here = lambda g: (0, g)
    block, eight = pl.BlockSpec((rows, LANES), here), pl.BlockSpec((8, LANES), here)
    return pl.pallas_call(
        gate_kernel,
        grid=(DI // LANES,),
        in_specs=[block, block, whole(cot.shape), pl.BlockSpec((LANES, width), lambda g: (g, 0)), whole(rk.shape), eight],
        out_specs=[block, block, eight],
        out_shape=[shaped((rows, DI), b16)] * 2 + [shaped((8, DI), jnp.float32)],
        scratch_shapes=[pltpu.VMEM((rows, LANES), jnp.float32)],
        compiler_params=params(),
        cost_estimate=cost(12000000000, 36000000),
    )(z, ssm, cot, weight, rk, gains)


def run_backward(base, count, first, x, ssm, ds, conv, gains, prep, states):
    rows = x.shape[0]
    f32, b16 = jnp.float32, jnp.bfloat16
    chunks = rows // Q
    at = lambda g: (0, g + base)
    here = lambda g: (0, g)
    block, eight = pl.BlockSpec((rows, LANES), at), pl.BlockSpec((8, LANES), at)
    own = pl.BlockSpec((8, LANES), here)
    return pl.pallas_call(
        functools.partial(backward_kernel, base),
        grid=(count,),
        in_specs=[smem(), block, block, block, eight, eight] + [whole(v.shape) for v in prep] + [pl.BlockSpec((chunks * NSTATE, LANES), at)],
        out_specs=[pl.BlockSpec((rows, LANES), here), own, whole((rows, 6 * Q)), own],
        out_shape=[shaped((rows, count * LANES), b16), shaped((8, count * LANES), f32), shaped((rows, 6 * Q), f32), shaped((8, count * LANES), f32)],
        scratch_shapes=[pltpu.VMEM((NSTATE, LANES), f32), pltpu.VMEM((rows + 8, LANES), f32), pltpu.VMEM((48, LANES), f32)],
        compiler_params=params(),
        cost_estimate=cost(count * 7000000000, count * 8000000),
    )(first, x, ssm, ds, conv, gains, *prep, states)


def run_post(first, bcd, conv, heads, prep, backs):
    rows = bcd.shape[0]
    bc = prep[2]
    f32 = jnp.float32
    sums = [t for some in zip(*backs) for t in some]
    return pl.pallas_call(
        functools.partial(post_kernel, len(backs)),
        grid=(1,),
        in_specs=[smem(), whole((rows, BCD)), whole((8, 2 * NSTATE)), whole((8, 128)), whole(bc.shape)] + [whole(t.shape) for t in sums],
        out_specs=[whole((rows, BCD)), whole((8, 2 * NSTATE)), whole((8, 128))],
        out_shape=[shaped((rows, BCD), jnp.bfloat16), shaped((8, 2 * NSTATE), f32), shaped((8, 128), f32)],
        scratch_shapes=[pltpu.VMEM((rows + 8, 2 * NSTATE), f32)],
        compiler_params=params(),
        cost_estimate=cost(4000000000, 8000000),
    )(first, bcd, conv, heads, bc, *sums)


def contract_rows(left, right, kind=jnp.float32):
    return lax.dot_general(left, right, (((0,), (0,)), ((), ())), preferred_element_type=kind)


def pad_lanes(v, width):
    return jnp.pad(v, ((0, 0), (0, width - v.shape[1])))


ORDER = (7, 3, 5, 1, 6, 2, 4, 0)
DOUBLED = (0, 2, 4, 6, 1, 3, 5, 7)
WIDE = 512


def project_kernel(places, me_ref, left_ref, *refs):
    pieces, (out_ref, full_ref) = refs[:-2], refs[-2:]
    part = full_ref.shape[0] // 8
    for (j, skip, rows), ref in zip(places, pieces):
        full_ref[pl.ds(pl.multiple_of((me_ref[0] ^ j) * part + skip, 16), rows), :] = ref[:rows, :]
    out_ref[...] = dot32(left_ref[...], full_ref[...])


def run_project(me, left, pieces, skip, cols):
    rows, inner = left.shape
    step = min(WIDE, cols)
    here = lambda g: (0, g)
    places = tuple((j, start, min(v.shape[0], inner // 8 - start)) for v, j, start in pieces)
    return pl.pallas_call(
        functools.partial(project_kernel, places),
        grid=(cols // step,),
        in_specs=[smem(), whole(left.shape)] + [pl.BlockSpec((v.shape[0], step), lambda g: (0, g + skip // step)) for v, _, _ in pieces],
        out_specs=[pl.BlockSpec((rows, step), here), pl.BlockSpec((inner, step), here)],
        out_shape=[shaped((rows, cols), jnp.float32), shaped((inner, cols), left.dtype)],
        compiler_params=params(),
        cost_estimate=cost(2 * rows * inner * cols, 4 * inner * (rows + cols) + 4 * rows * cols),
    )(me, left, *[v for v, _, _ in pieces])


def unpack_kernel(widths, me_ref, small_ref, gain_ref, conv_ref, heads_ref, gains_ref, found):
    for k, j in enumerate(DOUBLED):
        found[me_ref[0] ^ j] = small_ref[k * SMALL : (k + 1) * SMALL, :].astype(jnp.float32)
    for ref in (gain_ref, conv_ref, heads_ref, gains_ref):
        ref[...] = jnp.zeros_like(ref)
    wide, taps, few, long = widths
    for i in range(8):
        gain_ref[:, i * wide : (i + 1) * wide] = found[i, 0:1, :wide]
        conv_ref[0:5, i * taps : (i + 1) * taps] = found[i, 1:6, :taps]
        heads_ref[0:3, i * few : (i + 1) * few] = found[i, 6:9, :few]
        gains_ref[1:2, i * long : (i + 1) * long] = found[i, 9:10, :long]
    spread = (row_ids(0, 128, DI) == lax.broadcasted_iota(jnp.int32, (128, DI), 1) // HEAD_DIM).astype(jnp.float32)
    gains_ref[0:1, :] = dot32(heads_ref[...], spread, precision=lax.Precision.HIGHEST)[2:3, :]


def out_kernel(gated_ref, weight_ref, x_ref, cot_ref, r_ref, result_ref, rk_ref, acc):
    weight = weight_ref[...]
    branch = dot32(gated_ref[...], weight)
    result_ref[...] = (x_ref[...].astype(jnp.float32) + branch).astype(result_ref.dtype)
    product = cot_ref[...].astype(jnp.float32) * branch
    part = product[:, :Q]
    for p in range(1, product.shape[1] // Q):
        part = part + product[:, p * Q : (p + 1) * Q]

    @pl.when(pl.program_id(0) == 0)
    def _():
        acc[...] = part

    @pl.when(pl.program_id(0) > 0)
    def _():
        acc[...] += part

    @pl.when(pl.program_id(0) == pl.num_programs(0) - 1)
    def _():
        r = r_ref[...]
        pull = r * r * (jnp.sum(acc[...], axis=-1, keepdims=True) / DI)
        lane = lax.broadcasted_iota(jnp.int32, rk_ref.shape, 1)
        rk_ref[...] = jnp.where(lane == 0, r, jnp.where(lane == 1, pull, 0.0))


def run_out(gated, weight, x, cot, r):
    rows, inner = gated.shape
    width = x.shape[1]
    step = width // 3
    here = lambda g: (0, g)
    return pl.pallas_call(
        out_kernel,
        grid=(3,),
        in_specs=[whole(gated.shape)] + [pl.BlockSpec((v.shape[0], step), here) for v in (weight, x, cot)] + [whole(r.shape)],
        out_specs=[pl.BlockSpec((rows, step), here), whole((rows, 128))],
        out_shape=[shaped((rows, width), x.dtype), shaped((rows, 128), jnp.float32)],
        scratch_shapes=[pltpu.VMEM((rows, Q), jnp.float32)],
        compiler_params=params(),
        cost_estimate=cost(4 * rows * inner * width, 4 * inner * width + 8 * rows * width),
    )(gated, weight, x, cot, r)


def pack_kernel(calls, widths, *refs):
    x_refs, (b_ref, h_ref, g_ref, n_ref, out_ref, conv) = refs[:calls], refs[calls:]
    wide, taps, few, long = widths
    start = 0
    for ref in (*x_refs, b_ref):
        conv[:, start : start + ref.shape[1]] = ref[...]
        start += ref.shape[1]
    inner = 8 * long
    spread = (row_ids(0, inner, 128) // HEAD_DIM == lax.broadcasted_iota(jnp.int32, (inner, 128), 1)).astype(jnp.float32)
    skips = dot32(conv[:, :inner], spread, precision=lax.Precision.HIGHEST)
    out_ref[...] = jnp.zeros_like(out_ref)
    for i in range(8):
        fields = [n_ref[0:1, i * wide : (i + 1) * wide]]
        fields += [conv[k : k + 1, i * taps : (i + 1) * taps] for k in range(KW + 1)]
        fields += [h_ref[k : k + 1, i * few : (i + 1) * few] for k in range(2)] + [skips[5:6, i * few : (i + 1) * few]]
        fields += [g_ref[0:1, i * long : (i + 1) * long]]
        start = 0
        for field in fields:
            out_ref[i : i + 1, start : start + field.shape[1]] = field
            start += field.shape[1]


def run_pack(widths, x_grads, b_grads, h_grads, g_grads, n_grads):
    wide, taps, few, long = widths
    width = wide + (KW + 1) * taps + 3 * few + long
    width += -width % 128
    args = (*x_grads, b_grads, h_grads, g_grads, n_grads)
    return pl.pallas_call(
        functools.partial(pack_kernel, len(x_grads), widths),
        grid=(1,),
        in_specs=[whole(v.shape) for v in args],
        out_specs=whole((8, width)),
        out_shape=shaped((8, width), jnp.float32),
        scratch_shapes=[pltpu.VMEM((8, 8 * taps), jnp.float32)],
        compiler_params=params(),
        cost_estimate=cost(1000000, 1000000),
    )(*args)


def back_kernel(spans, based, *refs):
    out_ref = refs[-1]
    grid = pl.program_id(0)

    @pl.when(grid == 0)
    def _():
        out_ref[...] = refs[0][...] if based else jnp.zeros_like(out_ref)

    refs = refs[based:-1]
    for i, (start, stop) in enumerate(spans):

        @pl.when((grid >= start) & (grid < stop))
        def _():
            out_ref[...] += dot32(refs[2 * i][...], refs[2 * i + 1][...], NT)


def run_back(pairs, base=None):
    rows, inner = pairs[0][0].shape[0], pairs[0][2].shape[0]
    spans, specs, args, start = [], [], [], 0
    if base is not None:
        specs, args = [whole((rows, inner))], [base]
    for grad, left_skip, weight, right_skip, width in pairs:
        step = min(WIDE, width)
        steps = width // step
        spans.append((start, start + steps))

        def at(skip, g, start=start, steps=steps):
            return (0, jnp.clip(g - start, 0, steps - 1) + skip)

        specs += [pl.BlockSpec((rows, step), functools.partial(at, left_skip // step)), pl.BlockSpec((inner, step), functools.partial(at, right_skip // step))]
        args += [grad, weight]
        start += steps
    return pl.pallas_call(
        functools.partial(back_kernel, tuple(spans), int(base is not None)),
        grid=(start,),
        in_specs=specs,
        out_specs=whole((rows, inner)),
        out_shape=shaped((rows, inner), jnp.float32),
        input_output_aliases={0: 0} if base is not None else {},
        compiler_params=params(),
        cost_estimate=cost(3000, 3000),
    )(*args)


TN = (((0,), (0,)), ((), ()))


def restore_kernel(targets_ref, blocks_ref, out_ref):
    count, rows, _ = blocks_ref.shape
    for i in range(count):
        out_ref[i * rows : (i + 1) * rows, :] = blocks_ref[targets_ref[i]]


def run_restore(targets, blocks):
    count, rows, width = blocks.shape
    return pl.pallas_call(
        restore_kernel,
        grid=(1,),
        in_specs=[smem(), whole(blocks.shape)],
        out_specs=whole((count * rows, width)),
        out_shape=shaped((count * rows, width), blocks.dtype),
        compiler_params=params(),
        cost_estimate=cost(6000000000, 12000000),
    )(targets, blocks)


def terms_kernel(turned, left_ref, right_ref, got_ref, *outs):
    rows = outs[0].shape[0]
    if turned:
        product = dot32(left_ref[...], right_ref[...], TN)
    else:
        product = dot32(left_ref[...], right_ref[...])
    product = product + got_ref[...].astype(jnp.float32)
    for i, ref in enumerate(outs):
        ref[...] = product[i * rows : (i + 1) * rows, :].astype(ref.dtype)


def run_terms(left, right, got, turned=False):
    rows, cols = got.shape
    inner = right.shape[0]
    step = 512 if cols % 512 == 0 else cols
    here = lambda g: (0, g)
    kinds = [jnp.bfloat16] * 3 + [jnp.float32]
    half = pl.BlockSpec((inner, rows), lambda g: (0, 1)) if turned else pl.BlockSpec((rows, inner), lambda g: (1, 0))
    return pl.pallas_call(
        functools.partial(terms_kernel, turned),
        grid=(cols // step,),
        in_specs=[half, pl.BlockSpec((inner, step), here), pl.BlockSpec((rows, step), here)],
        out_specs=[pl.BlockSpec((rows // 4, step), here)] * 4,
        out_shape=[shaped((rows // 4, cols), kind) for kind in kinds],
        compiler_params=params(),
        cost_estimate=cost(2 * rows * inner * cols, 6 * rows * cols),
    )(left, right, got)


def norm_kernel(order, me_ref, x_ref, gain_ref, out_ref, sent_ref, turned):
    rows, width = x_ref.shape
    for c in range(rows // Q):
        place = slice(c * Q, c * Q + Q)
        v = x_ref[place, :].astype(jnp.float32)
        normed = v * lax.rsqrt(jnp.mean(v * v, axis=-1, keepdims=True) + epsilon) * gain_ref[...]
        out_ref[place, :] = normed.astype(out_ref.dtype)
        for p in range(width // Q):
            turned[p * Q : p * Q + Q, place] = normed[:, p * Q : p * Q + Q].T.astype(turned.dtype)
    part = width // len(order)
    for k, j in enumerate(order):
        sent_ref[k * part : (k + 1) * part, :] = turned[pl.ds(pl.multiple_of((me_ref[0] ^ j) * part, 16), part), :]


def run_norm(order, me, x, gain):
    rows, width = x.shape
    b16 = jnp.bfloat16
    return pl.pallas_call(
        functools.partial(norm_kernel, order),
        grid=(1,),
        in_specs=[smem(), whole(x.shape), whole((1, width))],
        out_specs=[whole(x.shape), whole((width, rows))],
        out_shape=[shaped(x.shape, b16), shaped((width, rows), b16)],
        scratch_shapes=[pltpu.VMEM((width, rows), b16)],
        compiler_params=params(),
        cost_estimate=cost(2000000000, 6 * rows * width),
    )(me, x, gain)


def open_kernel(places, widths, me_ref, first_ref, x_ref, small_ref, *refs):
    pieces, refs = refs[: len(places)], refs[len(places) :]
    gain_ref, conv_ref, heads_ref, gains_ref, out_ref, sent_ref, bcd_ref, full_ref, *prep_refs, found, turned = refs
    unpack_kernel(widths, me_ref, small_ref, gain_ref, conv_ref, heads_ref, gains_ref, found)
    norm_kernel(ORDER, me_ref, x_ref, gain_ref, out_ref, sent_ref, turned)
    project_kernel(places, me_ref, out_ref, *pieces, bcd_ref, full_ref)
    prep_kernel(first_ref, bcd_ref, conv_ref.at[:, pl.ds(DI, 2 * NSTATE)], heads_ref, *prep_refs)


def run_open(me, first, x, small, pieces, widths, skip):
    f32, b16 = jnp.float32, jnp.bfloat16
    toks, width = x.shape
    wide, taps, few, long = widths
    places = tuple((j, start, min(v.shape[0], width // 8 - start)) for v, j, start in pieces)
    shapes = [((1, 8 * wide), f32), ((8, 8 * taps), f32), ((8, 128), f32), ((8, 8 * long), f32)]
    shapes += [((toks, width), b16), ((width, toks), b16), ((toks, BCD), f32), ((width, BCD), b16)]
    shapes += [((toks, 4 * Q), f32), ((256, toks), f32), ((toks, 2 * NSTATE), b16), ((2 * NSTATE, toks), b16)]
    return pl.pallas_call(
        functools.partial(open_kernel, places, widths),
        grid=(1,),
        in_specs=[smem(), smem(), whole(x.shape), whole(small.shape)] + [pl.BlockSpec((v.shape[0], BCD), lambda g: (0, skip // BCD)) for v, _, _ in pieces],
        out_specs=[whole(s) for s, _ in shapes],
        out_shape=[shaped(s, d) for s, d in shapes],
        scratch_shapes=[pltpu.VMEM((8, SMALL, small.shape[1]), f32), pltpu.VMEM((width, toks), b16)],
        compiler_params=params(),
        cost_estimate=cost(6000000000, 10000000),
    )(me, first, x, small, *[v for v, _, _ in pieces])


def norm_back_kernel(d_ref, x_ref, cot_ref, gain_ref, out_ref, grad_ref):
    @pl.when(pl.program_id(0) == 0)
    def _():
        grad_ref[...] = jnp.zeros_like(grad_ref)

    v = x_ref[...].astype(jnp.float32)
    rn = lax.rsqrt(jnp.mean(v * v, axis=-1, keepdims=True) + epsilon)
    d = d_ref[...]
    grad_ref[0:1, :] += sum_rows(d * v * rn)
    scaled = d * gain_ref[...]
    pull = rn * rn * rn * jnp.mean(v * scaled, axis=-1, keepdims=True)
    out_ref[...] = (cot_ref[...].astype(jnp.float32) + rn * scaled - v * pull).astype(out_ref.dtype)


def run_norm_back(d, x, cot, gain):
    rows, width = x.shape
    block = pl.BlockSpec((Q, width), lambda g: (g, 0))
    return pl.pallas_call(
        norm_back_kernel,
        grid=(rows // Q,),
        in_specs=[block, block, block, whole((1, width))],
        out_specs=[block, whole((8, width))],
        out_shape=[shaped(x.shape, x.dtype), shaped((8, width), jnp.float32)],
        compiler_params=params(),
        cost_estimate=cost(3000, 3000),
    )(d, x, cot, gain)


SMALL = 16
CALLS = ((0, 4), (4, 2))


def partners(bit):
    return [(i, i ^ bit) for i in range(8)]


def rotated(step):
    return [(i, (i + step) % 4) for i in range(4)]


def tie(*values):
    return lax.optimization_barrier(values)


def custom():
    return lax.axis_size("fsdp") == 8 and lax.axis_size("rep") == 4


def gathered_rows(w, late=False):
    half = w.shape[0] // 32 * 16
    two, four = yield [(w, "fsdp", partners(j)) for j in (2, 4)], 1
    sent = [(two[:half], "fsdp", partners(4)), (four[half:], "fsdp", partners(2))]
    if late:
        top, bottom, one, three = yield sent + [(v, "fsdp", partners(1)) for v in (w, two)], 1
        five, other_top, other_bottom = yield [(v, "fsdp", partners(1)) for v in (four, top, bottom)], 1
    else:
        top, bottom, one, three, five = yield sent + [(v, "fsdp", partners(1)) for v in (w, two, four)], 1
        other_top, other_bottom = yield [(v, "fsdp", partners(1)) for v in (top, bottom)], 1
    near = [(w, 0, 0), (one, 1, 0), (two, 2, 0), (three, 3, 0), (four, 4, 0), (five, 5, 0)]
    return near + [(top, 6, 0), (bottom, 6, half), (other_top, 7, 0), (other_bottom, 7, half)]


def dealt(v, turns):
    (got,) = yield [(v, "fsdp", None)], turns
    return got


def widen(v):
    return v.astype(jnp.float32)


def group_sum(left, right):
    half = left.shape[0] // 2
    odd = jnp.dot(left[:half], right, preferred_element_type=jnp.float32).astype(jnp.bfloat16)
    (got,) = yield [(odd, "fsdp", partners(1))], 1
    *terms, own = run_terms(left, right, got)
    others = yield [(v, "fsdp", partners(j)) for v, j in zip(terms, ORDER[4:7])], 1
    return own + widen(others[0]) + widen(others[1]) + widen(others[2])


def relayed_sum(left, right):
    b16 = jnp.bfloat16
    rows = left.shape[1] // 8
    half = rows // 2

    def product(start, stop):
        return contract_rows(left[:, start * rows : stop * rows], right)

    (got,) = yield [(product(0, 4).astype(b16), "fsdp", partners(1))], 1
    far = (product(4, 5) + widen(got[:rows])).astype(b16)
    from_x, from_y = yield [(far[:half], "fsdp", partners(2)), (far[half:], "fsdp", partners(4))], 1
    low = jnp.pad(widen(from_y), ((half, 0), (0, 0)))
    high = jnp.pad(widen(from_x), ((0, half), (0, 0)))
    to_x = (product(5, 6) + widen(got[rows : 2 * rows]) + low).astype(b16)
    to_y = (product(6, 7) + widen(got[2 * rows : 3 * rows]) + high).astype(b16)
    got_x, got_y = yield [(to_x, "fsdp", partners(2)), (to_y, "fsdp", partners(4))], 1
    return product(7, 8) + widen(got[3 * rows :]) + widen(got_x) + widen(got_y)


def out_sum(left, right):
    own = yield from relayed_sum(left, right)
    return (yield from half_sum(own))


def half_sum(own):
    b16 = jnp.bfloat16
    place = lax.axis_index("rep")
    odd, late = place % 2 == 1, place >= 2
    across = [(0, 2), (1, 3), (2, 0), (3, 1)]
    beside = [(0, 1), (1, 0), (2, 3), (3, 2)]

    def halves(v, second):
        top, bottom = jnp.split(v, 2)
        return jnp.where(second, bottom, top), jnp.where(second, top, bottom)

    def joined(mine, other, second):
        return jnp.where(second, jnp.concatenate([other, mine]), jnp.concatenate([mine, other]))

    keep, send = halves(own, odd)
    (got,) = yield [(send.astype(b16), "rep", beside)], 1
    keep, send = halves(widen(keep) + widen(got), late)
    (got,) = yield [(send.astype(b16), "rep", across)], 1
    mine = (keep + widen(got)).astype(b16)
    (got,) = yield [(mine, "rep", across)], 1
    mine = joined(mine, got, late)
    (got,) = yield [(mine, "rep", beside)], 1
    return joined(mine, got, odd)


def small_sum(rows):
    me, place = lax.axis_index("fsdp"), lax.axis_index("rep")
    rows = rows[me ^ jnp.array(ORDER, jnp.int32)]
    (got,) = yield [(rows[:4], "fsdp", partners(1))], 1
    rows = rows[4:] + got
    others = yield [(rows[i : i + 1], "fsdp", partners(j)) for i, j in enumerate(ORDER[4:7])], 1
    row = rows[3:] + others[0] + others[1] + others[2]
    got = yield [(row, "rep", rotated(k)) for k in (1, 2, 3)], 1
    stack = jnp.concatenate([row, *got])
    return jnp.sum(stack[(place - jnp.arange(4)) % 4], axis=0)


def transfer(v, axis, pairs):
    if pairs is None:
        return lax.all_to_all(v, axis, split_axis=0, concat_axis=0, tiled=True)
    return lax.ppermute(v, axis, pairs)


def slice_sum(left, right):
    own = yield from group_sum(left, right)
    return (yield from half_sum(own))


class Moves:
    def __init__(self):
        self.active = []

    def add(self, generator):
        want, turns = next(generator)
        entry = {"gen": generator, "want": want, "turns": turns, "got": None, "value": None}
        self.active.append(entry)
        return entry

    def turn(self, work=None, *values):
        fresh = [e for e in self.active if e["got"] is None]
        arrays, values = tie([[item[0] for item in e["want"]] for e in fresh], values)
        for e, some in zip(fresh, arrays):
            e["got"] = [None] * len(some)
        alike = {}
        for e, some in zip(fresh, arrays):
            for i, (v, item) in enumerate(zip(some, e["want"])):
                kind = (item[1], str(item[2]), v.shape[0], v.dtype.name) if item[1] == "rep" else (id(e), i)
                alike.setdefault(kind, []).append((e, i, v, item))
        for group in alike.values():
            moved = transfer(jnp.concatenate([g[2] for g in group], axis=1) if len(group) > 1 else group[0][2], *group[0][3][1:])
            start = 0
            for e, i, v, _ in group:
                e["got"][i] = moved[:, start : start + v.shape[1]] if len(group) > 1 else moved
                start += v.shape[1]
        results = work(*values) if work else ()
        for e in self.active:
            e["turns"] -= 1
        due = [e for e in self.active if e["turns"] == 0]
        arrived, results = tie([e["got"] for e in due], results)
        for e, got in zip(due, arrived):
            try:
                e["want"], e["turns"] = e["gen"].send(got)
                e["got"] = None
            except StopIteration as stop:
                e["value"] = stop.value
                self.active.remove(e)
        return results

    def after(self, value):
        want = self.active[0]["want"]
        array, *rest = want[-1]
        value, array = tie(value, array)
        want[-1] = (array, *rest)
        return value

    def finish(self):
        while self.active:
            self.turn()


def per_device(tokens, cotangent, lengths, dealing, norm_gain, in_weight, conv_weight, conv_bias, dt_bias, a_log, d_skip, gated_gain, out_weight):
    f32, b16 = jnp.float32, jnp.bfloat16
    groups = lax.axis_size("fsdp")
    tok_rows, width = tokens.shape
    block_rows = tok_rows // groups
    targets = dealing.reshape(groups)
    inverse = jnp.argsort(targets)
    first = lengths.reshape(-1)[:1]
    me = lax.axis_index("fsdp").reshape(1)
    moves = Moves()

    def blocks(values):
        return values.reshape(groups, block_rows, width)[inverse]

    def deal(values):
        return lax.all_to_all(blocks(values), "fsdp", split_axis=0, concat_axis=0, tiled=True).reshape(tok_rows, width)

    def undeal(values):
        blocks = lax.all_to_all(values.reshape(groups, block_rows, width), "fsdp", split_axis=0, concat_axis=0, tiled=True)
        return blocks[targets].reshape(tok_rows, width)

    own_small = [norm_gain, conv_weight, conv_bias, dt_bias, a_log, d_skip, gated_gain]

    def rows_of(values):
        values = [v if v.ndim == 2 else v[None] for v in values]
        longest = max(v.shape[1] for v in values)
        packed = jnp.concatenate([pad_lanes(v, longest) for v in values])
        return jnp.pad(packed, ((0, SMALL - packed.shape[0]), (0, 0)))

    def doubled(v, bit):
        return (jnp.concatenate([v, lax.ppermute(v, "fsdp", partners(bit))]),)

    if custom():
        rows, span = in_weight.shape[0], DI + BCD
        w_xb = lax.pad(in_weight, jnp.zeros((), b16), ((0, 0, 0), (-DI, span + DI - in_weight.shape[1], 0)))
        e_xb = moves.add(gathered_rows(w_xb, True))

        def deal_out(values):
            return lax.all_to_all(values, "fsdp", split_axis=0, concat_axis=0, tiled=True)

        def first_turn(tokens, *values):
            ahead.append(deal_out(blocks(tokens)))
            return doubled(rows_of(values), 2)

        ahead = []
        (small,) = moves.turn(first_turn, tokens, *own_small)
        small, cot_blocks, x = moves.turn(lambda v, c: (*doubled(v, 4), blocks(c), ahead[0]), small, cotangent)
        out_weight = moves.after(out_weight)
        w_out = lax.all_gather(out_weight, "fsdp", axis=0, tiled=True)
        (small,) = moves.turn(lambda v: doubled(v, 1), small)
        pieces = e_xb["value"]
        x = x.reshape(tok_rows, width)
        widths = (norm_gain.size, conv_bias.size, dt_bias.size, gated_gain.size)
    else:
        x = deal(tokens)
        w_z = lax.all_gather(in_weight[:, :DI], "fsdp", axis=0, tiled=True)
        w_out = lax.all_gather(out_weight, "fsdp", axis=0, tiled=True)
        small_all = lax.all_gather(rows_of(own_small), "fsdp", axis=0, tiled=False).astype(f32)
        w_xb = lax.all_gather(pad_lanes(in_weight[:, DI:], DI + BCD), "fsdp", axis=0, tiled=True)
        parts, row = [], 0
        for v in (u if u.ndim == 2 else u[None] for u in own_small):
            parts.append(small_all[:, row : row + v.shape[0], : v.shape[1]].transpose(1, 0, 2).reshape(v.shape[0], -1))
            row += v.shape[0]
        gain, taps, bias, step_bias, rate, skip, ggain = parts
        conv = jnp.concatenate([taps, bias, jnp.zeros((3, bias.shape[1]), f32)])
        heads = pad_lanes(jnp.concatenate([step_bias, rate, jnp.zeros((6, HEADS), f32)]), 128)
        gains = jnp.concatenate([jnp.repeat(skip, HEAD_DIM, axis=1), ggain, jnp.zeros((6, DI), f32)])
    if custom():

        def open_up(x):
            gain, conv, heads, gains, normed, sent, bcd, w_b, *prep = run_open(me, first, x, small, pieces, widths, DI)
            return gain, conv, heads, gains, normed, sent, bcd, w_b, prep, *run_project(me, normed, pieces, 0, DI)

        e_z = moves.add(gathered_rows(in_weight[:, :DI]))
        gain, conv, heads, gains, normed, sent, bcd, w_b, prep, xr, w_x = moves.turn(open_up, x)
        conv_x, conv_bc = conv[:, :DI], conv[:, DI:]
        ssm, states = moves.turn(lambda v: run_forward(first, v, conv_x, gains, prep), xr)
        moves.turn()
        e_cot = moves.add(dealt(cot_blocks, 1))

        def close_up(ssm):
            z, full = run_project(me, normed, e_z["value"], 0, DI)
            return z, full, *run_gated(ORDER, me, z, ssm, gains)

        z, w_z, gated, gated_sent, r = moves.turn(close_up, ssm)
        cot = e_cot["value"].reshape(tok_rows, width)
        e_rows = moves.add(out_sum(gated_sent, cot))
        result, rk = moves.turn(lambda v: run_out(v, w_out, x, cot, r), gated)
    else:
        conv_x, conv_bc = conv[:, :DI], conv[:, DI:]
        normed, sent = run_norm((0,), me * 0, x, gain)
        w_x, w_b = w_xb[:, :DI], w_xb[:, DI:]
        bcd = jnp.dot(normed, w_b, preferred_element_type=f32)
        xr = jnp.dot(normed, w_x, preferred_element_type=f32)
        cot = deal(cotangent)
        prep = run_prep(first, bcd, conv_bc, heads)
        ssm, states = run_forward(first, xr, conv_x, gains, prep)
        z = jnp.dot(normed, w_z, preferred_element_type=f32)
        gated, _, r = run_gated(tuple(range(8)), me * 0, z, ssm, gains)
        result, rk = run_out(gated, w_out, x, cot, r)
        s_out = lax.psum_scatter(contract_rows(gated, cot, b16), "fsdp", scatter_dimension=0, tiled=True)

    def gate(rk):
        return run_gate(z, ssm, cot, w_out, rk, gains)

    def backward(base, count, ds):
        return run_backward(base, count, first, xr, ssm, ds, conv_x, gains, prep, states)

    def close(backs):
        return run_post(first, bcd, conv_bc, heads, prep, [b[2:] for b in backs])

    def back(backs, d_b):
        pairs = [(dz, 0, w_z, 0, DI)] + [(b[0], 0, w_x, base * LANES, count * LANES) for b, (base, count) in zip(backs, CALLS)]
        return run_back(pairs + [(d_b, 0, w_b, 0, BCD)])

    if custom():
        dz, ds, ggrads = moves.turn(gate, rk)

        def first_back(dz, ds):
            z_term, ds = tie(contract_rows(normed, dz, b16), ds)
            held.append(lax.psum_scatter(z_term, "fsdp", scatter_dimension=0, tiled=True))
            return backward(*CALLS[0], ds)

        held = []
        backs = [moves.turn(first_back, dz, ds)]
        (s_z,) = held
        e_first = moves.add(slice_sum(sent, backs[0][0]))

        def middle(ds):
            both = backs + [backward(*CALLS[1], ds)]
            return both[1], *close(both)

        last, d_b, bgrads, hgrads = moves.turn(middle, ds)
        backs.append(last)
        e_last = moves.add(slice_sum(sent, jnp.concatenate([last[0], d_b], axis=1)))
        e_z = moves.add(half_sum(s_z))
        (d_normed,) = moves.turn(lambda d: (back(backs, d),), d_b)

        def finish(d_normed):
            d_input, ngrads = run_norm_back(d_normed, x, cot, gain)
            ahead.append(deal_out(d_input.reshape(groups, block_rows, width)))
            return (run_pack(widths, [b[1] for b in backs], bgrads, hgrads, ggrads, ngrads),)

        (packed,) = moves.turn(finish, d_normed)
    else:
        dz, ds, ggrads = gate(rk)
        s_z = lax.psum_scatter(contract_rows(normed, dz, b16), "fsdp", scatter_dimension=0, tiled=True)
        backs = [backward(*call, ds) for call in CALLS]
        d_b, bgrads, hgrads = close(backs)
        d_normed = back(backs, d_b)
        d_input, ngrads = run_norm_back(d_normed, x, cot, gain)
        s_in = [lax.psum_scatter(contract_rows(normed, d, b16), "fsdp", scatter_dimension=0, tiled=True) for d in [b[0] for b in backs] + [d_b]]
        output, input_grad = undeal(result), undeal(d_input)

    if not custom():
        xgrads = jnp.concatenate([b[1] for b in backs], axis=1)
        g_ggain = ggrads[0]
        g_conv = jnp.concatenate([xgrads[:KW], bgrads[:KW]], axis=1)
        g_cbias = jnp.concatenate([xgrads[KW], bgrads[KW]])
        g_dskip = jnp.sum(xgrads[5].reshape(HEADS, HEAD_DIM), axis=1)
        spread = [
            ngrads[0].reshape(groups, -1),
            g_conv.reshape(KW, groups, -1).transpose(1, 0, 2).reshape(groups, -1),
            g_cbias.reshape(groups, -1),
            hgrads[0, :HEADS].reshape(groups, -1),
            hgrads[1, :HEADS].reshape(groups, -1),
            g_dskip.reshape(groups, -1),
            g_ggain.reshape(groups, -1),
        ]
        packed = jnp.concatenate(spread, axis=1)
        packed = pad_lanes(packed, packed.shape[1] + -packed.shape[1] % 128)
    sizes = [v.size for v in own_small]
    tail = in_weight.shape[1] - 2 * DI

    def cut(row):
        ends, outs = 0, []
        for size in sizes:
            outs.append(row[ends : ends + size])
            ends += size
        return outs

    if custom():
        e_small = moves.add(small_sum(packed))
        moves.turn()
        e_output = moves.add(dealt(result.reshape(groups, block_rows, width), 1))
        moves.turn()

        input_grad, r_out = moves.turn(lambda: (run_restore(targets, ahead[1]), widen(e_rows["value"])))
        (output,) = moves.turn(lambda: (run_restore(targets, e_output["value"]),))
        last = CALLS[-1][1] * LANES + tail

        def gather_up():
            known = jnp.concatenate([e_z["value"], e_first["value"], jnp.zeros((rows, last), b16)], axis=1)
            return widen(known), *cut(e_small["value"])

        r_in, *outs = moves.turn(gather_up)
        moves.finish()
        r_in = lax.dynamic_update_slice(r_in, widen(e_last["value"][:, :last]), (0, r_in.shape[1] - last))
    else:
        s_small = jnp.sum(lax.all_to_all(packed, "fsdp", split_axis=0, concat_axis=0, tiled=True), axis=0)
        r_small = jnp.sum(lax.all_gather(s_small, "rep", axis=0, tiled=False), axis=0)
        *r_in, r_out = lax.psum((s_z, *s_in, s_out), "rep")
        r_in = jnp.concatenate(r_in, axis=1)[:, : in_weight.shape[1]]
        outs = cut(r_small)
    return (output, input_grad, outs[0], r_in.astype(f32), outs[1].reshape(conv_weight.shape), outs[2], outs[3], outs[4], outs[5], outs[6], r_out.astype(f32))


def solution(mesh):
    placed = (
        P(("rep", "fsdp"), None),
        P(("rep", "fsdp"), None),
        P("rep", "fsdp", None),
        P("rep", "fsdp", None),
        P("fsdp"),
        P("fsdp", None),
        P(None, "fsdp"),
        P("fsdp"),
        P("fsdp"),
        P("fsdp"),
        P("fsdp"),
        P("fsdp"),
        P("fsdp", None),
    )
    return jax.shard_map(
        per_device,
        mesh=mesh,
        in_specs=placed,
        out_specs=(
            P(("rep", "fsdp"), None),
            P(("rep", "fsdp"), None),
            P("fsdp"),
            P("fsdp", None),
            P(None, "fsdp"),
            P("fsdp"),
            P("fsdp"),
            P("fsdp"),
            P("fsdp"),
            P("fsdp"),
            P("fsdp", None),
        ),
        check_vma=False,
    )
```
